32 devices in a mesh: ctx: 8 (over z, y), fsdp: 4 (over x, core).
Axes of the slice: x: 2, y: 2, z: 4, core: 2. Of those that a mesh axis runs over, the one named last changes fastest.
Arguments:
- tokens: bfloat16 [4, 2048, 768], P('fsdp', 'ctx'), may hold values from -6 to 6
- pair_order: int32 [8], replicated, may hold values from 0 to 7, each once
- norm_one: bfloat16 [768], P('fsdp'), may hold values from 0.099609375 to 1.8984375
- qkv_weight: bfloat16 [768, 2304], P('fsdp'), may hold values from -0.3125 to 0.3125
- out_weight: bfloat16 [768, 768], P('fsdp'), may hold values from -1.75 to 1.75
- norm_two: bfloat16 [768], P('fsdp'), may hold values from 0.099609375 to 1.8984375
- gateup_weight: bfloat16 [768, 2304], P('fsdp'), may hold values from -0.21875 to 0.21875
- down_weight: bfloat16 [1152, 768], P('fsdp'), may hold values from -0.1875 to 0.1875
- cotangent: bfloat16 [4, 2048, 768], P('fsdp', 'ctx'), may hold values from -6 to 6
Outputs:
- layer_out: bfloat16 [4, 2048, 768], P('fsdp', 'ctx')
- grad_tokens: float32 [4, 2048, 768], P('fsdp', 'ctx')
- grad_norm_one: float32 [768], P('fsdp')
- grad_qkv_weight: float32 [768, 2304], P('fsdp')
- grad_out_weight: float32 [768, 768], P('fsdp')
- grad_norm_two: float32 [768], P('fsdp')
- grad_gateup_weight: float32 [768, 2304], P('fsdp')
- grad_down_weight: float32 [1152, 768], P('fsdp')
The draws below stay inside these ranges and needn't reach their ends.
Inputs may be any that keep to these rules, and one draw needn't show every extreme that they name: Device j of ctx holds position block pair_order[j] of its sequence in its first 128 slots and block 15 - pair_order[j] in its last 128 slots; every block once.
All inputs are finite; a program needn't handle non-finite values.
Results may differ from the reference program's by a relative error of at most 0.018.
The reference program's roundings to bfloat16 on the way count: a program that leaves them out, or rounds other values in their place, can miss the bound.
Values may be sent and summed in bfloat16 or wider, within the bound.
No kernel may reach another device: no remote copies, remote signals or barrier semaphores. Data moves between devices by JAX's collectives and lax.ppermute only.
A program may use at most 320 MiB of HBM per device.

```python
import jax
import jax.numpy as jnp
from jax import lax

D = 768
HEADS = 12
HEAD_DIM = 64
FF = 1152
BLK = 128
KEYBLK = 512
SEQ_LEN = 2048
SEQS = 4
N_CTX = 8


def shard_levels(rng, shape, shards, low, largest):
    loudness, own = 1.0, jax.random.fold_in(rng, 6)
    for position, shards_of in shards:
        steps = jnp.exp(jax.random.uniform(jax.random.fold_in(own, position), (shards_of,), jnp.float32, low / len(shards), largest / len(shards)))
        loudness = loudness * jnp.repeat(steps, shape[position] // shards_of).reshape([-1 if axis == position else 1 for axis in range(len(shape))])
    return loudness


def centred(rng, extent, scale, limit, cuts=(), kind=jnp.bfloat16):
    entries = jax.random.normal(rng, extent, jnp.float32) * scale
    if len(cuts) > 0:
        entries = shard_levels(rng, extent, cuts, -0.22, 0.18) * entries
    return jnp.clip(entries, min=-limit, max=limit).astype(kind)


def setup_inputs(seed: int = 0) -> dict:
    keys = jax.random.split(jax.random.key(seed), 10)
    return {
        "tokens": centred(keys[0], (SEQS, SEQ_LEN, D), 1.0, 6.0, ((0, 4), (1, 8))),
        "pair_order": jax.random.permutation(keys[1], N_CTX).astype(jnp.int32),
        "norm_one": jnp.clip(1.0 + 0.18 * jax.random.normal(keys[2], (D,), jnp.float32), 0.099609375, 1.8984375).astype(jnp.bfloat16),
        "qkv_weight": centred(keys[3], (D, 3 * D), (D // 2) ** -0.5, 0.3125, ((0, 4),)),
        "out_weight": centred(keys[4], (D, D), (D // 64) ** -0.5, 1.75, ((0, 4),)),
        "norm_two": jnp.clip(1.0 + 0.18 * jax.random.normal(keys[5], (D,), jnp.float32), 0.099609375, 1.8984375).astype(jnp.bfloat16),
        "gateup_weight": centred(keys[6], (D, 2 * FF), D ** -0.5, 0.21875, ((0, 4),)),
        "down_weight": centred(keys[7], (FF, D), FF ** -0.5, 0.1875, ((0, 4),)),
        "cotangent": centred(keys[8], (SEQS, SEQ_LEN, D), 1.0, 6.0, ((0, 4), (1, 8))),
    }


theta_base = 160000.0
norm_eps = 1e-05
neg_large = -1e+30

@jax.custom_vjp
def low(v):
    return lax.optimization_barrier(v.astype(jnp.bfloat16)).astype(jnp.float32)

@jax.custom_vjp
def low_back(v):
    return v

def low_keep(v):
    return (low(v), None)

def low_pass(kept, grad):
    return (grad,)

def back_keep(v):
    return (v, None)

def back_low(kept, grad):
    return (low(grad),)
low.defvjp(low_keep, low_pass)
low_back.defvjp(back_keep, back_low)

def layer_norm(token_rows, gain_row):
    mean_value = lax.optimization_barrier(jnp.mean(token_rows, axis=-1, keepdims=True))
    centered = token_rows - mean_value
    spread = lax.optimization_barrier(jnp.mean(centered * centered, axis=-1, keepdims=True))
    return centered * lax.rsqrt(spread + norm_eps) * gain_row

def rotate(token_rows, positions):
    row_count = token_rows.shape[0]
    half_dim = HEAD_DIM // 2
    frequency = theta_base ** (-2.0 * jnp.arange(half_dim, dtype=jnp.float32) / HEAD_DIM)
    angles = positions.astype(jnp.float32)[:, None] * frequency[None, :]
    cosine = jnp.concatenate([jnp.cos(angles), jnp.cos(angles)], axis=1)[:, None, :]
    sine_table = jnp.concatenate([jnp.sin(angles), jnp.sin(angles)], axis=1)[:, None, :]
    by_heads = token_rows.reshape(row_count, HEADS, HEAD_DIM)
    turned = jnp.concatenate([-by_heads[..., half_dim:], by_heads[..., :half_dim]], axis=-1)
    return (by_heads * cosine + turned * sine_table).reshape(row_count, HEADS * HEAD_DIM)

def geglu(gate_part, up_part):
    return jax.nn.gelu(gate_part, approximate=False) * up_part

def slot_positions(pair_order):
    slot_ids = jnp.arange(SEQ_LEN, dtype=jnp.int32)
    device_ids = slot_ids // (2 * BLK)
    within = slot_ids % (2 * BLK)
    first_block = pair_order[device_ids].astype(jnp.int32)
    block_ids = jnp.where(within < BLK, first_block, 2 * N_CTX - 1 - first_block)
    return block_ids * BLK + within % BLK

def attend(query_heads, key_heads, value_heads, positions):
    scale = HEAD_DIM ** (-0.5)
    block_total = SEQ_LEN // KEYBLK
    query_blocks = query_heads.reshape(block_total, KEYBLK, HEADS, HEAD_DIM)
    position_blocks = positions.reshape(block_total, KEYBLK)

    def one_block(pieces):
        query_part, query_pos = pieces
        raw_scores = jnp.einsum('qhd,khd->hqk', query_part, key_heads, precision=lax.Precision.HIGHEST) * scale
        scores = low_back(raw_scores)
        allowed = positions[None, None, :] <= query_pos[None, :, None]
        scores = jnp.where(allowed, scores, neg_large)
        row_top = lax.optimization_barrier(jnp.max(scores, axis=-1, keepdims=True))
        log_total = row_top + jnp.log(lax.optimization_barrier(jnp.sum(jnp.exp(scores - row_top), axis=-1, keepdims=True)))
        probability = low(jnp.exp(scores - log_total))
        return jnp.einsum('hqk,khd->qhd', probability, value_heads, precision=lax.Precision.HIGHEST)
    attended = lax.map(jax.checkpoint(one_block), (query_blocks, position_blocks))
    return attended.reshape(SEQ_LEN, HEADS * HEAD_DIM)

def forward_one(token_rows, positions, weights):
    gain_one, weight_qkv, weight_out, gain_two, weight_gateup, weight_down = weights
    high = lax.Precision.HIGHEST
    normed = low(layer_norm(token_rows, gain_one))
    mixed_rows = low_back(jnp.dot(normed, weight_qkv, precision=high))
    queries = low(rotate(mixed_rows[:, :D], positions))
    keys_rot = low(rotate(mixed_rows[:, D:2 * D], positions))
    values = low(mixed_rows[:, 2 * D:])
    shape_heads = (SEQ_LEN, HEADS, HEAD_DIM)
    attended = attend(queries.reshape(shape_heads), keys_rot.reshape(shape_heads), values.reshape(shape_heads), positions)
    attended = low(low_back(attended))
    branch = low_back(jnp.dot(attended, weight_out, precision=high))
    middle = token_rows + branch
    normed_two = low(layer_norm(middle, gain_two))
    gateup = low_back(jnp.dot(normed_two, weight_gateup, precision=high))
    hidden = low(geglu(gateup[:, :FF], gateup[:, FF:]))
    return middle + jnp.dot(hidden, weight_down, precision=high)

def reference(tokens, pair_order, norm_one, qkv_weight, out_weight, norm_two, gateup_weight, down_weight, cotangent):
    positions = slot_positions(pair_order)
    weights = (norm_one.astype(jnp.float32), qkv_weight.astype(jnp.float32), out_weight.astype(jnp.float32), norm_two.astype(jnp.float32), gateup_weight.astype(jnp.float32), down_weight.astype(jnp.float32))

    def whole(all_rows, weight_set):
        return lax.map(lambda seq_rows: forward_one(seq_rows, positions, weight_set), all_rows)
    result, pullback = jax.vjp(whole, tokens.astype(jnp.float32), weights)
    grad_rows, grad_weights = pullback(cotangent.astype(jnp.float32))
    return (result.astype(jnp.bfloat16), grad_rows, grad_weights[0], grad_weights[1], grad_weights[2], grad_weights[3], grad_weights[4], grad_weights[5])
```

```python
from functools import partial

import jax
import jax.numpy as jnp
from jax import lax
from jax.experimental import pallas as pl
from jax.experimental.pallas import tpu as pltpu
from jax.sharding import PartitionSpec as P

D = 768
HEAD_DIM = 64
FF = 1152
LANES = 128
PAIRS = D // LANES
COLS = 256
SCALE = HEAD_DIM**-0.5

theta_base = 160000.0
norm_eps = 1e-05
neg_large = -1e30
f32 = jnp.float32
bf16 = jnp.bfloat16

SMEM = pl.BlockSpec(memory_space=pltpu.SMEM)
WHOLE = pl.BlockSpec(memory_space=pltpu.VMEM)


def params(megabytes):
    return pltpu.CompilerParams(vmem_limit_bytes=megabytes * 2**20)


def cost(flops, moved, exps=0):
    return pl.CostEstimate(flops=int(flops), bytes_accessed=int(moved), transcendentals=int(exps))


def dot(left, right, left_dim, right_dim):
    return lax.dot_general(
        left, right, (((left_dim,), (right_dim,)), ((), ())), preferred_element_type=f32
    )


def ring_device(place, count):
    return jnp.where(place < count // 2, 2 * place, 2 * (count - 1 - place) + 1)


def ring_place(device, count):
    return jnp.where(device % 2 == 0, device // 2, count - 1 - device // 2)


def shift(array, step, count):
    half = count // 2
    order = [2 * i if i < half else 2 * (count - 1 - i) + 1 for i in range(count)]
    pairs = [(order[i], order[(i + step) % count]) for i in range(count)]
    return lax.ppermute(array, "ctx", pairs)


def ring_offsets(count):
    half = count // 2
    offsets = [0]
    for distance in range(1, half):
        offsets += [-distance, distance]
    return offsets + [half]


def ring_gather(first, second, count):
    half = count // 2
    firsts, seconds = [first], [second]
    up, down = (first, second), (first, second)
    for _ in range(1, half):
        up = tuple(shift(part, 1, count) for part in up)
        down = tuple(shift(part, -1, count) for part in down)
        firsts += [up[0], down[0]]
        seconds += [up[1], down[1]]
    firsts.append(shift(up[0], 1, count))
    seconds.append(shift(down[1], -1, count))
    return firsts, seconds


def add_rounded(left, right):
    return (left.astype(f32) + right.astype(f32)).astype(bf16)


def ring_scatter(firsts, seconds, count):
    half = count // 2
    places = {offset: slot for slot, offset in enumerate(ring_offsets(count))}
    down = [shift(firsts[-1], -1, count), None]
    up = [None, shift(seconds[-1], 1, count)]
    for distance in range(half - 1, 0, -1):
        for side, sums in ((-1, down), (1, up)):
            slot = places[side * distance]
            for which, parts in enumerate((firsts, seconds)):
                part = parts[slot]
                if sums[which] is not None:
                    part = add_rounded(part, sums[which])
                sums[which] = shift(part, side, count)
    return (firsts[0], down[0], up[0]), (seconds[0], down[1], up[1])


def ring_total(rows, count):
    height, width = rows.shape
    if height % (8 * count) or width % LANES:
        return lax.psum(rows, "ctx").astype(f32)
    part = height // count
    cut = (width // LANES + 1) // 2 * LANES
    place = ring_place(lax.axis_index("ctx"), count)
    pieces = []
    for offset in ring_offsets(count):
        start = ((place + offset) % count) * part
        pieces.append(lax.dynamic_slice_in_dim(rows, start, part, 0))
    firsts = [piece[:, :cut] for piece in pieces]
    seconds = [piece[:, cut:] for piece in pieces]
    sums = ring_scatter(firsts, seconds, count)
    first, second = (
        (own.astype(f32) + one.astype(f32) + other.astype(f32)).astype(bf16)
        for own, one, other in sums
    )
    firsts, seconds = ring_gather(first, second, count)
    by_offset = {offset % count: slot for slot, offset in enumerate(ring_offsets(count))}
    line = [
        jnp.concatenate([firsts[by_offset[i]], seconds[by_offset[i]]], axis=1)
        for i in range(count)
    ]
    twice = jnp.concatenate(line + line, axis=0)
    return lax.dynamic_slice_in_dim(
        twice, ((count - place) % count) * part, height, 0
    ).astype(f32)


def swap(array, mask):
    return lax.ppermute(array, "fsdp", [(i, i ^ mask) for i in range(4)])


def gather_pieces(piece):
    far = swap(piece, 2)
    return [piece, swap(piece, 1), far, swap(far, 1)]


def scatter_pieces(pieces):
    far = add_rounded(pieces[2], swap(pieces[3], 1))
    near = swap(pieces[1], 1)
    return (pieces[0].astype(f32) + near.astype(f32) + swap(far, 2).astype(f32)).astype(bf16)


def in_order(pieces, me):
    odd = (me % 2) == 1
    high = (me // 2) == 1
    low_pair = [jnp.where(odd, pieces[1], pieces[0]), jnp.where(odd, pieces[0], pieces[1])]
    high_pair = [jnp.where(odd, pieces[3], pieces[2]), jnp.where(odd, pieces[2], pieces[3])]
    first = [jnp.where(high, b, a) for a, b in zip(low_pair, high_pair)]
    last = [jnp.where(high, a, b) for a, b in zip(low_pair, high_pair)]
    return jnp.concatenate(first + last, axis=0)


def out_of_order(whole, me):
    rows = whole.shape[0] // 4
    return [lax.dynamic_slice_in_dim(whole, (me ^ i) * rows, rows, 0) for i in range(4)]


def swap_halves(block):
    lane = lax.broadcasted_iota(jnp.int32, block.shape, 1)
    ahead = pltpu.roll(block, block.shape[1] - HEAD_DIM // 2, 1)
    behind = pltpu.roll(block, HEAD_DIM // 2, 1)
    return jnp.where(lane % HEAD_DIM < HEAD_DIM // 2, ahead, behind)


def normalise(rows):
    mean_value = jnp.mean(rows, axis=-1, keepdims=True)
    centered = rows - mean_value
    spread = jnp.mean(centered * centered, axis=-1, keepdims=True)
    inverse = lax.rsqrt(spread + norm_eps)
    return centered * inverse, inverse


def kv_kernel(me, tokens, gains, w0, w1, w2, w3, cosine, sine, keys, values, normed, gain_by):
    step = pl.program_id(0)
    quarter = D // 4
    mine = me[0]

    @pl.when(step == 0)
    def _():
        unit, _ = normalise(tokens[...].astype(f32))
        for i in range(4):
            gain_by[mine ^ i] = gains[i, 0:1, :]
        for i in range(4):
            normed[i] = (unit[:, i * quarter : (i + 1) * quarter] * gain_by[i]).astype(bf16)

    total = None
    for i, weight in enumerate((w0, w1, w2, w3)):
        part = dot(normed[mine ^ i], weight[...], 1, 0)
        total = part if total is None else total + part
    half = pl.num_programs(0) // 2

    @pl.when(step < half)
    def _():
        for i in range(COLS // LANES):
            columns = slice(i * LANES, (i + 1) * LANES)
            block = total[:, columns]
            keys[:, columns] = (
                block * cosine[...] + swap_halves(block) * sine[...]
            ).astype(bf16)

    @pl.when(step >= half)
    def _():
        values[...] = total.astype(bf16)


def project_kv(me, tokens, gains, weights, cosine, sine):
    rows = tokens.shape[0]
    half = D // COLS

    def fixed(*shape):
        return pl.BlockSpec(shape, lambda j: (0,) * len(shape))

    return pl.pallas_call(
        kv_kernel,
        grid=(2 * half,),
        in_specs=[SMEM, fixed(rows, D), fixed(*gains.shape)]
        + [pl.BlockSpec((D // 4, COLS), lambda j: (0, j))] * 4
        + [fixed(rows, LANES)] * 2,
        out_specs=[
            pl.BlockSpec((rows, COLS), lambda j: (0, jnp.minimum(j, half - 1))),
            pl.BlockSpec((rows, COLS), lambda j: (0, jnp.maximum(j - half, 0))),
            fixed(4, rows, D // 4),
        ],
        out_shape=[
            jax.ShapeDtypeStruct((rows, D), bf16),
            jax.ShapeDtypeStruct((rows, D), bf16),
            jax.ShapeDtypeStruct((4, rows, D // 4), bf16),
        ],
        scratch_shapes=[pltpu.VMEM((4, 1, D // 4), f32)],
        compiler_params=params(32),
        cost_estimate=cost(4 * rows * D * D, 4 * D * D),
        name="project_kv",
    )(me, tokens, gains, *weights, cosine, sine)


def q_kernel(me, normed, w0, w1, w2, w3, cosine, sine, queries):
    mine = me[0]
    total = None
    for i, weight in enumerate((w0, w1, w2, w3)):
        part = dot(normed[mine ^ i], weight[...], 1, 0)
        total = part if total is None else total + part
    for i in range(COLS // LANES):
        columns = slice(i * LANES, (i + 1) * LANES)
        block = total[:, columns]
        queries[:, columns] = (block * cosine[...] + swap_halves(block) * sine[...]).astype(bf16)


def project_q(me, normed, weights, cosine, sine):
    rows = normed.shape[1]

    def fixed(*shape):
        return pl.BlockSpec(shape, lambda j: (0,) * len(shape))

    return pl.pallas_call(
        q_kernel,
        grid=(D // COLS,),
        in_specs=[SMEM, fixed(4, rows, D // 4)]
        + [pl.BlockSpec((D // 4, COLS), lambda j: (0, j))] * 4
        + [fixed(rows, LANES)] * 2,
        out_specs=pl.BlockSpec((rows, COLS), lambda j: (0, j)),
        out_shape=jax.ShapeDtypeStruct((rows, D), bf16),
        compiler_params=params(32),
        cost_estimate=cost(2 * rows * D * D, 2 * D * D),
        name="project_q",
    )(me, normed, *weights, cosine, sine)


def stacked(block, factor=None):
    if factor is not None:
        block = block * jnp.asarray(factor, block.dtype)
    lane = lax.broadcasted_iota(jnp.int32, block.shape, 1)
    zero = jnp.zeros_like(block)
    return jnp.concatenate(
        [jnp.where(lane < HEAD_DIM, block, zero), jnp.where(lane < HEAD_DIM, zero, block)], axis=0
    )


def unstacked(block):
    rows = block.shape[0] // 2
    lane = lax.broadcasted_iota(jnp.int32, (rows, block.shape[1]), 1)
    return jnp.where(lane < HEAD_DIM, block[:rows], block[rows:])


def causal(scores):
    rows, columns = scores.shape
    row = lax.broadcasted_iota(jnp.int32, scores.shape, 0) % (rows // 2)
    column = lax.broadcasted_iota(jnp.int32, scores.shape, 1)
    return jnp.where(column <= row, scores, neg_large)


def over_chunks(groups, per, visit):
    for group in range(groups):
        first = 1 if group == 0 else 0
        if per == 1:
            if first == 0:
                visit(group, 0, group)
        else:

            def turn(i, carry, group=group):
                visit(group, i, group * per + i)
                return carry

            lax.fori_loop(first, per, turn, 0)


def attend_kernel(groups, per, blocks, queries, *refs):
    keys, values = refs[:groups], refs[groups : 2 * groups]
    attended, exact, log_total, stack, scores, tops, totals, coarse_sum, fine_sum = refs[2 * groups :]
    width = queries.shape[0] // 2
    own = blocks[0]
    low, high = slice(0, width), slice(width, 2 * width)

    def picked(chunk):
        which = (blocks[chunk] > own).astype(jnp.int32)
        return which, pl.ds(pl.multiple_of(which * width, width), width)

    for i in range(2):
        stack[i] = stacked(queries[i * width : (i + 1) * width, :], SCALE)

    first = causal(dot(stack[0], keys[0][0, low, :], 1, 1))
    second = causal(dot(stack[1], keys[0][0, high, :], 1, 1))
    third = dot(stack[1], keys[0][0, low, :], 1, 1)
    scores[0], scores[1], scores[2] = first, second, third
    tops[0] = first
    tops[1] = jnp.maximum(second, third)

    def score(group, i, chunk):
        which, rows = picked(chunk)
        full = dot(stack[1], keys[group][i, low, :], 1, 1)
        scores[2 * chunk + 1] = full
        tops[1] = jnp.maximum(tops[1], full)
        part = dot(stack[which], keys[group][i, rows, :], 1, 1)
        scores[2 * chunk + 2] = part
        tops[which] = jnp.maximum(tops[which], part)

    over_chunks(groups, per, score)
    for i in range(2):
        tops[i] = jnp.broadcast_to(jnp.max(tops[i], axis=1, keepdims=True), tops.shape[1:])

    for i in range(3):
        scores[i] = jnp.exp(scores[i] - tops[min(i, 1)])
    totals[0] = scores[0]
    totals[1] = scores[1] + scores[2]

    def exponent(group, i, chunk):
        which, _ = picked(chunk)
        full = jnp.exp(scores[2 * chunk + 1] - tops[1])
        scores[2 * chunk + 1] = full
        totals[1] += full
        part = jnp.exp(scores[2 * chunk + 2] - tops[which])
        scores[2 * chunk + 2] = part
        totals[which] += part

    over_chunks(groups, per, exponent)
    for i in range(2):
        total = jnp.broadcast_to(jnp.sum(totals[i], axis=1, keepdims=True), totals.shape[1:])
        log_total[0, i] = tops[i] + jnp.log(total)
        totals[i] = 1.0 / total

    def weigh(slot, which, value_rows):
        probability = scores[slot] * totals[which]
        coarse = probability.astype(bf16)
        remainder = (probability - coarse.astype(f32)).astype(bf16)
        return dot(coarse, value_rows, 1, 0), dot(remainder, value_rows, 1, 0)

    coarse_sum[0], fine_sum[0] = weigh(0, 0, values[0][0, low, :])
    one = weigh(1, 1, values[0][0, high, :])
    two = weigh(2, 1, values[0][0, low, :])
    coarse_sum[1], fine_sum[1] = one[0] + two[0], one[1] + two[1]

    def collect(group, i, chunk):
        which, rows = picked(chunk)
        coarse, fine = weigh(2 * chunk + 1, 1, values[group][i, low, :])
        coarse_sum[1] += coarse
        fine_sum[1] += fine
        coarse, fine = weigh(2 * chunk + 2, which, values[group][i, rows, :])
        coarse_sum[which] += coarse
        fine_sum[which] += fine

    over_chunks(groups, per, collect)
    for i, rows in enumerate((low, high)):
        attended[rows, :] = unstacked(coarse_sum[i]).astype(bf16)
        exact[rows, :] = unstacked(coarse_sum[i] + fine_sum[i])


def attend(blocks, queries, keys, values):
    rows = queries.shape[0]
    groups, per = len(keys), keys[0].shape[0]
    count = groups * per
    column = pl.BlockSpec((rows, LANES), lambda j: (0, j))
    chunk = pl.BlockSpec((per, rows, LANES), lambda j: (0, 0, j))
    stat = pltpu.VMEM((2, rows, LANES), f32)
    return pl.pallas_call(
        partial(attend_kernel, groups, per),
        grid=(PAIRS,),
        in_specs=[SMEM, column] + [chunk] * (2 * groups),
        out_specs=[column, column, pl.BlockSpec((1, 2, rows, LANES), lambda j: (j, 0, 0, 0))],
        out_shape=[
            jax.ShapeDtypeStruct((rows, D), bf16),
            jax.ShapeDtypeStruct((rows, D), f32),
            jax.ShapeDtypeStruct((PAIRS, 2, rows, LANES), f32),
        ],
        scratch_shapes=[
            pltpu.VMEM((2, rows, LANES), bf16),
            pltpu.VMEM((2 * count + 1, rows, LANES), f32),
            stat,
            stat,
            stat,
            stat,
        ],
        compiler_params=params(56),
        cost_estimate=cost(6 * rows * rows * count * D, 4 * rows * count * D, rows * rows * 6 * count),
        name="attend",
    )(blocks, queries, *keys, *values)


def attend_back_kernel(groups, per, blocks, queries, grads, exact, log_total, cosine, sine, *refs):
    keys, values = refs[:groups], refs[groups : 2 * groups]
    grad_queries = refs[2 * groups]
    grad_keys = refs[2 * groups + 1 : 3 * groups + 1]
    grad_values = refs[3 * groups + 1 : 4 * groups + 1]
    stack, grad_stack, deltas, query_sum = refs[4 * groups + 1 :]
    width = queries.shape[0] // 2
    own = blocks[0]
    low, high = slice(0, width), slice(width, 2 * width)

    for i, rows in enumerate((low, high)):
        stack[i] = stacked(queries[rows, :], SCALE)
        grad_rows = stacked(grads[rows, :])
        grad_stack[i] = grad_rows
        twice = jnp.concatenate([exact[rows, :], exact[rows, :]], axis=0)
        delta = jnp.sum(grad_rows.astype(f32) * twice, axis=1, keepdims=True)
        deltas[i] = jnp.broadcast_to(delta, deltas.shape[1:])

    def block(which, key_rows, value_rows, diagonal=False):
        query_rows, grad_rows = stack[which], grad_stack[which]
        raw = dot(query_rows, key_rows, 1, 1)
        if diagonal:
            raw = causal(raw)
        probability = jnp.exp(raw - log_total[0, which])
        grad_prob = dot(grad_rows, value_rows, 1, 1)
        grad_scores = (probability * (grad_prob - deltas[which])).astype(bf16)
        return (
            dot(grad_scores, key_rows, 1, 0),
            dot(grad_scores, query_rows, 0, 0),
            dot(probability.astype(bf16), grad_rows, 0, 0),
        )

    key_low, value_low = keys[0][0, low, :], values[0][0, low, :]
    query_one, key_one, value_one = block(0, key_low, value_low, True)
    query_two, key_two, value_two = block(1, keys[0][0, high, :], values[0][0, high, :], True)
    query_all, key_all, value_all = block(1, key_low, value_low)
    query_sum[0] = query_one
    query_sum[1] = query_two + query_all
    grad_keys[0][0, low, :] = (key_one + key_all).astype(bf16)
    grad_values[0][0, low, :] = (value_one + value_all).astype(bf16)
    grad_keys[0][0, high, :] = key_two.astype(bf16)
    grad_values[0][0, high, :] = value_two.astype(bf16)

    def visit(group, i, chunk):
        up = blocks[chunk] > own
        which = up.astype(jnp.int32)
        rows = pl.ds(pl.multiple_of(which * width, width), width)
        query_all, key_all, value_all = block(1, keys[group][i, low, :], values[group][i, low, :])
        query_sum[1] += query_all
        query_one, key_one, value_one = block(
            which, keys[group][i, rows, :], values[group][i, rows, :]
        )
        query_sum[which] += query_one
        for target, whole, part in (
            (grad_keys[group], key_all, key_one),
            (grad_values[group], value_all, value_one),
        ):
            zero = jnp.zeros_like(part)
            target[i, low, :] = (whole + jnp.where(up, zero, part)).astype(bf16)
            target[i, high, :] = jnp.where(up, part, zero).astype(bf16)

    over_chunks(groups, per, visit)
    for i, rows in enumerate((low, high)):
        grad = unstacked(query_sum[i]) * SCALE
        turned = grad * cosine[rows, :] - swap_halves(grad) * sine[rows, :]
        grad_queries[rows, :] = turned.astype(bf16)


def attend_back(blocks, queries, grads, exact, log_total, cosine, sine, keys, values):
    rows = queries.shape[0]
    groups, per = len(keys), keys[0].shape[0]
    count = groups * per
    column = pl.BlockSpec((rows, LANES), lambda j: (0, j))
    table = pl.BlockSpec((rows, LANES), lambda j: (0, 0))
    chunk = pl.BlockSpec((per, rows, LANES), lambda j: (0, 0, j))
    stat = pltpu.VMEM((2, rows, LANES), f32)
    half = pltpu.VMEM((2, rows, LANES), bf16)
    result = pl.pallas_call(
        partial(attend_back_kernel, groups, per),
        grid=(PAIRS,),
        in_specs=[SMEM, column, column, column]
        + [pl.BlockSpec((1, 2, rows, LANES), lambda j: (j, 0, 0, 0)), table, table]
        + [chunk] * (2 * groups),
        out_specs=[column] + [chunk] * (2 * groups),
        out_shape=[jax.ShapeDtypeStruct((rows, D), bf16)]
        + [jax.ShapeDtypeStruct((per, rows, D), bf16)] * (2 * groups),
        scratch_shapes=[half, half, stat, stat],
        compiler_params=params(56),
        cost_estimate=cost(10 * rows * rows * count * D, 8 * rows * count * D, rows * rows * 6 * count),
        name="attend_back",
    )(blocks, queries, grads, exact, log_total, cosine, sine, *keys, *values)
    return result[0], result[1 : groups + 1], result[groups + 1 :]


def q_back_kernel(me, normed, grads, w0, w1, w2, w3, g0, g1, g2, g3, back):
    mine = me[0]
    step = pl.program_id(0)
    block = grads[...]
    for i, (weight, target) in enumerate(((w0, g0), (w1, g1), (w2, g2), (w3, g3))):
        target[...] = dot(normed[mine ^ i], block, 0, 0).astype(bf16)
        part = dot(block, weight[...], 1, 1)

        @pl.when(step == 0)
        def _(i=i, part=part):
            back[mine ^ i] = part

        @pl.when(step > 0)
        def _(i=i, part=part):
            back[mine ^ i] += part


def q_back(me, normed, grads, weights):
    rows = grads.shape[0]

    def fixed(*shape):
        return pl.BlockSpec(shape, lambda j: (0,) * len(shape))

    column = pl.BlockSpec((D // 4, COLS), lambda j: (0, j))
    result = pl.pallas_call(
        q_back_kernel,
        grid=(D // COLS,),
        in_specs=[SMEM, fixed(4, rows, D // 4), pl.BlockSpec((rows, COLS), lambda j: (0, j))]
        + [column] * 4,
        out_specs=[column] * 4 + [fixed(4, rows, D // 4)],
        out_shape=[jax.ShapeDtypeStruct((D // 4, D), bf16)] * 4
        + [jax.ShapeDtypeStruct((4, rows, D // 4), f32)],
        compiler_params=params(32),
        cost_estimate=cost(4 * rows * D * D, 4 * D * D),
        name="q_back",
    )(me, normed, grads, *weights)
    return result[:4], result[4]


def kv_back_kernel(
    me, normed, k_own, k_one, k_two, v_own, v_one, v_two, w0, w1, w2, w3, cosine, sine,
    start, tokens, gains, grad_middle, g0, g1, g2, g3, grad_tokens, grad_gain, back, gain_by, block_of,
):
    mine = me[0]
    step = pl.program_id(0)
    last = pl.num_programs(0) - 1
    half = pl.num_programs(0) // 2
    quarter = D // 4

    @pl.when(step == 0)
    def _():
        back[...] = start[...]

    @pl.when(step < half)
    def _():
        total = k_own[...].astype(f32) + k_one[...].astype(f32) + k_two[...].astype(f32)
        for i in range(COLS // LANES):
            columns = slice(i * LANES, (i + 1) * LANES)
            part = total[:, columns]
            turned = part * cosine[...] - swap_halves(part) * sine[...]
            block_of[:, columns] = turned.astype(bf16)

    @pl.when(step >= half)
    def _():
        total = v_own[...].astype(f32) + v_one[...].astype(f32) + v_two[...].astype(f32)
        block_of[...] = total.astype(bf16)

    block = block_of[...]
    for i, (weight, target) in enumerate(((w0, g0), (w1, g1), (w2, g2), (w3, g3))):
        target[...] = dot(normed[mine ^ i], block, 0, 0).astype(bf16)
        back[mine ^ i] += dot(block, weight[...], 1, 1)

    @pl.when(step == last)
    def _():
        unit, inverse = normalise(tokens[...].astype(f32))
        for i in range(4):
            gain_by[mine ^ i] = gains[i, 0:1, :]
        incoming = jnp.concatenate([back[i] for i in range(4)], axis=1)
        gain = jnp.concatenate([gain_by[i] for i in range(4)], axis=1)
        grad_gain[...] = jnp.sum(incoming * unit, axis=0, keepdims=True)
        scaled = incoming * gain
        mean_one = jnp.mean(scaled, axis=-1, keepdims=True)
        mean_two = jnp.mean(scaled * unit, axis=-1, keepdims=True)
        grad_tokens[...] = grad_middle[...] + inverse * (scaled - mean_one - unit * mean_two)


def kv_back(me, normed, key_sums, value_sums, weights, cosine, sine, start, tokens, gains, grad_middle):
    rows = tokens.shape[0]
    half = D // COLS

    def fixed(*shape):
        return pl.BlockSpec(shape, lambda j: (0,) * len(shape))

    column = pl.BlockSpec((D // 4, COLS), lambda j: (0, j))
    key_block = pl.BlockSpec((rows, COLS), lambda j: (0, jnp.minimum(j, half - 1)))
    value_block = pl.BlockSpec((rows, COLS), lambda j: (0, jnp.maximum(j - half, 0)))
    result = pl.pallas_call(
        kv_back_kernel,
        grid=(2 * half,),
        in_specs=[SMEM, fixed(4, rows, D // 4)]
        + [key_block] * 3
        + [value_block] * 3
        + [column] * 4
        + [fixed(rows, LANES)] * 2
        + [fixed(4, rows, D // 4), fixed(rows, D), fixed(*gains.shape), fixed(rows, D)],
        out_specs=[column] * 4 + [fixed(rows, D), fixed(1, D)],
        out_shape=[jax.ShapeDtypeStruct((D // 4, 2 * D), bf16)] * 4
        + [jax.ShapeDtypeStruct((rows, D), f32), jax.ShapeDtypeStruct((1, D), f32)],
        scratch_shapes=[
            pltpu.VMEM((4, rows, D // 4), f32),
            pltpu.VMEM((4, 1, D // 4), f32),
            pltpu.VMEM((rows, COLS), bf16),
        ],
        compiler_params=params(32),
        cost_estimate=cost(8 * rows * D * D, 8 * D * D),
        name="kv_back",
    )(me, normed, *key_sums, *value_sums, *weights, cosine, sine, start, tokens, gains, grad_middle)
    return result[:4], result[4], result[5]


def layer_norm(token_rows, gain_row):
    mean_value = jnp.mean(token_rows, axis=-1, keepdims=True)
    centered = token_rows - mean_value
    spread = jnp.mean(centered * centered, axis=-1, keepdims=True)
    return centered * lax.rsqrt(spread + norm_eps) * gain_row


def geglu(gate_part, up_part):
    return jax.nn.gelu(gate_part, approximate=False) * up_part


def rope_tables(positions):
    half = HEAD_DIM // 2
    frequency = theta_base ** (-2.0 * jnp.arange(half, dtype=f32) / HEAD_DIM)
    angles = positions.astype(f32)[:, None] * frequency[None, :]
    cosine, sine = jnp.cos(angles), jnp.sin(angles)
    return (
        jnp.concatenate([cosine] * 4, axis=1),
        jnp.concatenate([-sine, sine, -sine, sine], axis=1),
    )


def on_device(
    tokens,
    pair_order,
    norm_one,
    qkv_weight,
    out_weight,
    norm_two,
    gateup_weight,
    down_weight,
    cotangent,
):
    count = lax.axis_size("ctx")
    me = lax.axis_index("fsdp")
    me_row = jnp.reshape(me, (1,)).astype(jnp.int32)
    place = ring_place(lax.axis_index("ctx"), count)
    width = tokens.shape[1] // 2
    offsets = jnp.asarray(ring_offsets(count), jnp.int32)
    chunk_devices = ring_device((place + offsets) % count, count)
    blocks = jnp.sum(
        jnp.where(
            chunk_devices[:, None] == jnp.arange(count, dtype=jnp.int32)[None, :],
            pair_order[None, :],
            0,
        ),
        axis=1,
    )
    low_block = blocks[0]
    high_block = 2 * count - 1 - low_block
    within = jnp.arange(width, dtype=jnp.int32)
    positions = jnp.concatenate([low_block * width + within, high_block * width + within])
    cosine, sine = rope_tables(positions)

    gains = jnp.stack(gather_pieces(jnp.stack([norm_one, norm_two]).astype(f32)))
    kv_weights = gather_pieces(qkv_weight[:, D:])
    q_weights = gather_pieces(qkv_weight[:, :D])
    out_pieces = gather_pieces(out_weight)
    gateup_pieces = gather_pieces(gateup_weight)
    down_pieces = gather_pieces(down_weight)

    token_rows = tokens[0]
    keys, values, normed = project_kv(me_row, token_rows, gains, kv_weights, cosine, sine)
    all_keys, all_values = ring_gather(keys, values, count)
    queries = project_q(me_row, normed, q_weights, cosine, sine)
    per = max(1, count // 8)
    group_keys = [jnp.stack(all_keys[i : i + per]) for i in range(0, count, per)]
    group_values = [jnp.stack(all_values[i : i + per]) for i in range(0, count, per)]
    attended, exact, log_total = attend(blocks, queries, group_keys, group_values)

    weight_out = in_order(out_pieces, me)
    weight_gateup = in_order(gateup_pieces, me)
    weight_down = in_order(down_pieces, me)
    gain_two = in_order([gains[i, 1] for i in range(4)], me)
    middle = token_rows.astype(f32) + jnp.dot(attended, weight_out, preferred_element_type=f32)
    normed_two_f, norm_pull_two = jax.vjp(layer_norm, middle, gain_two)
    normed_two = normed_two_f.astype(bf16)
    gateup = jnp.dot(normed_two, weight_gateup, preferred_element_type=f32)
    hidden_f, geglu_pull = jax.vjp(geglu, gateup[:, :FF], gateup[:, FF:])
    hidden = hidden_f.astype(bf16)
    result = middle + jnp.dot(hidden, weight_down, preferred_element_type=f32)
    grad_out = cotangent[0]
    acc_down = dot(hidden, grad_out, 0, 0).astype(bf16)
    grad_hidden = dot(grad_out, weight_down, 1, 1)
    grad_gate, grad_up = geglu_pull(grad_hidden)
    grad_gateup = jnp.concatenate([grad_gate, grad_up], axis=1).astype(bf16)
    acc_gateup = dot(normed_two, grad_gateup, 0, 0).astype(bf16)
    grad_normed_two = dot(grad_gateup, weight_gateup, 1, 1)
    grad_middle_part, grad_gain_two = norm_pull_two(grad_normed_two)
    grad_middle = grad_out.astype(f32) + grad_middle_part
    grad_branch = grad_middle.astype(bf16)
    acc_out = dot(attended, grad_branch, 0, 0).astype(bf16)
    grad_attended = dot(grad_branch, weight_out, 1, 1).astype(bf16)

    grad_queries, key_grads, value_grads = attend_back(
        blocks, queries, grad_attended, exact, log_total, cosine, sine, group_keys, group_values
    )
    key_list = [part[i] for part in key_grads for i in range(per)]
    value_list = [part[i] for part in value_grads for i in range(per)]
    key_sums, value_sums = ring_scatter(key_list, value_list, count)
    q_pieces, start = q_back(me_row, normed, grad_queries, q_weights)

    def fold(piece):
        top, rest = piece[: D // 4], piece[D // 4 :]
        return jnp.concatenate(
            [top, jnp.concatenate([rest[:, : D // 2], rest[:, D // 2 :]], axis=0)], axis=1
        )

    def unfold(piece):
        top, rest = piece[:, :D], piece[:, D:]
        return jnp.concatenate(
            [top, jnp.concatenate([rest[: D // 8], rest[D // 8 :]], axis=1)], axis=0
        )

    packed = [
        jnp.concatenate([part[0], part[1], fold(part[2]), part[3]], axis=1)
        for part in zip(
            out_of_order(acc_gateup, me), out_of_order(acc_out, me), out_of_order(acc_down, me), q_pieces
        )
    ]
    middle_total = ring_total(scatter_pieces(packed), count)

    kv_pieces, grad_tokens, grad_gain_one = kv_back(
        me_row, normed, key_sums, value_sums, kv_weights, cosine, sine, start, token_rows, gains, grad_middle
    )
    kv_total = ring_total(scatter_pieces(kv_pieces), count)
    gain_grads = lax.psum(jnp.stack([grad_gain_one[0], grad_gain_two]), ("ctx", "fsdp"))
    gain_own = lax.dynamic_slice_in_dim(gain_grads, me * (D // 4), D // 4, 1)
    ends = (3 * D, 4 * D, 4 * D + FF, 5 * D + FF)
    return (
        result.astype(bf16)[None],
        grad_tokens[None],
        gain_own[0],
        jnp.concatenate([middle_total[:, ends[2] : ends[3]], kv_total], axis=1),
        middle_total[:, ends[0] : ends[1]],
        gain_own[1],
        middle_total[:, : ends[0]],
        unfold(middle_total[:, ends[1] : ends[2]]),
    )


def solution(mesh):
    return jax.shard_map(
        on_device,
        mesh=mesh,
        in_specs=(
            P("fsdp", "ctx", None),
            P(),
            P("fsdp"),
            P("fsdp", None),
            P("fsdp", None),
            P("fsdp"),
            P("fsdp", None),
            P("fsdp", None),
            P("fsdp", "ctx", None),
        ),
        out_specs=(
            P("fsdp", "ctx", None),
            P("fsdp", "ctx", None),
            P("fsdp"),
            P("fsdp", None),
            P("fsdp", None),
            P("fsdp"),
            P("fsdp", None),
            P("fsdp", None),
        ),
        check_vma=False,
    )
```

```python
from functools import partial

import jax
import jax.numpy as jnp
from jax import lax
from jax.experimental import pallas as pl
from jax.experimental.pallas import tpu as pltpu
from jax.sharding import PartitionSpec as P

D = 768
HEAD_DIM = 64
FF = 1152
LANES = 128
PAIRS = D // LANES
COLS = 256
SCALE = HEAD_DIM**-0.5

theta_base = 160000.0
norm_eps = 1e-05
neg_large = -1e30
f32 = jnp.float32
bf16 = jnp.bfloat16

SMEM = pl.BlockSpec(memory_space=pltpu.SMEM)
WHOLE = pl.BlockSpec(memory_space=pltpu.VMEM)


def params(megabytes):
    return pltpu.CompilerParams(vmem_limit_bytes=megabytes * 2**20)


def cost(microseconds):
    return pl.CostEstimate(flops=int(microseconds * 1.15e9), bytes_accessed=1000, transcendentals=0)


def dot(left, right, left_dim, right_dim):
    return lax.dot_general(
        left, right, (((left_dim,), (right_dim,)), ((), ())), preferred_element_type=f32
    )


def ring_device(place, count):
    return jnp.where(place < count // 2, 2 * place, 2 * (count - 1 - place) + 1)


def ring_place(device, count):
    return jnp.where(device % 2 == 0, device // 2, count - 1 - device // 2)


def shift(array, step, count):
    half = count // 2
    order = [2 * i if i < half else 2 * (count - 1 - i) + 1 for i in range(count)]
    pairs = [(order[i], order[(i + step) % count]) for i in range(count)]
    return lax.ppermute(array, "ctx", pairs)


def ring_offsets(count):
    half = count // 2
    offsets = [0]
    for distance in range(1, half):
        offsets += [-distance, distance]
    return offsets + [half]


def ring_gather(first, second, count):
    half = count // 2
    firsts, seconds = [first], [second]
    up, down = (first, second), (first, second)
    for _ in range(1, half):
        up = tuple(shift(part, 1, count) for part in up)
        down = tuple(shift(part, -1, count) for part in down)
        firsts += [up[0], down[0]]
        seconds += [up[1], down[1]]
    firsts.append(shift(up[0], 1, count))
    seconds.append(shift(down[1], -1, count))
    return firsts, seconds


def add_rounded(left, right):
    return (left.astype(f32) + right.astype(f32)).astype(bf16)


class RingTotal:
    def __init__(self, rows, count):
        self.rows, self.count = rows, count
        self.half = count // 2
        self.place = ring_place(lax.axis_index("ctx"), count)
        self.part = rows.shape[0] // count
        self.fits = rows.shape[0] % (8 * count) == 0
        self.hops = 2 * self.half if self.fits else 0
        self.done = 0
        self.up = self.down = None
        self.parts = [None] * count
        if not self.fits:
            self.total = lax.psum(rows, "ctx")

    def piece(self, offset):
        start = ((self.place + offset) % self.count) * self.part
        return lax.dynamic_slice_in_dim(self.rows, start, self.part, 0)

    def state(self):
        return [array for array in (self.up, self.down) if array is not None]

    def hop(self, earlier=()):
        if self.done >= self.hops:
            return
        self.done += 1
        if self.done <= self.half:
            distance = self.half + 1 - self.done
            down = self.piece(-distance)
            down = down if self.down is None else add_rounded(down, self.down)
            up = None
            if distance < self.half:
                up = self.piece(distance)
                up = up if self.up is None else add_rounded(up, self.up)
        else:
            if self.done == self.half + 1:
                own = self.piece(0).astype(f32) + self.down.astype(f32) + self.up.astype(f32)
                self.up = self.down = self.parts[0] = own.astype(bf16)
            distance = self.done - self.half
            up, down = self.up, (self.down if distance < self.half else None)
            if distance == self.half:
                self.down = None
        if earlier:
            up, down, _ = lax.optimization_barrier((up, down, earlier))
        if self.done <= self.half:
            self.down = shift(down, -1, self.count)
            if up is not None:
                self.up = shift(up, 1, self.count)
        else:
            self.up = self.parts[self.count - distance] = shift(up, 1, self.count)
            if down is not None:
                self.down = self.parts[distance] = shift(down, -1, self.count)

    def columns(self, columns):
        if not self.fits:
            return self.total[:, columns].astype(f32)
        line = [one[:, columns] for one in self.parts]
        twice = jnp.concatenate(line + line, axis=0)
        start = ((self.count - self.place) % self.count) * self.part
        return lax.dynamic_slice_in_dim(twice, start, self.rows.shape[0], 0).astype(f32)


def swap(array, mask):
    return lax.ppermute(array, "fsdp", [(i, i ^ mask) for i in range(4)])


def gather_pieces(piece):
    far = swap(piece, 2)
    return [piece, swap(piece, 1), far, swap(far, 1)]


def core_sums(pieces):
    near, far = swap(pieces[1], 1), swap(pieces[3], 1)
    return (pieces[0], near), add_all([(pieces[2], far)])[0]


def add_all(groups):
    return [sum(part.astype(f32) for part in group).astype(bf16) for group in groups]


def after(array, earlier):
    return lax.optimization_barrier((array, earlier))[0]


def in_order(pieces, me):
    odd = (me % 2) == 1
    high = (me // 2) == 1
    low_pair = [jnp.where(odd, pieces[1], pieces[0]), jnp.where(odd, pieces[0], pieces[1])]
    high_pair = [jnp.where(odd, pieces[3], pieces[2]), jnp.where(odd, pieces[2], pieces[3])]
    first = [jnp.where(high, b, a) for a, b in zip(low_pair, high_pair)]
    last = [jnp.where(high, a, b) for a, b in zip(low_pair, high_pair)]
    return jnp.concatenate(first + last, axis=0)


def out_of_order(whole, me):
    rows = whole.shape[0] // 4
    return [lax.dynamic_slice_in_dim(whole, (me ^ i) * rows, rows, 0) for i in range(4)]


def swap_halves(block):
    lane = lax.broadcasted_iota(jnp.int32, block.shape, 1)
    ahead = pltpu.roll(block, block.shape[1] - HEAD_DIM // 2, 1)
    behind = pltpu.roll(block, HEAD_DIM // 2, 1)
    return jnp.where(lane % HEAD_DIM < HEAD_DIM // 2, ahead, behind)


def normalise(rows):
    mean_value = jnp.mean(rows, axis=-1, keepdims=True)
    centered = rows - mean_value
    spread = jnp.mean(centered * centered, axis=-1, keepdims=True)
    inverse = lax.rsqrt(spread + norm_eps)
    return centered * inverse, inverse


def normed_times(normed, weights, mine):
    total = None
    for i, weight in enumerate(weights):
        part = dot(normed[mine ^ i], weight[: D // 4, :], 1, 0)
        total = part if total is None else total + part
    return total


def rotated(total, cosine, sine, target):
    for i in range(COLS // LANES):
        columns = slice(i * LANES, (i + 1) * LANES)
        block = total[:, columns]
        target[:, columns] = (block * cosine[...] + swap_halves(block) * sine[...]).astype(bf16)


def key_kernel(me, tokens, w0, w1, w2, w3, cosine, sine, keys, normed, gains):
    quarter = D // 4
    mine = me[0]
    weights = (w0, w1, w2, w3)

    @pl.when(pl.program_id(0) == 0)
    def _():
        unit, _ = normalise(tokens[...].astype(f32))
        for i, weight in enumerate(weights):
            gains[mine ^ i] = weight[quarter : quarter + 16, :quarter].astype(f32)[0:1, :]
        for i in range(4):
            normed[i] = (unit[:, i * quarter : (i + 1) * quarter] * gains[i]).astype(bf16)

    rotated(normed_times(normed, weights, mine), cosine, sine, keys)


def fixed(*shape):
    return pl.BlockSpec(shape, lambda j: (0,) * len(shape))


def project_keys(me, tokens, weights, cosine, sine):
    rows = tokens.shape[0]
    return pl.pallas_call(
        key_kernel,
        grid=(D // COLS,),
        in_specs=[SMEM, fixed(rows, D)]
        + [pl.BlockSpec((D // 4 + 16, COLS), lambda j: (0, j))] * 4
        + [fixed(rows, LANES)] * 2,
        out_specs=[
            pl.BlockSpec((rows, COLS), lambda j: (0, j)),
            fixed(4, rows, D // 4),
            fixed(4, 1, D // 4),
        ],
        out_shape=[
            jax.ShapeDtypeStruct((rows, D), bf16),
            jax.ShapeDtypeStruct((4, rows, D // 4), bf16),
            jax.ShapeDtypeStruct((4, 1, D // 4), f32),
        ],
        compiler_params=params(32),
        cost_estimate=cost(2),
        name="project_keys",
    )(me, tokens, *weights, cosine, sine)


def query_kernel(me, normed, w0, w1, w2, w3, cosine, sine, queries):
    rotated(normed_times(normed, (w0, w1, w2, w3), me[0]), cosine, sine, queries)


def value_kernel(me, normed, w0, w1, w2, w3, values):
    values[...] = normed_times(normed, (w0, w1, w2, w3), me[0]).astype(bf16)


def project(me, normed, weights, tables=()):
    rows = normed.shape[1]
    return pl.pallas_call(
        query_kernel if tables else value_kernel,
        grid=(D // COLS,),
        in_specs=[SMEM, fixed(4, rows, D // 4)]
        + [pl.BlockSpec((D // 4, COLS), lambda j: (0, j))] * 4
        + [fixed(rows, LANES)] * len(tables),
        out_specs=pl.BlockSpec((rows, COLS), lambda j: (0, j)),
        out_shape=jax.ShapeDtypeStruct((rows, D), bf16),
        compiler_params=params(32),
        cost_estimate=cost(2),
        name="project_queries" if tables else "project_values",
    )(me, normed, *weights, *tables)


def stacked(block, factor=None):
    if factor is not None:
        block = block * jnp.asarray(factor, block.dtype)
    lane = lax.broadcasted_iota(jnp.int32, block.shape, 1)
    zero = jnp.zeros_like(block)
    return jnp.concatenate(
        [jnp.where(lane < HEAD_DIM, block, zero), jnp.where(lane < HEAD_DIM, zero, block)], axis=0
    )


def unstacked(block):
    rows = block.shape[0] // 2
    lane = lax.broadcasted_iota(jnp.int32, (rows, block.shape[1]), 1)
    return jnp.where(lane < HEAD_DIM, block[:rows], block[rows:])


def causal(scores):
    rows, columns = scores.shape
    row = lax.broadcasted_iota(jnp.int32, scores.shape, 0) % (rows // 2)
    column = lax.broadcasted_iota(jnp.int32, scores.shape, 1)
    return jnp.where(column <= row, scores, neg_large)


def over_chunks(groups, per, first, visit, carry):
    for group in range(groups):
        start = first if group == 0 else 0
        if per == 1:
            if start == 0:
                carry = visit(group, 0, group, carry)
        else:

            def turn(i, held, group=group):
                return visit(group, i, group * per + i, held)

            carry = lax.fori_loop(start, per, turn, carry)
    return carry


def by_head(stacked_column):
    return unstacked(jnp.broadcast_to(stacked_column, (stacked_column.shape[0], LANES)))


def of_heads(block):
    shape = block.shape
    return jnp.concatenate(
        [
            jnp.broadcast_to(block[:, :1], shape),
            jnp.broadcast_to(block[:, HEAD_DIM : HEAD_DIM + 1], shape),
        ],
        axis=0,
    )


def attend_kernel(groups, per, base, merge, blocks, queries, *refs):
    keys, values = refs[:groups], refs[groups : 2 * groups]
    rest = refs[2 * groups :]
    before, rest = (rest[:4], rest[4:]) if merge else ((), rest)
    results, (stack, scores) = rest[:-2], rest[-2:]
    width = queries.shape[0] // 2
    own = blocks[0]
    low, high = slice(0, width), slice(width, 2 * width)
    with_own = base == 0
    empty = jnp.full((2 * width, LANES), neg_large, f32)
    nothing = jnp.zeros((2 * width, LANES), f32)

    def picked(chunk):
        up = blocks[base + chunk] > own
        which = up.astype(jnp.int32)
        return up, which, pl.ds(pl.multiple_of(which * width, width), width)

    for i, rows in enumerate((low, high)):
        stack[i] = stacked(queries[rows, :], SCALE)

    tops = (empty, empty)
    if with_own:
        first = causal(dot(stack[0], keys[0][0, low, :], 1, 1))
        second = causal(dot(stack[1], keys[0][0, high, :], 1, 1))
        third = dot(stack[1], keys[0][0, low, :], 1, 1)
        scores[0], scores[1], scores[2] = first, second, third
        tops = (first, jnp.maximum(second, third))

    def score(group, i, chunk, held):
        up, which, rows = picked(chunk)
        full = dot(stack[1], keys[group][i, low, :], 1, 1)
        part = dot(stack[which], keys[group][i, rows, :], 1, 1)
        scores[2 * chunk + 1] = full
        scores[2 * chunk + 2] = part
        return (
            jnp.maximum(held[0], jnp.where(up, empty, part)),
            jnp.maximum(jnp.maximum(held[1], full), jnp.where(up, part, empty)),
        )

    tops = over_chunks(groups, per, int(with_own), score, tops)
    top_low, top_high = (jnp.max(top, axis=1, keepdims=True) for top in tops)

    def weigh(slot, top, value_rows):
        weight = jnp.exp(scores[slot] - top)
        coarse = weight.astype(bf16)
        fine = (weight - coarse.astype(f32)).astype(bf16)
        return (
            weight,
            unstacked(dot(coarse, value_rows, 1, 0)),
            unstacked(dot(fine, value_rows, 1, 0)),
        )

    def summed(*parts):
        return tuple(sum(terms[1:], terms[0]) for terms in zip(*parts))

    none = (nothing, nothing[low], nothing[low])
    sums = (none, none)
    if with_own:
        sums = (
            weigh(0, top_low, values[0][0, low, :]),
            summed(
                weigh(1, top_high, values[0][0, high, :]), weigh(2, top_high, values[0][0, low, :])
            ),
        )

    def collect(group, i, chunk, held):
        up, which, rows = picked(chunk)
        full = weigh(2 * chunk + 1, top_high, values[group][i, low, :])
        part = weigh(
            2 * chunk + 2, jnp.where(up, top_high, top_low), values[group][i, rows, :]
        )
        to_low = tuple(jnp.where(up, jnp.zeros_like(term), term) for term in part)
        to_high = tuple(jnp.where(up, term, jnp.zeros_like(term)) for term in part)
        return summed(held[0], to_low), summed(held[1], full, to_high)

    sums = over_chunks(groups, per, int(with_own), collect, sums)
    for rows, top, (weight, coarse, fine) in zip((low, high), (top_low, top_high), sums):
        top = by_head(top)
        total = by_head(jnp.sum(weight, axis=1, keepdims=True))
        exact = coarse + fine
        if merge:
            old_top, old_total, old_coarse, old_exact = (ref[rows, :] for ref in before)
            new_top = jnp.maximum(top, old_top)
            now, then = jnp.exp(top - new_top), jnp.exp(old_top - new_top)
            total = total * now + old_total * then
            inverse = 1.0 / total
            attended, exact_out, log_total = results
            attended[rows, :] = ((coarse * now + old_coarse * then) * inverse).astype(bf16)
            exact_out[rows, :] = (exact * now + old_exact * then) * inverse
            log_total[rows, :] = new_top + jnp.log(total)
        else:
            for ref, value in zip(results, (top, total, coarse, exact)):
                ref[rows, :] = value


def grouped(chunks):
    per = 1 if len(chunks) <= 8 else len(chunks) // 4
    if per == 1:
        return [chunk[None] for chunk in chunks]
    return [jnp.stack(chunks[i : i + per]) for i in range(0, len(chunks), per)]


def column_block(rows):
    return pl.BlockSpec((rows, LANES), lambda j: (0, j))


def attend(base, blocks, queries, key_chunks, value_chunks, before=()):
    rows = queries.shape[0]
    keys, values = grouped(key_chunks), grouped(value_chunks)
    groups, per, count = len(keys), keys[0].shape[0], len(key_chunks)
    column = column_block(rows)
    chunk = pl.BlockSpec((per, rows, LANES), lambda j: (0, 0, j))
    types = (bf16, f32, f32) if before else (f32,) * 4
    return pl.pallas_call(
        partial(attend_kernel, groups, per, base, bool(before)),
        grid=(PAIRS,),
        in_specs=[SMEM, column] + [chunk] * (2 * groups) + [column] * len(before),
        out_specs=[column] * len(types),
        out_shape=[jax.ShapeDtypeStruct((rows, D), kind) for kind in types],
        scratch_shapes=[
            pltpu.VMEM((2, rows, LANES), bf16),
            pltpu.VMEM((2 * count + 1, rows, LANES), f32),
        ],
        compiler_params=params(56),
        cost_estimate=cost(2 * count),
        name=f"attend_{base}",
    )(blocks, queries, *keys, *values, *before)


def attend_back_kernel(groups, per, base, carried, blocks, queries, grads, exact, log_total, *refs):
    keys, values = refs[:groups], refs[groups : 2 * groups]
    rest = refs[2 * groups :]
    before, rest = (rest[:1], rest[1:]) if carried else ((), rest)
    with_own = base == 0
    (cosine, sine), rest = (rest[:2], rest[2:]) if with_own else ((None, None), rest)
    grad_queries = rest[0]
    grad_keys = rest[1 : groups + 1]
    grad_values = rest[groups + 1 : 2 * groups + 1]
    stack, grad_stack, deltas, logs = rest[2 * groups + 1 :]
    width = queries.shape[0] // 2
    own = blocks[0]
    low, high = slice(0, width), slice(width, 2 * width)

    for i, rows in enumerate((low, high)):
        stack[i] = stacked(queries[rows, :], SCALE)
        grad_rows = stacked(grads[rows, :])
        grad_stack[i] = grad_rows
        twice = jnp.concatenate([exact[rows, :], exact[rows, :]], axis=0)
        delta = jnp.sum(grad_rows.astype(f32) * twice, axis=1, keepdims=True)
        deltas[i] = jnp.broadcast_to(delta, deltas.shape[1:])
        logs[i] = of_heads(log_total[rows, :])

    def block(which, key_rows, value_rows, diagonal=False):
        query_rows, grad_rows = stack[which], grad_stack[which]
        raw = dot(query_rows, key_rows, 1, 1)
        if diagonal:
            raw = causal(raw)
        probability = jnp.exp(raw - logs[which])
        grad_prob = dot(grad_rows, value_rows, 1, 1)
        grad_scores = (probability * (grad_prob - deltas[which])).astype(bf16)
        return (
            unstacked(dot(grad_scores, key_rows, 1, 0)),
            dot(grad_scores, query_rows, 0, 0),
            dot(probability.astype(bf16), grad_rows, 0, 0),
        )

    if carried:
        sums = (before[0][low, :], before[0][high, :])
    else:
        sums = (jnp.zeros((width, LANES), f32),) * 2
    if with_own:
        key_low, value_low = keys[0][0, low, :], values[0][0, low, :]
        query_one, key_one, value_one = block(0, key_low, value_low, True)
        query_two, key_two, value_two = block(1, keys[0][0, high, :], values[0][0, high, :], True)
        query_all, key_all, value_all = block(1, key_low, value_low)
        sums = (sums[0] + query_one, sums[1] + query_two + query_all)
        grad_keys[0][0, low, :] = (key_one + key_all).astype(bf16)
        grad_values[0][0, low, :] = (value_one + value_all).astype(bf16)
        grad_keys[0][0, high, :] = key_two.astype(bf16)
        grad_values[0][0, high, :] = value_two.astype(bf16)

    def visit(group, i, chunk, held):
        up = blocks[base + chunk] > own
        which = up.astype(jnp.int32)
        rows = pl.ds(pl.multiple_of(which * width, width), width)
        query_all, key_all, value_all = block(1, keys[group][i, low, :], values[group][i, low, :])
        query_one, key_one, value_one = block(
            which, keys[group][i, rows, :], values[group][i, rows, :]
        )
        for target, whole, part in (
            (grad_keys[group], key_all, key_one),
            (grad_values[group], value_all, value_one),
        ):
            zero = jnp.zeros_like(part)
            target[i, low, :] = (whole + jnp.where(up, zero, part)).astype(bf16)
            target[i, high, :] = jnp.where(up, part, zero).astype(bf16)
        zero = jnp.zeros_like(query_one)
        return (
            held[0] + jnp.where(up, zero, query_one),
            held[1] + query_all + jnp.where(up, query_one, zero),
        )

    sums = over_chunks(groups, per, int(with_own), visit, sums)
    for rows, grad in zip((low, high), sums):
        if with_own:
            grad = grad * SCALE
            turned = grad * cosine[rows, :] - swap_halves(grad) * sine[rows, :]
            grad_queries[rows, :] = turned.astype(bf16)
        else:
            grad_queries[rows, :] = grad


def attend_back(base, blocks, queries, grads, exact, log_total, key_chunks, value_chunks, before, tables):
    rows = queries.shape[0]
    keys, values = grouped(key_chunks), grouped(value_chunks)
    groups, per, count = len(keys), keys[0].shape[0], len(key_chunks)
    column = column_block(rows)
    chunk = pl.BlockSpec((per, rows, LANES), lambda j: (0, 0, j))
    stat = pltpu.VMEM((2, rows, LANES), f32)
    half = pltpu.VMEM((2, rows, LANES), bf16)
    extra = (() if before is None else (before,)) + (tuple(tables) if base == 0 else ())
    extra_specs = ([] if before is None else [column]) + ([fixed(rows, LANES)] * 2 if base == 0 else [])
    result = pl.pallas_call(
        partial(attend_back_kernel, groups, per, base, before is not None),
        grid=(PAIRS,),
        in_specs=[SMEM] + [column] * 4 + [chunk] * (2 * groups) + extra_specs,
        out_specs=[column] + [chunk] * (2 * groups),
        out_shape=[jax.ShapeDtypeStruct((rows, D), bf16 if base == 0 else f32)]
        + [jax.ShapeDtypeStruct((per, rows, D), bf16)] * (2 * groups),
        scratch_shapes=[half, half, stat, stat],
        compiler_params=params(56),
        cost_estimate=cost(4.5 * count),
        name=f"attend_back_{base}",
    )(blocks, queries, grads, exact, log_total, *keys, *values, *extra)
    key_grads = [part[i] for part in result[1 : groups + 1] for i in range(per)]
    value_grads = [part[i] for part in result[groups + 1 :] for i in range(per)]
    return result[0], key_grads, value_grads


def q_back_kernel(me, normed, grads, w0, w1, w2, w3, g0, g1, g2, g3, back):
    mine = me[0]
    step = pl.program_id(0)
    block = grads[...]
    for i, (weight, target) in enumerate(((w0, g0), (w1, g1), (w2, g2), (w3, g3))):
        target[...] = dot(normed[mine ^ i], block, 0, 0).astype(bf16)
        part = dot(block, weight[...], 1, 1)

        @pl.when(step == 0)
        def _(i=i, part=part):
            back[mine ^ i] = part

        @pl.when(step > 0)
        def _(i=i, part=part):
            back[mine ^ i] += part


def q_back(me, normed, grads, weights):
    rows = grads.shape[0]

    column = pl.BlockSpec((D // 4, COLS), lambda j: (0, j))
    result = pl.pallas_call(
        q_back_kernel,
        grid=(D // COLS,),
        in_specs=[SMEM, fixed(4, rows, D // 4), pl.BlockSpec((rows, COLS), lambda j: (0, j))]
        + [column] * 4,
        out_specs=[column] * 4 + [fixed(4, rows, D // 4)],
        out_shape=[jax.ShapeDtypeStruct((D // 4, D), bf16)] * 4
        + [jax.ShapeDtypeStruct((4, rows, D // 4), f32)],
        compiler_params=params(32),
        cost_estimate=cost(4),
        name="q_back",
    )(me, normed, grads, *weights)
    return result[:4], result[4]


def middle_grads_kernel(me, normed, grad_gateup, attended, grad_branch, hidden, grad_out, gain, *refs):
    gateups, others = refs[:4], refs[4:8]
    normed_by, attended_by, hidden_by, gain_by = refs[8:]
    mine = me[0]
    quarter, part = D // 4, FF // 4
    ones = jnp.ones((normed.shape[0], LANES), bf16)
    coarse = gain[...].astype(bf16)
    fine = (gain[...] - coarse.astype(f32)).astype(bf16)
    for i in range(4):
        columns = slice(i * quarter, (i + 1) * quarter)
        normed_by[i] = normed[:, columns]
        attended_by[i] = attended[:, columns]
        hidden_by[i] = hidden[:, i * part : (i + 1) * part]
        gain_by[i] = dot(coarse[:, columns], ones, 0, 0) + dot(fine[:, columns], ones, 0, 0)
    for i in (3, 1, 2, 0):
        for first in range(0, 2 * FF, D):
            columns = slice(first, first + D)
            gateups[i][:, columns] = dot(normed_by[mine ^ i], grad_gateup[:, columns], 0, 0).astype(bf16)
        others[i][:, :D] = dot(attended_by[mine ^ i], grad_branch[...], 0, 0).astype(bf16)
        down = dot(hidden_by[mine ^ i], grad_out[...], 0, 0).astype(bf16)
        others[i][:, D : 2 * D] = down[:quarter]
        others[i][: quarter // 2, 2 * D : D + FF] = down[quarter:, : D // 2]
        others[i][quarter // 2 :, 2 * D : D + FF] = down[quarter:, D // 2 :]
        others[i][:, D + FF :] = gain_by[mine ^ i].astype(bf16)


def middle_grads(me, normed, grad_gateup, attended, grad_branch, hidden, grad_out, gain):
    rows = normed.shape[0]
    result = pl.pallas_call(
        middle_grads_kernel,
        in_specs=[SMEM] + [WHOLE] * 7,
        out_specs=[WHOLE] * 8,
        out_shape=[jax.ShapeDtypeStruct((D // 4, 2 * FF), bf16)] * 4
        + [jax.ShapeDtypeStruct((D // 4, D + FF + LANES), bf16)] * 4,
        scratch_shapes=[
            pltpu.VMEM((4, rows, D // 4), bf16),
            pltpu.VMEM((4, rows, D // 4), bf16),
            pltpu.VMEM((4, rows, FF // 4), bf16),
            pltpu.VMEM((4, D // 4, LANES), f32),
        ],
        compiler_params=params(32),
        cost_estimate=cost(4),
        name="middle_grads",
    )(me, normed, grad_gateup, attended, grad_branch, hidden, grad_out, gain)
    return result[:4], result[4:]


def kv_back_kernel(
    me, normed, k_own, k_one, k_two, v_own, v_one, v_two, k0, k1, k2, k3, v0, v1, v2, v3, cosine, sine,
    start, tokens, gains, grad_middle, g0, g1, g2, g3, grad_tokens, back, block_of,
):
    mine = me[0]
    step = pl.program_id(0)
    half = (pl.num_programs(0) - 1) // 2
    quarter = D // 4
    targets = (g0, g1, g2, g3)

    @pl.when(step == 0)
    def _():
        back[...] = start[...]

    @pl.when(step < half)
    def _():
        total = k_own[...].astype(f32) + k_one[...].astype(f32) + k_two[...].astype(f32)
        for i in range(COLS // LANES):
            columns = slice(i * LANES, (i + 1) * LANES)
            part = total[:, columns]
            turned = part * cosine[...] - swap_halves(part) * sine[...]
            block_of[:, columns] = turned.astype(bf16)
        for i, weight in enumerate((k0, k1, k2, k3)):
            targets[i][...] = dot(normed[mine ^ i], block_of[...], 0, 0).astype(bf16)
            back[mine ^ i] += dot(block_of[...], weight[:quarter, :], 1, 1)

    @pl.when((step >= half) & (step < 2 * half))
    def _():
        total = v_own[...].astype(f32) + v_one[...].astype(f32) + v_two[...].astype(f32)
        block = total.astype(bf16)
        for i, weight in enumerate((v0, v1, v2, v3)):
            targets[i][...] = dot(normed[mine ^ i], block, 0, 0).astype(bf16)
            back[mine ^ i] += dot(block, weight[...], 1, 1)

    @pl.when(step == 2 * half)
    def _():
        unit, inverse = normalise(tokens[...].astype(f32))
        ones = jnp.ones((unit.shape[0], COLS), bf16)
        for i in range(4):
            part = back[i] * unit[:, i * quarter : (i + 1) * quarter]
            coarse = part.astype(bf16)
            fine = (part - coarse.astype(f32)).astype(bf16)
            total = (dot(coarse, ones, 0, 0) + dot(fine, ones, 0, 0)).astype(bf16)
            for k in range(4):

                @pl.when((mine ^ k) == i)
                def _(k=k, total=total):
                    targets[k][...] = total

        incoming = jnp.concatenate([back[i] for i in range(4)], axis=1)
        gain = jnp.concatenate([gains[i] for i in range(4)], axis=1)
        scaled = incoming * gain
        mean_one = jnp.mean(scaled, axis=-1, keepdims=True)
        mean_two = jnp.mean(scaled * unit, axis=-1, keepdims=True)
        grad_tokens[...] = grad_middle[...] + inverse * (scaled - mean_one - unit * mean_two)


def kv_back(
    me, normed, key_sums, value_sums, k_weights, v_weights, cosine, sine, start, tokens, gains, grad_middle
):
    rows = tokens.shape[0]
    half = D // COLS

    def early(height):
        return pl.BlockSpec((height, COLS), lambda j: (0, jnp.minimum(j, half - 1)))

    def late(height):
        return pl.BlockSpec((height, COLS), lambda j: (0, jnp.clip(j - half, 0, half - 1)))

    result = pl.pallas_call(
        kv_back_kernel,
        grid=(2 * half + 1,),
        in_specs=[SMEM, fixed(4, rows, D // 4)]
        + [early(rows)] * 3
        + [late(rows)] * 3
        + [early(D // 4 + 16)] * 4
        + [late(D // 4)] * 4
        + [fixed(rows, LANES)] * 2
        + [fixed(4, rows, D // 4), fixed(rows, D), fixed(4, 1, D // 4), fixed(rows, D)],
        out_specs=[pl.BlockSpec((D // 4, COLS), lambda j: (0, j))] * 4 + [fixed(rows, D)],
        out_shape=[jax.ShapeDtypeStruct((D // 4, 2 * D + COLS), bf16)] * 4
        + [jax.ShapeDtypeStruct((rows, D), f32)],
        scratch_shapes=[
            pltpu.VMEM((4, rows, D // 4), f32),
            pltpu.VMEM((rows, COLS), bf16),
        ],
        compiler_params=params(32),
        cost_estimate=cost(8),
        name="kv_back",
    )(
        me, normed, *key_sums, *value_sums, *k_weights, *v_weights, cosine, sine, start, tokens, gains, grad_middle
    )
    return result[:4], result[4]


def layer_norm(token_rows, gain_row):
    mean_value = jnp.mean(token_rows, axis=-1, keepdims=True)
    centered = token_rows - mean_value
    spread = jnp.mean(centered * centered, axis=-1, keepdims=True)
    return centered * lax.rsqrt(spread + norm_eps) * gain_row


def geglu(gate_part, up_part):
    return jax.nn.gelu(gate_part, approximate=False) * up_part


def rope_tables(positions):
    half = HEAD_DIM // 2
    frequency = theta_base ** (-2.0 * jnp.arange(half, dtype=f32) / HEAD_DIM)
    angles = positions.astype(f32)[:, None] * frequency[None, :]
    cosine, sine = jnp.cos(angles), jnp.sin(angles)
    return (
        jnp.concatenate([cosine] * 4, axis=1),
        jnp.concatenate([-sine, sine, -sine, sine], axis=1),
    )


def on_device(
    tokens,
    pair_order,
    norm_one,
    qkv_weight,
    out_weight,
    norm_two,
    gateup_weight,
    down_weight,
    cotangent,
):
    count = lax.axis_size("ctx")
    me = lax.axis_index("fsdp")
    me_row = jnp.reshape(me, (1,)).astype(jnp.int32)
    gain_row = jnp.concatenate(
        [jnp.pad(norm_one, (0, COLS - D // 4)), jnp.pad(norm_two, (0, D - COLS - D // 4))]
    )
    gain_rows = jnp.broadcast_to(gain_row[None, :], (16, D))
    k_weights = gather_pieces(jnp.concatenate([qkv_weight[:, D : 2 * D], gain_rows], axis=0))
    v_weights = gather_pieces(after(qkv_weight[:, 2 * D :], k_weights[2]))
    q_weights = gather_pieces(after(qkv_weight[:, :D], v_weights[2]))
    out_pieces = gather_pieces(after(out_weight, q_weights[2]))
    gateup_pieces = gather_pieces(after(gateup_weight, out_pieces[2]))
    down_pieces = gather_pieces(after(down_weight, gateup_pieces[2]))
    pair_order = after(pair_order, k_weights[1])
    place = ring_place(lax.axis_index("ctx"), count)
    width = tokens.shape[1] // 2
    offsets = jnp.asarray(ring_offsets(count), jnp.int32)
    chunk_devices = ring_device((place + offsets) % count, count)
    blocks = jnp.sum(
        jnp.where(
            chunk_devices[:, None] == jnp.arange(count, dtype=jnp.int32)[None, :],
            pair_order[None, :],
            0,
        ),
        axis=1,
    )
    low_block = blocks[0]
    high_block = 2 * count - 1 - low_block
    within = jnp.arange(width, dtype=jnp.int32)
    positions = jnp.concatenate([low_block * width + within, high_block * width + within])
    cosine, sine = rope_tables(positions)

    token_rows = tokens[0]
    keys, normed, gains = project_keys(me_row, token_rows, k_weights, cosine, sine)
    values = project(me_row, normed, v_weights)
    all_keys, all_values = ring_gather(keys, values, count)
    queries = project(me_row, normed, q_weights, (cosine, sine))
    split = count - 3 if count == 8 else count // 2
    so_far = attend(0, blocks, queries, all_keys[:split], all_values[:split])
    attended, exact, log_total = attend(
        split, blocks, queries, all_keys[split:], all_values[split:], so_far
    )

    weight_out = in_order(out_pieces, me)
    weight_gateup = in_order(gateup_pieces, me)
    weight_down = in_order(down_pieces, me)
    gain_two = in_order([part[D // 4, COLS : COLS + D // 4] for part in k_weights], me).astype(f32)
    middle = token_rows.astype(f32) + jnp.dot(attended, weight_out, preferred_element_type=f32)
    normed_two = layer_norm(middle, gain_two).astype(bf16)
    gateup = jnp.dot(normed_two, weight_gateup, preferred_element_type=f32)
    hidden_f, geglu_pull = jax.vjp(geglu, gateup[:, :FF], gateup[:, FF:])
    hidden = hidden_f.astype(bf16)
    result = middle + jnp.dot(hidden, weight_down, preferred_element_type=f32)
    grad_out = cotangent[0]
    grad_hidden = dot(grad_out, weight_down, 1, 1)
    grad_gate, grad_up = geglu_pull(grad_hidden)
    grad_gateup = jnp.concatenate([grad_gate, grad_up], axis=1).astype(bf16)
    grad_normed_two = dot(grad_gateup, weight_gateup, 1, 1)
    unit_two, inverse_two = normalise(middle)
    scaled = grad_normed_two * gain_two
    mean_one = jnp.mean(scaled, axis=-1, keepdims=True)
    mean_two = jnp.mean(scaled * unit_two, axis=-1, keepdims=True)
    gain_product = grad_normed_two * unit_two
    grad_middle = grad_out.astype(f32) + inverse_two * (scaled - mean_one - unit_two * mean_two)
    grad_branch = grad_middle.astype(bf16)
    grad_attended = dot(grad_branch, weight_out, 1, 1).astype(bf16)

    cuts = [0, 3, 8] if count == 8 else [0, count // 2, count]
    slots = {offset: slot for slot, offset in enumerate(ring_offsets(count))}
    key_parts, value_parts = [None] * count, [None] * count
    grad_queries = None

    def back_part(which, held, earlier):
        first, last = cuts[which], cuts[which + 1]
        query_rows, _ = lax.optimization_barrier((queries, earlier))
        held, key_parts[first:last], value_parts[first:last] = attend_back(
            first, blocks, query_rows, grad_attended, exact, log_total,
            all_keys[first:last], all_values[first:last], held, (cosine, sine),
        )
        return held

    def unfold(piece):
        top, rest = piece[:, :D], piece[:, D:]
        return jnp.concatenate(
            [top, jnp.concatenate([rest[: D // 8], rest[D // 8 :]], axis=1)], axis=0
        )

    def added(parts, which, down, up, distance):
        pair = [parts[slots[-distance]], parts[slots[distance]]]
        groups = [(one, sums[which]) for one, sums in zip(pair, (down, up)) if sums[which] is not None]
        sums = iter(add_all(groups)) if groups else None
        return [
            one if held[which] is None else next(sums) for one, held in zip(pair, (down, up))
        ]

    def hop(down, up, distance):
        arrived = ([], [])
        for which, parts in enumerate((key_parts, value_parts)):
            one, other = added(parts, which, down, up, distance)
            arrived[0].append(shift(one, -1, count))
            arrived[1].append(shift(other, 1, count))
        return arrived

    def mirror(pieces):
        return add_rounded(pieces[2], pieces[3])

    def over_cores(pieces):
        return [pieces[0], swap(pieces[1], 1), pieces[2], swap(pieces[3], 1)]

    def ended(*values):
        return lax.optimization_barrier(values)

    first = cuts[1]
    grad_queries = back_part(1, None, ())
    down = [shift(key_parts[-1], -1, count), None]
    up = [None, shift(value_parts[-1], 1, count)]
    hidden = after(hidden, (key_parts[-1], value_parts[-1]))
    gateup_grads, middle_grads_all = middle_grads(
        me_row, normed_two, grad_gateup, attended, grad_branch, hidden, grad_out, gain_product
    )
    down[0], up[1], gateup_grads, middle_grads_all, grad_queries = ended(
        down[0], up[1], gateup_grads, middle_grads_all, grad_queries
    )
    distances = list(range(count // 2 - 1, 0, -1))
    down, up = hop(down, up, distances[0])
    gateup_grads, middle_grads_all = over_cores(gateup_grads), over_cores(middle_grads_all)
    grad_queries = back_part(0, grad_queries, gateup_grads[0])
    (down, up, gateup_grads, middle_grads_all, grad_queries, key_parts[:first], value_parts[:first]) = ended(
        down, up, gateup_grads, middle_grads_all, grad_queries, key_parts[:first], value_parts[:first]
    )
    down, up = hop(down, up, distances[1])
    gateup_last = swap(mirror(gateup_grads), 2)
    middle_far = mirror(middle_grads_all)
    q_pieces, start = q_back(me_row, normed, grad_queries, q_weights)
    down, up, gateup_last, middle_far, q_pieces, start = ended(
        down, up, gateup_last, middle_far, q_pieces, start
    )
    for distance in distances[2:]:
        down, up = hop(down, up, distance)
    middle_last = swap(middle_far, 2)
    q_pieces = over_cores(q_pieces)
    down, up, middle_last, q_pieces = ended(down, up, middle_last, q_pieces)
    key_sums = (key_parts[0], down[0], up[0])
    value_sums = (value_parts[0], down[1], up[1])
    q_last = swap(mirror(q_pieces), 2)
    kv_pieces, grad_tokens = kv_back(
        me_row, normed, key_sums, value_sums, k_weights, v_weights, cosine, sine, start, token_rows, gains, grad_middle
    )
    gateup_sum, middle_sum = (
        add_all([(pieces[0], pieces[1], last)])[0]
        for pieces, last in ((gateup_grads, gateup_last), (middle_grads_all, middle_last))
    )
    kv_pieces, q_last, gateup_sum, middle_sum = ended(kv_pieces, q_last, gateup_sum, middle_sum)
    q_sum = add_all([(q_pieces[0], q_pieces[1], q_last)])[0]
    middle_total = RingTotal(jnp.concatenate([gateup_sum, middle_sum, q_sum], axis=1), count)
    middle_total.hop()
    kv_pieces = over_cores(kv_pieces)
    kv_pieces, middle_total.up, middle_total.down = ended(
        kv_pieces, middle_total.up, middle_total.down
    )
    kv_last = swap(mirror(kv_pieces), 2)
    middle_total.hop()
    middle_total.hop()
    kv_last, middle_total.up, middle_total.down = ended(
        kv_last, middle_total.up, middle_total.down
    )
    kv_total = RingTotal(add_all([(kv_pieces[0], kv_pieces[1], kv_last)])[0], count)
    while kv_total.done < kv_total.hops - 1:
        kv_total.hop()
        middle_total.hop()
        kv_total.up, kv_total.down, middle_total.up, middle_total.down = ended(
            kv_total.up, kv_total.down, middle_total.up, middle_total.down
        )
    ends = (0, 3 * D, 4 * D, 4 * D + FF, 4 * D + FF + LANES, 5 * D + FF + LANES)
    grad_gateup_weight, grad_out_weight, grad_down, grad_gain, grad_q = (
        middle_total.columns(slice(ends[i], ends[i + 1])) for i in range(5)
    )
    gain_two_own = grad_gain[:, 0]
    grad_down_weight = unfold(grad_down)
    kv_total.hop((grad_gateup_weight, grad_out_weight, grad_down_weight, gain_two_own))
    return (
        result.astype(bf16)[None],
        grad_tokens[None],
        kv_total.columns(slice(2 * D, 2 * D + LANES))[:, 0],
        jnp.concatenate([grad_q, kv_total.columns(slice(0, 2 * D))], axis=1),
        grad_out_weight,
        gain_two_own,
        grad_gateup_weight,
        grad_down_weight,
    )


def solution(mesh):
    return jax.shard_map(
        on_device,
        mesh=mesh,
        in_specs=(
            P("fsdp", "ctx", None),
            P(),
            P("fsdp"),
            P("fsdp", None),
            P("fsdp", None),
            P("fsdp"),
            P("fsdp", None),
            P("fsdp", None),
            P("fsdp", "ctx", None),
        ),
        out_specs=(
            P("fsdp", "ctx", None),
            P("fsdp", "ctx", None),
            P("fsdp"),
            P("fsdp", None),
            P("fsdp", None),
            P("fsdp"),
            P("fsdp", None),
            P("fsdp", None),
        ),
        check_vma=False,
    )
```

```python
from functools import partial

import jax
import jax.numpy as jnp
from jax import lax
from jax.experimental import pallas as pl
from jax.experimental.pallas import tpu as pltpu
from jax.sharding import PartitionSpec as P

D = 768
HEAD_DIM = 64
FF = 1152
LANES = 128
PAIRS = D // LANES
COLS = 256
SCALE = HEAD_DIM**-0.5

theta_base = 160000.0
norm_eps = 1e-05
neg_large = -1e30
f32 = jnp.float32
bf16 = jnp.bfloat16

SMEM = pl.BlockSpec(memory_space=pltpu.SMEM)
WHOLE = pl.BlockSpec(memory_space=pltpu.VMEM)


def params(megabytes):
    return pltpu.CompilerParams(vmem_limit_bytes=megabytes * 2**20)


def cost(microseconds):
    return pl.CostEstimate(flops=int(microseconds * 1.15e9), bytes_accessed=1000, transcendentals=0)


def dot(left, right, left_dim, right_dim):
    return lax.dot_general(
        left, right, (((left_dim,), (right_dim,)), ((), ())), preferred_element_type=f32
    )


def ring_device(place, count):
    return jnp.where(place < count // 2, 2 * place, 2 * (count - 1 - place) + 1)


def ring_place(device, count):
    return jnp.where(device % 2 == 0, device // 2, count - 1 - device // 2)


def shift(array, step, count):
    half = count // 2
    order = [2 * i if i < half else 2 * (count - 1 - i) + 1 for i in range(count)]
    pairs = [(order[i], order[(i + step) % count]) for i in range(count)]
    return lax.ppermute(array, "ctx", pairs)


def ring_offsets(count):
    half = count // 2
    offsets = [0]
    for distance in range(1, half):
        offsets += [-distance, distance]
    return offsets + [half]


def ring_gather(first, second, count):
    half = count // 2
    firsts, seconds = [first], [second]
    up, down = (first, second), (first, second)
    for _ in range(1, half):
        up = tuple(shift(part, 1, count) for part in up)
        down = tuple(shift(part, -1, count) for part in down)
        firsts += [up[0], down[0]]
        seconds += [up[1], down[1]]
    firsts.append(shift(up[0], 1, count))
    seconds.append(shift(down[1], -1, count))
    return firsts, seconds


def add_rounded(left, right):
    return (left.astype(f32) + right.astype(f32)).astype(bf16)


class RingTotal:
    def __init__(self, rows, count):
        self.rows, self.count = rows, count
        self.half = count // 2
        self.place = ring_place(lax.axis_index("ctx"), count)
        self.part = rows.shape[0] // count
        self.fits = rows.shape[0] % (8 * count) == 0
        self.hops = 2 * self.half if self.fits else 0
        self.done = 0
        self.up = self.down = None
        self.parts = [None] * count
        if not self.fits:
            self.total = lax.psum(rows, "ctx")

    def piece(self, offset):
        start = ((self.place + offset) % self.count) * self.part
        return lax.dynamic_slice_in_dim(self.rows, start, self.part, 0)

    def state(self):
        return [array for array in (self.up, self.down) if array is not None]

    def hop(self, earlier=()):
        if self.done >= self.hops:
            return
        self.done += 1
        if self.done <= self.half:
            distance = self.half + 1 - self.done
            down = self.piece(-distance)
            down = down if self.down is None else add_rounded(down, self.down)
            up = None
            if distance < self.half:
                up = self.piece(distance)
                up = up if self.up is None else add_rounded(up, self.up)
        else:
            if self.done == self.half + 1:
                own = self.piece(0).astype(f32) + self.down.astype(f32) + self.up.astype(f32)
                self.up = self.down = self.parts[0] = own.astype(bf16)
            distance = self.done - self.half
            up, down = self.up, (self.down if distance < self.half else None)
            if distance == self.half:
                self.down = None
        if earlier:
            up, down, _ = lax.optimization_barrier((up, down, earlier))
        if self.done <= self.half:
            self.down = shift(down, -1, self.count)
            if up is not None:
                self.up = shift(up, 1, self.count)
        else:
            self.up = self.parts[self.count - distance] = shift(up, 1, self.count)
            if down is not None:
                self.down = self.parts[distance] = shift(down, -1, self.count)

    def columns(self, columns):
        if not self.fits:
            return self.total[:, columns].astype(f32)
        line = [one[:, columns] for one in self.parts]
        twice = jnp.concatenate(line + line, axis=0)
        start = ((self.count - self.place) % self.count) * self.part
        return lax.dynamic_slice_in_dim(twice, start, self.rows.shape[0], 0).astype(f32)


def swap(array, mask):
    return lax.ppermute(array, "fsdp", [(i, i ^ mask) for i in range(4)])


def gather_pieces(piece):
    far = swap(piece, 2)
    return [piece, swap(piece, 1), far, swap(far, 1)]


def core_sums(pieces):
    near, far = swap(pieces[1], 1), swap(pieces[3], 1)
    return (pieces[0], near), add_all([(pieces[2], far)])[0]


def add_all(groups):
    return [sum(part.astype(f32) for part in group).astype(bf16) for group in groups]


def after(array, earlier):
    return lax.optimization_barrier((array, earlier))[0]


def in_order(pieces, me):
    odd = (me % 2) == 1
    high = (me // 2) == 1
    low_pair = [jnp.where(odd, pieces[1], pieces[0]), jnp.where(odd, pieces[0], pieces[1])]
    high_pair = [jnp.where(odd, pieces[3], pieces[2]), jnp.where(odd, pieces[2], pieces[3])]
    first = [jnp.where(high, b, a) for a, b in zip(low_pair, high_pair)]
    last = [jnp.where(high, a, b) for a, b in zip(low_pair, high_pair)]
    return jnp.concatenate(first + last, axis=0)


def out_of_order(whole, me):
    rows = whole.shape[0] // 4
    return [lax.dynamic_slice_in_dim(whole, (me ^ i) * rows, rows, 0) for i in range(4)]


def swap_halves(block):
    lane = lax.broadcasted_iota(jnp.int32, block.shape, 1)
    ahead = pltpu.roll(block, block.shape[1] - HEAD_DIM // 2, 1)
    behind = pltpu.roll(block, HEAD_DIM // 2, 1)
    return jnp.where(lane % HEAD_DIM < HEAD_DIM // 2, ahead, behind)


def normalise(rows):
    mean_value = jnp.mean(rows, axis=-1, keepdims=True)
    centered = rows - mean_value
    spread = jnp.mean(centered * centered, axis=-1, keepdims=True)
    inverse = lax.rsqrt(spread + norm_eps)
    return centered * inverse, inverse


def normed_times(normed, weights, mine):
    total = None
    for i, weight in enumerate(weights):
        part = dot(normed[mine ^ i], weight[: D // 4, :], 1, 0)
        total = part if total is None else total + part
    return total


def rotated(total, cosine, sine, target):
    for i in range(COLS // LANES):
        columns = slice(i * LANES, (i + 1) * LANES)
        block = total[:, columns]
        target[:, columns] = (block * cosine[...] + swap_halves(block) * sine[...]).astype(bf16)


def key_kernel(me, tokens, w0, w1, w2, w3, cosine, sine, keys, normed, gains):
    quarter = D // 4
    mine = me[0]
    weights = (w0, w1, w2, w3)

    @pl.when(pl.program_id(0) == 0)
    def _():
        unit, _ = normalise(tokens[...].astype(f32))
        for i, weight in enumerate(weights):
            gains[mine ^ i] = weight[quarter : quarter + 16, :quarter].astype(f32)[0:1, :]
        for i in range(4):
            normed[i] = (unit[:, i * quarter : (i + 1) * quarter] * gains[i]).astype(bf16)

    rotated(normed_times(normed, weights, mine), cosine, sine, keys)


def fixed(*shape):
    return pl.BlockSpec(shape, lambda j: (0,) * len(shape))


def project_keys(me, tokens, weights, cosine, sine):
    rows = tokens.shape[0]
    return pl.pallas_call(
        key_kernel,
        grid=(D // COLS,),
        in_specs=[SMEM, fixed(rows, D)]
        + [pl.BlockSpec((D // 4 + 16, COLS), lambda j: (0, j))] * 4
        + [fixed(rows, LANES)] * 2,
        out_specs=[
            pl.BlockSpec((rows, COLS), lambda j: (0, j)),
            fixed(4, rows, D // 4),
            fixed(4, 1, D // 4),
        ],
        out_shape=[
            jax.ShapeDtypeStruct((rows, D), bf16),
            jax.ShapeDtypeStruct((4, rows, D // 4), bf16),
            jax.ShapeDtypeStruct((4, 1, D // 4), f32),
        ],
        compiler_params=params(32),
        cost_estimate=cost(2),
        name="project_keys",
    )(me, tokens, *weights, cosine, sine)


def query_kernel(me, normed, w0, w1, w2, w3, cosine, sine, queries):
    rotated(normed_times(normed, (w0, w1, w2, w3), me[0]), cosine, sine, queries)


def value_kernel(me, normed, w0, w1, w2, w3, values):
    values[...] = normed_times(normed, (w0, w1, w2, w3), me[0]).astype(bf16)


def project(me, normed, weights, tables=()):
    rows = normed.shape[1]
    return pl.pallas_call(
        query_kernel if tables else value_kernel,
        grid=(D // COLS,),
        in_specs=[SMEM, fixed(4, rows, D // 4)]
        + [pl.BlockSpec((D // 4, COLS), lambda j: (0, j))] * 4
        + [fixed(rows, LANES)] * len(tables),
        out_specs=pl.BlockSpec((rows, COLS), lambda j: (0, j)),
        out_shape=jax.ShapeDtypeStruct((rows, D), bf16),
        compiler_params=params(32),
        cost_estimate=cost(2),
        name="project_queries" if tables else "project_values",
    )(me, normed, *weights, *tables)


def stacked(block, factor=None):
    if factor is not None:
        block = block * jnp.asarray(factor, block.dtype)
    lane = lax.broadcasted_iota(jnp.int32, block.shape, 1)
    zero = jnp.zeros_like(block)
    return jnp.concatenate(
        [jnp.where(lane < HEAD_DIM, block, zero), jnp.where(lane < HEAD_DIM, zero, block)], axis=0
    )


def unstacked(block):
    rows = block.shape[0] // 2
    lane = lax.broadcasted_iota(jnp.int32, (rows, block.shape[1]), 1)
    return jnp.where(lane < HEAD_DIM, block[:rows], block[rows:])


def causal(scores):
    rows, columns = scores.shape
    row = lax.broadcasted_iota(jnp.int32, scores.shape, 0) % (rows // 2)
    column = lax.broadcasted_iota(jnp.int32, scores.shape, 1)
    return jnp.where(column <= row, scores, neg_large)


def over_chunks(groups, per, first, visit, carry):
    for group in range(groups):
        start = first if group == 0 else 0
        if per == 1:
            if start == 0:
                carry = visit(group, 0, group, carry)
        else:

            def turn(i, held, group=group):
                return visit(group, i, group * per + i, held)

            carry = lax.fori_loop(start, per, turn, carry)
    return carry


def by_head(stacked_column):
    return unstacked(jnp.broadcast_to(stacked_column, (stacked_column.shape[0], LANES)))


def of_heads(block):
    shape = block.shape
    return jnp.concatenate(
        [
            jnp.broadcast_to(block[:, :1], shape),
            jnp.broadcast_to(block[:, HEAD_DIM : HEAD_DIM + 1], shape),
        ],
        axis=0,
    )


def attend_kernel(groups, per, base, merge, blocks, queries, *refs):
    keys, values = refs[:groups], refs[groups : 2 * groups]
    rest = refs[2 * groups :]
    before, rest = (rest[:4], rest[4:]) if merge else ((), rest)
    results, (stack, scores) = rest[:-2], rest[-2:]
    width = queries.shape[0] // 2
    own = blocks[0]
    low, high = slice(0, width), slice(width, 2 * width)
    with_own = base == 0
    empty = jnp.full((2 * width, LANES), neg_large, f32)
    nothing = jnp.zeros((2 * width, LANES), f32)

    def picked(chunk):
        up = blocks[base + chunk] > own
        which = up.astype(jnp.int32)
        return up, which, pl.ds(pl.multiple_of(which * width, width), width)

    for i, rows in enumerate((low, high)):
        stack[i] = stacked(queries[rows, :], SCALE)

    tops = (empty, empty)
    if with_own:
        first = causal(dot(stack[0], keys[0][0, low, :], 1, 1))
        second = causal(dot(stack[1], keys[0][0, high, :], 1, 1))
        third = dot(stack[1], keys[0][0, low, :], 1, 1)
        scores[0], scores[1], scores[2] = first, second, third
        tops = (first, jnp.maximum(second, third))

    def score(group, i, chunk, held):
        up, which, rows = picked(chunk)
        full = dot(stack[1], keys[group][i, low, :], 1, 1)
        part = dot(stack[which], keys[group][i, rows, :], 1, 1)
        scores[2 * chunk + 1] = full
        scores[2 * chunk + 2] = part
        return (
            jnp.maximum(held[0], jnp.where(up, empty, part)),
            jnp.maximum(jnp.maximum(held[1], full), jnp.where(up, part, empty)),
        )

    tops = over_chunks(groups, per, int(with_own), score, tops)
    top_low, top_high = (jnp.max(top, axis=1, keepdims=True) for top in tops)

    def weigh(slot, top, value_rows):
        weight = jnp.exp(scores[slot] - top)
        coarse = weight.astype(bf16)
        fine = (weight - coarse.astype(f32)).astype(bf16)
        return (
            weight,
            unstacked(dot(coarse, value_rows, 1, 0)),
            unstacked(dot(fine, value_rows, 1, 0)),
        )

    def summed(*parts):
        return tuple(sum(terms[1:], terms[0]) for terms in zip(*parts))

    none = (nothing, nothing[low], nothing[low])
    sums = (none, none)
    if with_own:
        sums = (
            weigh(0, top_low, values[0][0, low, :]),
            summed(
                weigh(1, top_high, values[0][0, high, :]), weigh(2, top_high, values[0][0, low, :])
            ),
        )

    def collect(group, i, chunk, held):
        up, which, rows = picked(chunk)
        full = weigh(2 * chunk + 1, top_high, values[group][i, low, :])
        part = weigh(
            2 * chunk + 2, jnp.where(up, top_high, top_low), values[group][i, rows, :]
        )
        to_low = tuple(jnp.where(up, jnp.zeros_like(term), term) for term in part)
        to_high = tuple(jnp.where(up, term, jnp.zeros_like(term)) for term in part)
        return summed(held[0], to_low), summed(held[1], full, to_high)

    sums = over_chunks(groups, per, int(with_own), collect, sums)
    for rows, top, (weight, coarse, fine) in zip((low, high), (top_low, top_high), sums):
        top = by_head(top)
        total = by_head(jnp.sum(weight, axis=1, keepdims=True))
        exact = coarse + fine
        if merge:
            old_top, old_total, old_coarse, old_exact = (ref[rows, :] for ref in before)
            new_top = jnp.maximum(top, old_top)
            now, then = jnp.exp(top - new_top), jnp.exp(old_top - new_top)
            total = total * now + old_total * then
            inverse = 1.0 / total
            attended, exact_out, log_total = results
            attended[rows, :] = ((coarse * now + old_coarse * then) * inverse).astype(bf16)
            exact_out[rows, :] = (exact * now + old_exact * then) * inverse
            log_total[rows, :] = new_top + jnp.log(total)
        else:
            for ref, value in zip(results, (top, total, coarse, exact)):
                ref[rows, :] = value


def grouped(chunks):
    per = 1 if len(chunks) <= 8 else len(chunks) // 4
    if per == 1:
        return [chunk[None] for chunk in chunks]
    return [jnp.stack(chunks[i : i + per]) for i in range(0, len(chunks), per)]


def column_block(rows):
    return pl.BlockSpec((rows, LANES), lambda j: (0, j))


def attend(base, blocks, queries, key_chunks, value_chunks, before=()):
    rows = queries.shape[0]
    keys, values = grouped(key_chunks), grouped(value_chunks)
    groups, per, count = len(keys), keys[0].shape[0], len(key_chunks)
    column = column_block(rows)
    chunk = pl.BlockSpec((per, rows, LANES), lambda j: (0, 0, j))
    types = (bf16, f32, f32) if before else (f32,) * 4
    return pl.pallas_call(
        partial(attend_kernel, groups, per, base, bool(before)),
        grid=(PAIRS,),
        in_specs=[SMEM, column] + [chunk] * (2 * groups) + [column] * len(before),
        out_specs=[column] * len(types),
        out_shape=[jax.ShapeDtypeStruct((rows, D), kind) for kind in types],
        scratch_shapes=[
            pltpu.VMEM((2, rows, LANES), bf16),
            pltpu.VMEM((2 * count + 1, rows, LANES), f32),
        ],
        compiler_params=params(56),
        cost_estimate=cost(2 * count),
        name=f"attend_{base}",
    )(blocks, queries, *keys, *values, *before)


def attend_back_kernel(groups, per, base, carried, blocks, queries, grads, exact, log_total, *refs):
    keys, values = refs[:groups], refs[groups : 2 * groups]
    rest = refs[2 * groups :]
    before, rest = (rest[:1], rest[1:]) if carried else ((), rest)
    with_own = base == 0
    (cosine, sine), rest = (rest[:2], rest[2:]) if with_own else ((None, None), rest)
    grad_queries = rest[0]
    grad_keys = rest[1 : groups + 1]
    grad_values = rest[groups + 1 : 2 * groups + 1]
    stack, grad_stack, deltas, logs = rest[2 * groups + 1 :]
    width = queries.shape[0] // 2
    own = blocks[0]
    low, high = slice(0, width), slice(width, 2 * width)

    for i, rows in enumerate((low, high)):
        stack[i] = stacked(queries[rows, :], SCALE)
        grad_rows = stacked(grads[rows, :])
        grad_stack[i] = grad_rows
        twice = jnp.concatenate([exact[rows, :], exact[rows, :]], axis=0)
        delta = jnp.sum(grad_rows.astype(f32) * twice, axis=1, keepdims=True)
        deltas[i] = jnp.broadcast_to(delta, deltas.shape[1:])
        logs[i] = of_heads(log_total[rows, :])

    def block(which, key_rows, value_rows, diagonal=False):
        query_rows, grad_rows = stack[which], grad_stack[which]
        raw = dot(query_rows, key_rows, 1, 1)
        if diagonal:
            raw = causal(raw)
        probability = jnp.exp(raw - logs[which])
        grad_prob = dot(grad_rows, value_rows, 1, 1)
        grad_scores = (probability * (grad_prob - deltas[which])).astype(bf16)
        return (
            unstacked(dot(grad_scores, key_rows, 1, 0)),
            dot(grad_scores, query_rows, 0, 0),
            dot(probability.astype(bf16), grad_rows, 0, 0),
        )

    if carried:
        sums = (before[0][low, :], before[0][high, :])
    else:
        sums = (jnp.zeros((width, LANES), f32),) * 2
    if with_own:
        key_low, value_low = keys[0][0, low, :], values[0][0, low, :]
        query_one, key_one, value_one = block(0, key_low, value_low, True)
        query_two, key_two, value_two = block(1, keys[0][0, high, :], values[0][0, high, :], True)
        query_all, key_all, value_all = block(1, key_low, value_low)
        sums = (sums[0] + query_one, sums[1] + query_two + query_all)
        grad_keys[0][0, low, :] = (key_one + key_all).astype(bf16)
        grad_values[0][0, low, :] = (value_one + value_all).astype(bf16)
        grad_keys[0][0, high, :] = key_two.astype(bf16)
        grad_values[0][0, high, :] = value_two.astype(bf16)

    def visit(group, i, chunk, held):
        up = blocks[base + chunk] > own
        which = up.astype(jnp.int32)
        rows = pl.ds(pl.multiple_of(which * width, width), width)
        query_all, key_all, value_all = block(1, keys[group][i, low, :], values[group][i, low, :])
        query_one, key_one, value_one = block(
            which, keys[group][i, rows, :], values[group][i, rows, :]
        )
        for target, whole, part in (
            (grad_keys[group], key_all, key_one),
            (grad_values[group], value_all, value_one),
        ):
            zero = jnp.zeros_like(part)
            target[i, low, :] = (whole + jnp.where(up, zero, part)).astype(bf16)
            target[i, high, :] = jnp.where(up, part, zero).astype(bf16)
        zero = jnp.zeros_like(query_one)
        return (
            held[0] + jnp.where(up, zero, query_one),
            held[1] + query_all + jnp.where(up, query_one, zero),
        )

    sums = over_chunks(groups, per, int(with_own), visit, sums)
    for rows, grad in zip((low, high), sums):
        if with_own:
            grad = grad * SCALE
            turned = grad * cosine[rows, :] - swap_halves(grad) * sine[rows, :]
            grad_queries[rows, :] = turned.astype(bf16)
        else:
            grad_queries[rows, :] = grad


def attend_back(base, blocks, queries, grads, exact, log_total, key_chunks, value_chunks, before, tables):
    rows = queries.shape[0]
    keys, values = grouped(key_chunks), grouped(value_chunks)
    groups, per, count = len(keys), keys[0].shape[0], len(key_chunks)
    column = column_block(rows)
    chunk = pl.BlockSpec((per, rows, LANES), lambda j: (0, 0, j))
    stat = pltpu.VMEM((2, rows, LANES), f32)
    half = pltpu.VMEM((2, rows, LANES), bf16)
    extra = (() if before is None else (before,)) + (tuple(tables) if base == 0 else ())
    extra_specs = ([] if before is None else [column]) + ([fixed(rows, LANES)] * 2 if base == 0 else [])
    result = pl.pallas_call(
        partial(attend_back_kernel, groups, per, base, before is not None),
        grid=(PAIRS,),
        in_specs=[SMEM] + [column] * 4 + [chunk] * (2 * groups) + extra_specs,
        out_specs=[column] + [chunk] * (2 * groups),
        out_shape=[jax.ShapeDtypeStruct((rows, D), bf16 if base == 0 else f32)]
        + [jax.ShapeDtypeStruct((per, rows, D), bf16)] * (2 * groups),
        scratch_shapes=[half, half, stat, stat],
        compiler_params=params(56),
        cost_estimate=cost(4.5 * count),
        name=f"attend_back_{base}",
    )(blocks, queries, grads, exact, log_total, *keys, *values, *extra)
    key_grads = [part[i] for part in result[1 : groups + 1] for i in range(per)]
    value_grads = [part[i] for part in result[groups + 1 :] for i in range(per)]
    return result[0], key_grads, value_grads


def q_back_kernel(me, normed, grads, w0, w1, w2, w3, g0, g1, g2, g3, back):
    mine = me[0]
    step = pl.program_id(0)
    block = grads[...]
    for i, (weight, target) in enumerate(((w0, g0), (w1, g1), (w2, g2), (w3, g3))):
        target[...] = dot(normed[mine ^ i], block, 0, 0).astype(bf16)
        part = dot(block, weight[...], 1, 1)

        @pl.when(step == 0)
        def _(i=i, part=part):
            back[mine ^ i] = part

        @pl.when(step > 0)
        def _(i=i, part=part):
            back[mine ^ i] += part


def q_back(me, normed, grads, weights):
    rows = grads.shape[0]

    column = pl.BlockSpec((D // 4, COLS), lambda j: (0, j))
    result = pl.pallas_call(
        q_back_kernel,
        grid=(D // COLS,),
        in_specs=[SMEM, fixed(4, rows, D // 4), pl.BlockSpec((rows, COLS), lambda j: (0, j))]
        + [column] * 4,
        out_specs=[column] * 4 + [fixed(4, rows, D // 4)],
        out_shape=[jax.ShapeDtypeStruct((D // 4, D), bf16)] * 4
        + [jax.ShapeDtypeStruct((4, rows, D // 4), f32)],
        compiler_params=params(32),
        cost_estimate=cost(4),
        name="q_back",
    )(me, normed, grads, *weights)
    return result[:4], result[4]


def middle_grads_kernel(me, normed, grad_gateup, attended, grad_branch, hidden, grad_out, gain, *refs):
    gateups, others = refs[:4], refs[4:8]
    normed_by, attended_by, hidden_by, gain_by = refs[8:]
    mine = me[0]
    quarter, part = D // 4, FF // 4
    ones = jnp.ones((normed.shape[0], LANES), bf16)
    coarse = gain[...].astype(bf16)
    fine = (gain[...] - coarse.astype(f32)).astype(bf16)
    for i in range(4):
        columns = slice(i * quarter, (i + 1) * quarter)
        normed_by[i] = normed[:, columns]
        attended_by[i] = attended[:, columns]
        hidden_by[i] = hidden[:, i * part : (i + 1) * part]
        gain_by[i] = dot(coarse[:, columns], ones, 0, 0) + dot(fine[:, columns], ones, 0, 0)
    for i in (3, 1, 2, 0):
        for first in range(0, 2 * FF, D):
            columns = slice(first, first + D)
            gateups[i][:, columns] = dot(normed_by[mine ^ i], grad_gateup[:, columns], 0, 0).astype(bf16)
        others[i][:, :D] = dot(attended_by[mine ^ i], grad_branch[...], 0, 0).astype(bf16)
        down = dot(hidden_by[mine ^ i], grad_out[...], 0, 0).astype(bf16)
        others[i][:, D : 2 * D] = down[:quarter]
        others[i][: quarter // 2, 2 * D : D + FF] = down[quarter:, : D // 2]
        others[i][quarter // 2 :, 2 * D : D + FF] = down[quarter:, D // 2 :]
        others[i][:, D + FF :] = gain_by[mine ^ i].astype(bf16)


def middle_grads(me, normed, grad_gateup, attended, grad_branch, hidden, grad_out, gain):
    rows = normed.shape[0]
    result = pl.pallas_call(
        middle_grads_kernel,
        in_specs=[SMEM] + [WHOLE] * 7,
        out_specs=[WHOLE] * 8,
        out_shape=[jax.ShapeDtypeStruct((D // 4, 2 * FF), bf16)] * 4
        + [jax.ShapeDtypeStruct((D // 4, D + FF + LANES), bf16)] * 4,
        scratch_shapes=[
            pltpu.VMEM((4, rows, D // 4), bf16),
            pltpu.VMEM((4, rows, D // 4), bf16),
            pltpu.VMEM((4, rows, FF // 4), bf16),
            pltpu.VMEM((4, D // 4, LANES), f32),
        ],
        compiler_params=params(32),
        cost_estimate=cost(4),
        name="middle_grads",
    )(me, normed, grad_gateup, attended, grad_branch, hidden, grad_out, gain)
    return result[:4], result[4:]


def kv_back_kernel(
    me, normed, k_own, k_one, k_two, v_own, v_one, v_two, k0, k1, k2, k3, v0, v1, v2, v3, cosine, sine,
    start, tokens, gains, grad_middle, g0, g1, g2, g3, grad_tokens, back, block_of,
):
    mine = me[0]
    step = pl.program_id(0)
    half = (pl.num_programs(0) - 1) // 2
    quarter = D // 4
    targets = (g0, g1, g2, g3)

    @pl.when(step == 0)
    def _():
        back[...] = start[...]

    @pl.when(step < half)
    def _():
        total = k_own[...].astype(f32) + k_one[...].astype(f32) + k_two[...].astype(f32)
        for i in range(COLS // LANES):
            columns = slice(i * LANES, (i + 1) * LANES)
            part = total[:, columns]
            turned = part * cosine[...] - swap_halves(part) * sine[...]
            block_of[:, columns] = turned.astype(bf16)
        for i, weight in enumerate((k0, k1, k2, k3)):
            targets[i][...] = dot(normed[mine ^ i], block_of[...], 0, 0).astype(bf16)
            back[mine ^ i] += dot(block_of[...], weight[:quarter, :], 1, 1)

    @pl.when((step >= half) & (step < 2 * half))
    def _():
        total = v_own[...].astype(f32) + v_one[...].astype(f32) + v_two[...].astype(f32)
        block = total.astype(bf16)
        for i, weight in enumerate((v0, v1, v2, v3)):
            targets[i][...] = dot(normed[mine ^ i], block, 0, 0).astype(bf16)
            back[mine ^ i] += dot(block, weight[...], 1, 1)

    @pl.when(step == 2 * half)
    def _():
        unit, inverse = normalise(tokens[...].astype(f32))
        ones = jnp.ones((unit.shape[0], COLS), bf16)
        for i in range(4):
            part = back[i] * unit[:, i * quarter : (i + 1) * quarter]
            coarse = part.astype(bf16)
            fine = (part - coarse.astype(f32)).astype(bf16)
            total = (dot(coarse, ones, 0, 0) + dot(fine, ones, 0, 0)).astype(bf16)
            for k in range(4):

                @pl.when((mine ^ k) == i)
                def _(k=k, total=total):
                    targets[k][...] = total

        incoming = jnp.concatenate([back[i] for i in range(4)], axis=1)
        gain = jnp.concatenate([gains[i] for i in range(4)], axis=1)
        scaled = incoming * gain
        mean_one = jnp.mean(scaled, axis=-1, keepdims=True)
        mean_two = jnp.mean(scaled * unit, axis=-1, keepdims=True)
        grad_tokens[...] = grad_middle[...] + inverse * (scaled - mean_one - unit * mean_two)


def kv_back(
    me, normed, key_sums, value_sums, k_weights, v_weights, cosine, sine, start, tokens, gains, grad_middle
):
    rows = tokens.shape[0]
    half = D // COLS

    def early(height):
        return pl.BlockSpec((height, COLS), lambda j: (0, jnp.minimum(j, half - 1)))

    def late(height):
        return pl.BlockSpec((height, COLS), lambda j: (0, jnp.clip(j - half, 0, half - 1)))

    result = pl.pallas_call(
        kv_back_kernel,
        grid=(2 * half + 1,),
        in_specs=[SMEM, fixed(4, rows, D // 4)]
        + [early(rows)] * 3
        + [late(rows)] * 3
        + [early(D // 4 + 16)] * 4
        + [late(D // 4)] * 4
        + [fixed(rows, LANES)] * 2
        + [fixed(4, rows, D // 4), fixed(rows, D), fixed(4, 1, D // 4), fixed(rows, D)],
        out_specs=[pl.BlockSpec((D // 4, COLS), lambda j: (0, j))] * 4 + [fixed(rows, D)],
        out_shape=[jax.ShapeDtypeStruct((D // 4, 2 * D + COLS), bf16)] * 4
        + [jax.ShapeDtypeStruct((rows, D), f32)],
        scratch_shapes=[
            pltpu.VMEM((4, rows, D // 4), f32),
            pltpu.VMEM((rows, COLS), bf16),
        ],
        compiler_params=params(56),
        cost_estimate=cost(8),
        name="kv_back",
    )(
        me, normed, *key_sums, *value_sums, *k_weights, *v_weights, cosine, sine, start, tokens, gains, grad_middle
    )
    return result[:4], result[4]


def layer_norm(token_rows, gain_row):
    mean_value = jnp.mean(token_rows, axis=-1, keepdims=True)
    centered = token_rows - mean_value
    spread = jnp.mean(centered * centered, axis=-1, keepdims=True)
    return centered * lax.rsqrt(spread + norm_eps) * gain_row


def geglu(gate_part, up_part):
    return jax.nn.gelu(gate_part, approximate=False) * up_part


def rope_tables(positions):
    half = HEAD_DIM // 2
    frequency = theta_base ** (-2.0 * jnp.arange(half, dtype=f32) / HEAD_DIM)
    angles = positions.astype(f32)[:, None] * frequency[None, :]
    cosine, sine = jnp.cos(angles), jnp.sin(angles)
    return (
        jnp.concatenate([cosine] * 4, axis=1),
        jnp.concatenate([-sine, sine, -sine, sine], axis=1),
    )


def on_device(
    tokens,
    pair_order,
    norm_one,
    qkv_weight,
    out_weight,
    norm_two,
    gateup_weight,
    down_weight,
    cotangent,
):
    count = lax.axis_size("ctx")
    me = lax.axis_index("fsdp")
    me_row = jnp.reshape(me, (1,)).astype(jnp.int32)
    gain_row = jnp.concatenate(
        [jnp.pad(norm_one, (0, COLS - D // 4)), jnp.pad(norm_two, (0, D - COLS - D // 4))]
    )
    gain_rows = jnp.broadcast_to(gain_row[None, :], (16, D))
    k_weights = gather_pieces(jnp.concatenate([qkv_weight[:, D : 2 * D], gain_rows], axis=0))
    v_piece = after(qkv_weight[:, 2 * D :], k_weights[2])
    v_far = swap(v_piece, 2)
    q_weights = gather_pieces(after(qkv_weight[:, :D], v_far))
    out_pieces = gather_pieces(after(out_weight, q_weights[2]))
    gateup_pieces = gather_pieces(after(gateup_weight, out_pieces[2]))
    down_pieces = gather_pieces(after(down_weight, gateup_pieces[2]))
    pair_order = after(pair_order, k_weights[1])
    place = ring_place(lax.axis_index("ctx"), count)
    width = tokens.shape[1] // 2
    offsets = jnp.asarray(ring_offsets(count), jnp.int32)
    chunk_devices = ring_device((place + offsets) % count, count)
    blocks = jnp.sum(
        jnp.where(
            chunk_devices[:, None] == jnp.arange(count, dtype=jnp.int32)[None, :],
            pair_order[None, :],
            0,
        ),
        axis=1,
    )
    low_block = blocks[0]
    high_block = 2 * count - 1 - low_block
    within = jnp.arange(width, dtype=jnp.int32)
    positions = jnp.concatenate([low_block * width + within, high_block * width + within])
    cosine, sine = rope_tables(positions)

    token_rows = tokens[0]
    keys, normed, gains = project_keys(me_row, token_rows, k_weights, cosine, sine)
    v_weights = [v_piece, swap(v_piece, 1), v_far, swap(after(v_far, keys), 1)]
    values = project(me_row, normed, v_weights)
    all_keys, all_values = ring_gather(keys, values, count)
    queries = project(me_row, normed, q_weights, (cosine, sine))
    split = count - 3 if count == 8 else count // 2
    so_far = attend(0, blocks, queries, all_keys[:split], all_values[:split])
    attended, exact, log_total = attend(
        split, blocks, queries, all_keys[split:], all_values[split:], so_far
    )

    weight_out = in_order(out_pieces, me)
    weight_gateup = in_order(gateup_pieces, me)
    weight_down = in_order(down_pieces, me)
    gain_two = in_order([part[D // 4, COLS : COLS + D // 4] for part in k_weights], me).astype(f32)
    middle = token_rows.astype(f32) + jnp.dot(attended, weight_out, preferred_element_type=f32)
    normed_two = layer_norm(middle, gain_two).astype(bf16)
    gateup = jnp.dot(normed_two, weight_gateup, preferred_element_type=f32)
    hidden_f, geglu_pull = jax.vjp(geglu, gateup[:, :FF], gateup[:, FF:])
    hidden = hidden_f.astype(bf16)
    result = middle + jnp.dot(hidden, weight_down, preferred_element_type=f32)
    grad_out = cotangent[0]
    grad_hidden = dot(grad_out, weight_down, 1, 1)
    grad_gate, grad_up = geglu_pull(grad_hidden)
    grad_gateup = jnp.concatenate([grad_gate, grad_up], axis=1).astype(bf16)
    grad_normed_two = dot(grad_gateup, weight_gateup, 1, 1)
    unit_two, inverse_two = normalise(middle)
    scaled = grad_normed_two * gain_two
    mean_one = jnp.mean(scaled, axis=-1, keepdims=True)
    mean_two = jnp.mean(scaled * unit_two, axis=-1, keepdims=True)
    gain_product = grad_normed_two * unit_two
    grad_middle = grad_out.astype(f32) + inverse_two * (scaled - mean_one - unit_two * mean_two)
    grad_branch = grad_middle.astype(bf16)
    grad_attended = dot(grad_branch, weight_out, 1, 1).astype(bf16)

    cuts = [0, 3, 5, 8] if count == 8 else [0, count // 4, count // 2, count]
    slots = {offset: slot for slot, offset in enumerate(ring_offsets(count))}
    key_parts, value_parts = [None] * count, [None] * count
    grad_queries = None

    def back_part(which, held, earlier):
        first, last = cuts[which], cuts[which + 1]
        query_rows, _ = lax.optimization_barrier((queries, earlier))
        held, key_parts[first:last], value_parts[first:last] = attend_back(
            first, blocks, query_rows, grad_attended, exact, log_total,
            all_keys[first:last], all_values[first:last], held, (cosine, sine),
        )
        return held

    def unfold(piece):
        top, rest = piece[:, :D], piece[:, D:]
        return jnp.concatenate(
            [top, jnp.concatenate([rest[: D // 8], rest[D // 8 :]], axis=1)], axis=0
        )

    def added(parts, which, down, up, distance):
        pair = [parts[slots[-distance]], parts[slots[distance]]]
        groups = [(one, sums[which]) for one, sums in zip(pair, (down, up)) if sums[which] is not None]
        sums = iter(add_all(groups)) if groups else None
        return [
            one if held[which] is None else next(sums) for one, held in zip(pair, (down, up))
        ]

    sent = []

    def hop(down, up, distance):
        arrived = ([], [])
        for which, parts in enumerate((key_parts, value_parts)):
            one, other = added(parts, which, down, up, distance)
            sent.extend([one, other])
            arrived[0].append(shift(one, -1, count))
            arrived[1].append(shift(other, 1, count))
        return arrived

    def mirror(pieces):
        return add_rounded(pieces[2], pieces[3])

    def over_cores(pieces):
        return [pieces[0], swap(pieces[1], 1), pieces[2], swap(pieces[3], 1)]

    def ended(*values):
        return lax.optimization_barrier(values)

    first, second = cuts[1], cuts[2]
    gateup_grads, middle_grads_all = middle_grads(
        me_row, normed_two, grad_gateup, attended, grad_branch, hidden, grad_out, gain_product
    )
    gateup_grads, middle_grads_all = over_cores(gateup_grads), over_cores(middle_grads_all)
    grad_queries = back_part(2, None, gateup_grads[0])
    gateup_grads, middle_grads_all, grad_queries, key_parts[second:], value_parts[second:] = ended(
        gateup_grads, middle_grads_all, grad_queries, key_parts[second:], value_parts[second:]
    )
    down = [shift(key_parts[-1], -1, count), None]
    up = [None, shift(value_parts[-1], 1, count)]
    gateup_far = mirror(gateup_grads)
    gateup_last = [swap(gateup_far[:, :FF], 2)]
    grad_queries = back_part(1, grad_queries, gateup_far)
    (down[0], up[1], gateup_last[0], gateup_far, middle_grads_all, grad_queries, key_parts[first:second], value_parts[first:second]) = ended(
        down[0], up[1], gateup_last[0], gateup_far, middle_grads_all, grad_queries, key_parts[first:second], value_parts[first:second]
    )
    distances = list(range(count // 2 - 1, 0, -1))
    down, up = hop(down, up, distances[0])
    gateup_last.append(swap(gateup_far[:, FF:], 2))
    middle_far = mirror(middle_grads_all)
    grad_queries = back_part(0, grad_queries, middle_far)
    gateup_last, middle_far, grad_queries, key_parts[:second], value_parts[:second] = ended(
        gateup_last, middle_far, grad_queries, key_parts[:second], value_parts[:second]
    )
    gateup_last = jnp.concatenate(gateup_last, axis=1)
    middle_last = swap(middle_far, 2)
    for distance in distances[1:-1]:
        down, up = hop(down, up, distance)
    q_pieces, start = q_back(me_row, normed, after(grad_queries, sent[-4:]), q_weights)
    q_pieces = over_cores(q_pieces)
    down[0], up[0], middle_last, q_pieces = ended(down[0], up[0], middle_last, q_pieces)
    down, up = hop(down, up, distances[-1])
    q_last = swap(mirror(q_pieces), 2)
    gateup_sum, middle_sum = (
        add_all([(pieces[0], pieces[1], last)])[0]
        for pieces, last in ((gateup_grads, gateup_last), (middle_grads_all, middle_last))
    )
    middle_total = RingTotal(jnp.concatenate([gateup_sum, middle_sum], axis=1), count)
    middle_total.hop()
    down, up, q_last, middle_total.up, middle_total.down = ended(
        down, up, q_last, middle_total.up, middle_total.down
    )
    middle_total.hop()
    key_sums = (key_parts[0], down[0], up[0])
    value_sums = (value_parts[0], down[1], up[1])
    kv_pieces, grad_tokens = kv_back(
        me_row, normed, key_sums, value_sums, k_weights, v_weights, cosine, sine, start, token_rows, gains, grad_middle
    )
    q_sum = add_all([(q_pieces[0], q_pieces[1], q_last)])[0]
    kv_pieces, q_sum, middle_total.up, middle_total.down = ended(
        kv_pieces, q_sum, middle_total.up, middle_total.down
    )
    kv_pieces = over_cores(kv_pieces)
    kv_last = swap(mirror(kv_pieces), 2)
    middle_total.hop()
    middle_total.hop()
    kv_last, middle_total.up, middle_total.down = ended(
        kv_last, middle_total.up, middle_total.down
    )
    kv_sum = add_all([(kv_pieces[0], kv_pieces[1], kv_last)])[0]
    kv_total = RingTotal(jnp.concatenate([q_sum, kv_sum], axis=1), count)
    while kv_total.done < kv_total.hops - 1:
        kv_total.hop()
        middle_total.hop()
        kv_total.up, kv_total.down, middle_total.up, middle_total.down = ended(
            kv_total.up, kv_total.down, middle_total.up, middle_total.down
        )
    ends = (0, 3 * D, 4 * D, 4 * D + FF, 4 * D + FF + LANES)
    grad_gateup_weight, grad_out_weight, grad_down, grad_gain = (
        middle_total.columns(slice(ends[i], ends[i + 1])) for i in range(4)
    )
    gain_two_own = grad_gain[:, 0]
    grad_down_weight = unfold(grad_down)
    kv_total.hop((grad_gateup_weight, grad_out_weight, grad_down_weight, gain_two_own))
    return (
        result.astype(bf16)[None],
        grad_tokens[None],
        kv_total.columns(slice(3 * D, 3 * D + LANES))[:, 0],
        kv_total.columns(slice(0, 3 * D)),
        grad_out_weight,
        gain_two_own,
        grad_gateup_weight,
        grad_down_weight,
    )


def solution(mesh):
    return jax.shard_map(
        on_device,
        mesh=mesh,
        in_specs=(
            P("fsdp", "ctx", None),
            P(),
            P("fsdp"),
            P("fsdp", None),
            P("fsdp", None),
            P("fsdp"),
            P("fsdp", None),
            P("fsdp", None),
            P("fsdp", "ctx", None),
        ),
        out_specs=(
            P("fsdp", "ctx", None),
            P("fsdp", "ctx", None),
            P("fsdp"),
            P("fsdp", None),
            P("fsdp", None),
            P("fsdp"),
            P("fsdp", None),
            P("fsdp", None),
        ),
        check_vma=False,
    )
```

```python
from functools import partial

import jax
import jax.numpy as jnp
from jax import lax
from jax.experimental import pallas as pl
from jax.experimental.pallas import tpu as pltpu
from jax.sharding import PartitionSpec as P

D = 768
HEAD_DIM = 64
FF = 1152
LANES = 128
PAIRS = D // LANES
COLS = 256
SCALE = HEAD_DIM**-0.5

theta_base = 160000.0
norm_eps = 1e-05
neg_large = -1e30
f32 = jnp.float32
bf16 = jnp.bfloat16

SMEM = pl.BlockSpec(memory_space=pltpu.SMEM)
WHOLE = pl.BlockSpec(memory_space=pltpu.VMEM)


def params(megabytes):
    return pltpu.CompilerParams(vmem_limit_bytes=megabytes * 2**20)


def cost(microseconds):
    return pl.CostEstimate(flops=int(microseconds * 1.15e9), bytes_accessed=1000, transcendentals=0)


def dot(left, right, left_dim, right_dim):
    return lax.dot_general(
        left, right, (((left_dim,), (right_dim,)), ((), ())), preferred_element_type=f32
    )


def ring_device(place, count):
    return jnp.where(place < count // 2, 2 * place, 2 * (count - 1 - place) + 1)


def ring_place(device, count):
    return jnp.where(device % 2 == 0, device // 2, count - 1 - device // 2)


def shift(array, step, count):
    half = count // 2
    order = [2 * i if i < half else 2 * (count - 1 - i) + 1 for i in range(count)]
    pairs = [(order[i], order[(i + step) % count]) for i in range(count)]
    return lax.ppermute(array, "ctx", pairs)


def ring_offsets(count):
    half = count // 2
    offsets = [0]
    for distance in range(1, half):
        offsets += [-distance, distance]
    return offsets + [half]


def ring_gather(first, second, count):
    half = count // 2
    firsts, seconds = [first], [second]
    up, down = (first, second), (first, second)
    for _ in range(1, half):
        up = tuple(shift(part, 1, count) for part in up)
        down = tuple(shift(part, -1, count) for part in down)
        firsts += [up[0], down[0]]
        seconds += [up[1], down[1]]
    firsts.append(shift(up[0], 1, count))
    seconds.append(shift(down[1], -1, count))
    return firsts, seconds


def add_rounded(left, right):
    return (left.astype(f32) + right.astype(f32)).astype(bf16)


class RingTotal:
    def __init__(self, rows, count):
        self.rows, self.count = rows, count
        self.half = count // 2
        self.place = ring_place(lax.axis_index("ctx"), count)
        self.part = rows.shape[0] // count
        self.fits = rows.shape[0] % (8 * count) == 0
        self.hops = 2 * self.half if self.fits else 0
        self.done = 0
        self.up = self.down = None
        self.parts = [None] * count
        if not self.fits:
            self.total = lax.psum(rows, "ctx")

    def piece(self, offset):
        start = ((self.place + offset) % self.count) * self.part
        return lax.dynamic_slice_in_dim(self.rows, start, self.part, 0)

    def state(self):
        return [array for array in (self.up, self.down) if array is not None]

    def hop(self, earlier=()):
        if self.done >= self.hops:
            return
        self.done += 1
        if self.done <= self.half:
            distance = self.half + 1 - self.done
            down = self.piece(-distance)
            down = down if self.down is None else add_rounded(down, self.down)
            up = None
            if distance < self.half:
                up = self.piece(distance)
                up = up if self.up is None else add_rounded(up, self.up)
        else:
            if self.done == self.half + 1:
                own = self.piece(0).astype(f32) + self.down.astype(f32) + self.up.astype(f32)
                self.up = self.down = self.parts[0] = own.astype(bf16)
            distance = self.done - self.half
            up, down = self.up, (self.down if distance < self.half else None)
            if distance == self.half:
                self.down = None
        if earlier:
            up, down, _ = lax.optimization_barrier((up, down, earlier))
        if self.done <= self.half:
            self.down = shift(down, -1, self.count)
            if up is not None:
                self.up = shift(up, 1, self.count)
        else:
            self.up = self.parts[self.count - distance] = shift(up, 1, self.count)
            if down is not None:
                self.down = self.parts[distance] = shift(down, -1, self.count)

    def columns(self, columns):
        if not self.fits:
            return self.total[:, columns].astype(f32)
        line = [one[:, columns] for one in self.parts]
        twice = jnp.concatenate(line + line, axis=0)
        start = ((self.count - self.place) % self.count) * self.part
        return lax.dynamic_slice_in_dim(twice, start, self.rows.shape[0], 0).astype(f32)


def swap(array, mask):
    return lax.ppermute(array, "fsdp", [(i, i ^ mask) for i in range(4)])


def gather_pieces(piece):
    far = swap(piece, 2)
    return [piece, swap(piece, 1), far, swap(far, 1)]


def core_sums(pieces):
    near, far = swap(pieces[1], 1), swap(pieces[3], 1)
    return (pieces[0], near), add_all([(pieces[2], far)])[0]


def add_all(groups):
    return [sum(part.astype(f32) for part in group).astype(bf16) for group in groups]


def after(array, earlier):
    return lax.optimization_barrier((array, earlier))[0]


def in_order(pieces, me):
    odd = (me % 2) == 1
    high = (me // 2) == 1
    low_pair = [jnp.where(odd, pieces[1], pieces[0]), jnp.where(odd, pieces[0], pieces[1])]
    high_pair = [jnp.where(odd, pieces[3], pieces[2]), jnp.where(odd, pieces[2], pieces[3])]
    first = [jnp.where(high, b, a) for a, b in zip(low_pair, high_pair)]
    last = [jnp.where(high, a, b) for a, b in zip(low_pair, high_pair)]
    return jnp.concatenate(first + last, axis=0)


def out_of_order(whole, me):
    rows = whole.shape[0] // 4
    return [lax.dynamic_slice_in_dim(whole, (me ^ i) * rows, rows, 0) for i in range(4)]


def swap_halves(block):
    lane = lax.broadcasted_iota(jnp.int32, block.shape, 1)
    ahead = pltpu.roll(block, block.shape[1] - HEAD_DIM // 2, 1)
    behind = pltpu.roll(block, HEAD_DIM // 2, 1)
    return jnp.where(lane % HEAD_DIM < HEAD_DIM // 2, ahead, behind)


def normalise(rows):
    mean_value = jnp.mean(rows, axis=-1, keepdims=True)
    centered = rows - mean_value
    spread = jnp.mean(centered * centered, axis=-1, keepdims=True)
    inverse = lax.rsqrt(spread + norm_eps)
    return centered * inverse, inverse


def normed_times(normed, weights, mine):
    total = None
    for i, weight in enumerate(weights):
        part = dot(normed[mine ^ i], weight[: D // 4, :], 1, 0)
        total = part if total is None else total + part
    return total


def rotated(total, cosine, sine, target):
    for i in range(COLS // LANES):
        columns = slice(i * LANES, (i + 1) * LANES)
        block = total[:, columns]
        target[:, columns] = (block * cosine[...] + swap_halves(block) * sine[...]).astype(bf16)


def key_kernel(me, tokens, w0, w1, w2, w3, cosine, sine, keys, normed, gains):
    quarter = D // 4
    mine = me[0]
    weights = (w0, w1, w2, w3)

    @pl.when(pl.program_id(0) == 0)
    def _():
        unit, _ = normalise(tokens[...].astype(f32))
        for i, weight in enumerate(weights):
            gains[mine ^ i] = weight[quarter : quarter + 16, :quarter].astype(f32)[0:1, :]
        for i in range(4):
            normed[i] = (unit[:, i * quarter : (i + 1) * quarter] * gains[i]).astype(bf16)

    rotated(normed_times(normed, weights, mine), cosine, sine, keys)


def fixed(*shape):
    return pl.BlockSpec(shape, lambda j: (0,) * len(shape))


def project_keys(me, tokens, weights, cosine, sine):
    rows = tokens.shape[0]
    return pl.pallas_call(
        key_kernel,
        grid=(D // COLS,),
        in_specs=[SMEM, fixed(rows, D)]
        + [pl.BlockSpec((D // 4 + 16, COLS), lambda j: (0, j))] * 4
        + [fixed(rows, LANES)] * 2,
        out_specs=[
            pl.BlockSpec((rows, COLS), lambda j: (0, j)),
            fixed(4, rows, D // 4),
            fixed(4, 1, D // 4),
        ],
        out_shape=[
            jax.ShapeDtypeStruct((rows, D), bf16),
            jax.ShapeDtypeStruct((4, rows, D // 4), bf16),
            jax.ShapeDtypeStruct((4, 1, D // 4), f32),
        ],
        compiler_params=params(32),
        cost_estimate=cost(2),
        name="project_keys",
    )(me, tokens, *weights, cosine, sine)


def query_kernel(me, normed, w0, w1, w2, w3, cosine, sine, queries):
    rotated(normed_times(normed, (w0, w1, w2, w3), me[0]), cosine, sine, queries)


def value_kernel(me, normed, w0, w1, w2, w3, values):
    values[...] = normed_times(normed, (w0, w1, w2, w3), me[0]).astype(bf16)


def project(me, normed, weights, tables=()):
    rows = normed.shape[1]
    return pl.pallas_call(
        query_kernel if tables else value_kernel,
        grid=(D // COLS,),
        in_specs=[SMEM, fixed(4, rows, D // 4)]
        + [pl.BlockSpec((D // 4, COLS), lambda j: (0, j))] * 4
        + [fixed(rows, LANES)] * len(tables),
        out_specs=pl.BlockSpec((rows, COLS), lambda j: (0, j)),
        out_shape=jax.ShapeDtypeStruct((rows, D), bf16),
        compiler_params=params(32),
        cost_estimate=cost(2),
        name="project_queries" if tables else "project_values",
    )(me, normed, *weights, *tables)


def stacked(block, factor=None):
    if factor is not None:
        block = block * jnp.asarray(factor, block.dtype)
    lane = lax.broadcasted_iota(jnp.int32, block.shape, 1)
    zero = jnp.zeros_like(block)
    return jnp.concatenate(
        [jnp.where(lane < HEAD_DIM, block, zero), jnp.where(lane < HEAD_DIM, zero, block)], axis=0
    )


def unstacked(block):
    rows = block.shape[0] // 2
    lane = lax.broadcasted_iota(jnp.int32, (rows, block.shape[1]), 1)
    return jnp.where(lane < HEAD_DIM, block[:rows], block[rows:])


def causal(scores):
    rows, columns = scores.shape
    row = lax.broadcasted_iota(jnp.int32, scores.shape, 0) % (rows // 2)
    column = lax.broadcasted_iota(jnp.int32, scores.shape, 1)
    return jnp.where(column <= row, scores, neg_large)


def over_chunks(groups, per, first, visit, carry):
    for group in range(groups):
        start = first if group == 0 else 0
        if per == 1:
            if start == 0:
                carry = visit(group, 0, group, carry)
        else:

            def turn(i, held, group=group):
                return visit(group, i, group * per + i, held)

            carry = lax.fori_loop(start, per, turn, carry)
    return carry


def by_head(stacked_column):
    return unstacked(jnp.broadcast_to(stacked_column, (stacked_column.shape[0], LANES)))


def of_heads(block):
    shape = block.shape
    return jnp.concatenate(
        [
            jnp.broadcast_to(block[:, :1], shape),
            jnp.broadcast_to(block[:, HEAD_DIM : HEAD_DIM + 1], shape),
        ],
        axis=0,
    )


def attend_kernel(groups, per, base, merge, blocks, queries, *refs):
    keys, values = refs[:groups], refs[groups : 2 * groups]
    rest = refs[2 * groups :]
    before, rest = (rest[:4], rest[4:]) if merge else ((), rest)
    results, (stack, scores) = rest[:-2], rest[-2:]
    width = queries.shape[0] // 2
    own = blocks[0]
    low, high = slice(0, width), slice(width, 2 * width)
    with_own = base == 0
    empty = jnp.full((2 * width, LANES), neg_large, f32)
    nothing = jnp.zeros((2 * width, LANES), f32)

    def picked(chunk):
        up = blocks[base + chunk] > own
        which = up.astype(jnp.int32)
        return up, which, pl.ds(pl.multiple_of(which * width, width), width)

    for i, rows in enumerate((low, high)):
        stack[i] = stacked(queries[rows, :], SCALE)

    tops = (empty, empty)
    if with_own:
        first = causal(dot(stack[0], keys[0][0, low, :], 1, 1))
        second = causal(dot(stack[1], keys[0][0, high, :], 1, 1))
        third = dot(stack[1], keys[0][0, low, :], 1, 1)
        scores[0], scores[1], scores[2] = first, second, third
        tops = (first, jnp.maximum(second, third))

    def score(group, i, chunk, held):
        up, which, rows = picked(chunk)
        full = dot(stack[1], keys[group][i, low, :], 1, 1)
        part = dot(stack[which], keys[group][i, rows, :], 1, 1)
        scores[2 * chunk + 1] = full
        scores[2 * chunk + 2] = part
        return (
            jnp.maximum(held[0], jnp.where(up, empty, part)),
            jnp.maximum(jnp.maximum(held[1], full), jnp.where(up, part, empty)),
        )

    tops = over_chunks(groups, per, int(with_own), score, tops)
    top_low, top_high = (jnp.max(top, axis=1, keepdims=True) for top in tops)

    def weigh(slot, top, value_rows):
        weight = jnp.exp(scores[slot] - top)
        coarse = weight.astype(bf16)
        fine = (weight - coarse.astype(f32)).astype(bf16)
        return (
            weight,
            unstacked(dot(coarse, value_rows, 1, 0)),
            unstacked(dot(fine, value_rows, 1, 0)),
        )

    def summed(*parts):
        return tuple(sum(terms[1:], terms[0]) for terms in zip(*parts))

    none = (nothing, nothing[low], nothing[low])
    sums = (none, none)
    if with_own:
        sums = (
            weigh(0, top_low, values[0][0, low, :]),
            summed(
                weigh(1, top_high, values[0][0, high, :]), weigh(2, top_high, values[0][0, low, :])
            ),
        )

    def collect(group, i, chunk, held):
        up, which, rows = picked(chunk)
        full = weigh(2 * chunk + 1, top_high, values[group][i, low, :])
        part = weigh(
            2 * chunk + 2, jnp.where(up, top_high, top_low), values[group][i, rows, :]
        )
        to_low = tuple(jnp.where(up, jnp.zeros_like(term), term) for term in part)
        to_high = tuple(jnp.where(up, term, jnp.zeros_like(term)) for term in part)
        return summed(held[0], to_low), summed(held[1], full, to_high)

    sums = over_chunks(groups, per, int(with_own), collect, sums)
    for rows, top, (weight, coarse, fine) in zip((low, high), (top_low, top_high), sums):
        top = by_head(top)
        total = by_head(jnp.sum(weight, axis=1, keepdims=True))
        exact = coarse + fine
        if merge:
            old_top, old_total, old_coarse, old_exact = (ref[rows, :] for ref in before)
            new_top = jnp.maximum(top, old_top)
            now, then = jnp.exp(top - new_top), jnp.exp(old_top - new_top)
            total = total * now + old_total * then
            inverse = 1.0 / total
            attended, exact_out, log_total = results
            attended[rows, :] = ((coarse * now + old_coarse * then) * inverse).astype(bf16)
            exact_out[rows, :] = (exact * now + old_exact * then) * inverse
            log_total[rows, :] = new_top + jnp.log(total)
        else:
            for ref, value in zip(results, (top, total, coarse, exact)):
                ref[rows, :] = value


def grouped(chunks):
    per = 1 if len(chunks) <= 8 else len(chunks) // 4
    if per == 1:
        return [chunk[None] for chunk in chunks]
    return [jnp.stack(chunks[i : i + per]) for i in range(0, len(chunks), per)]


def column_block(rows):
    return pl.BlockSpec((rows, LANES), lambda j: (0, j))


def attend(base, blocks, queries, key_chunks, value_chunks, before=()):
    rows = queries.shape[0]
    keys, values = grouped(key_chunks), grouped(value_chunks)
    groups, per, count = len(keys), keys[0].shape[0], len(key_chunks)
    column = column_block(rows)
    chunk = pl.BlockSpec((per, rows, LANES), lambda j: (0, 0, j))
    types = (bf16, f32, f32) if before else (f32,) * 4
    return pl.pallas_call(
        partial(attend_kernel, groups, per, base, bool(before)),
        grid=(PAIRS,),
        in_specs=[SMEM, column] + [chunk] * (2 * groups) + [column] * len(before),
        out_specs=[column] * len(types),
        out_shape=[jax.ShapeDtypeStruct((rows, D), kind) for kind in types],
        scratch_shapes=[
            pltpu.VMEM((2, rows, LANES), bf16),
            pltpu.VMEM((2 * count + 1, rows, LANES), f32),
        ],
        compiler_params=params(56),
        cost_estimate=cost(2 * count),
        name=f"attend_{base}",
    )(blocks, queries, *keys, *values, *before)


def attend_back_kernel(groups, per, base, carried, blocks, queries, grads, exact, log_total, *refs):
    keys, values = refs[:groups], refs[groups : 2 * groups]
    rest = refs[2 * groups :]
    before, rest = (rest[:1], rest[1:]) if carried else ((), rest)
    with_own = base == 0
    (cosine, sine), rest = (rest[:2], rest[2:]) if with_own else ((None, None), rest)
    grad_queries = rest[0]
    grad_keys = rest[1 : groups + 1]
    grad_values = rest[groups + 1 : 2 * groups + 1]
    stack, grad_stack, deltas, logs = rest[2 * groups + 1 :]
    width = queries.shape[0] // 2
    own = blocks[0]
    low, high = slice(0, width), slice(width, 2 * width)

    for i, rows in enumerate((low, high)):
        stack[i] = stacked(queries[rows, :], SCALE)
        grad_rows = stacked(grads[rows, :])
        grad_stack[i] = grad_rows
        twice = jnp.concatenate([exact[rows, :], exact[rows, :]], axis=0)
        delta = jnp.sum(grad_rows.astype(f32) * twice, axis=1, keepdims=True)
        deltas[i] = jnp.broadcast_to(delta, deltas.shape[1:])
        logs[i] = of_heads(log_total[rows, :])

    def block(which, key_rows, value_rows, diagonal=False):
        query_rows, grad_rows = stack[which], grad_stack[which]
        raw = dot(query_rows, key_rows, 1, 1)
        if diagonal:
            raw = causal(raw)
        probability = jnp.exp(raw - logs[which])
        grad_prob = dot(grad_rows, value_rows, 1, 1)
        grad_scores = (probability * (grad_prob - deltas[which])).astype(bf16)
        return (
            unstacked(dot(grad_scores, key_rows, 1, 0)),
            dot(grad_scores, query_rows, 0, 0),
            dot(probability.astype(bf16), grad_rows, 0, 0),
        )

    if carried:
        sums = (before[0][low, :], before[0][high, :])
    else:
        sums = (jnp.zeros((width, LANES), f32),) * 2
    if with_own:
        key_low, value_low = keys[0][0, low, :], values[0][0, low, :]
        query_one, key_one, value_one = block(0, key_low, value_low, True)
        query_two, key_two, value_two = block(1, keys[0][0, high, :], values[0][0, high, :], True)
        query_all, key_all, value_all = block(1, key_low, value_low)
        sums = (sums[0] + query_one, sums[1] + query_two + query_all)
        grad_keys[0][0, low, :] = (key_one + key_all).astype(bf16)
        grad_values[0][0, low, :] = (value_one + value_all).astype(bf16)
        grad_keys[0][0, high, :] = key_two.astype(bf16)
        grad_values[0][0, high, :] = value_two.astype(bf16)

    def visit(group, i, chunk, held):
        up = blocks[base + chunk] > own
        which = up.astype(jnp.int32)
        rows = pl.ds(pl.multiple_of(which * width, width), width)
        query_all, key_all, value_all = block(1, keys[group][i, low, :], values[group][i, low, :])
        query_one, key_one, value_one = block(
            which, keys[group][i, rows, :], values[group][i, rows, :]
        )
        for target, whole, part in (
            (grad_keys[group], key_all, key_one),
            (grad_values[group], value_all, value_one),
        ):
            zero = jnp.zeros_like(part)
            target[i, low, :] = (whole + jnp.where(up, zero, part)).astype(bf16)
            target[i, high, :] = jnp.where(up, part, zero).astype(bf16)
        zero = jnp.zeros_like(query_one)
        return (
            held[0] + jnp.where(up, zero, query_one),
            held[1] + query_all + jnp.where(up, query_one, zero),
        )

    sums = over_chunks(groups, per, int(with_own), visit, sums)
    for rows, grad in zip((low, high), sums):
        if with_own:
            grad = grad * SCALE
            turned = grad * cosine[rows, :] - swap_halves(grad) * sine[rows, :]
            grad_queries[rows, :] = turned.astype(bf16)
        else:
            grad_queries[rows, :] = grad


def attend_back(base, blocks, queries, grads, exact, log_total, key_chunks, value_chunks, before, tables):
    rows = queries.shape[0]
    keys, values = grouped(key_chunks), grouped(value_chunks)
    groups, per, count = len(keys), keys[0].shape[0], len(key_chunks)
    column = column_block(rows)
    chunk = pl.BlockSpec((per, rows, LANES), lambda j: (0, 0, j))
    stat = pltpu.VMEM((2, rows, LANES), f32)
    half = pltpu.VMEM((2, rows, LANES), bf16)
    extra = (() if before is None else (before,)) + (tuple(tables) if base == 0 else ())
    extra_specs = ([] if before is None else [column]) + ([fixed(rows, LANES)] * 2 if base == 0 else [])
    result = pl.pallas_call(
        partial(attend_back_kernel, groups, per, base, before is not None),
        grid=(PAIRS,),
        in_specs=[SMEM] + [column] * 4 + [chunk] * (2 * groups) + extra_specs,
        out_specs=[column] + [chunk] * (2 * groups),
        out_shape=[jax.ShapeDtypeStruct((rows, D), bf16 if base == 0 else f32)]
        + [jax.ShapeDtypeStruct((per, rows, D), bf16)] * (2 * groups),
        scratch_shapes=[half, half, stat, stat],
        compiler_params=params(56),
        cost_estimate=cost(4.5 * count),
        name=f"attend_back_{base}",
    )(blocks, queries, grads, exact, log_total, *keys, *values, *extra)
    key_grads = [part[i] for part in result[1 : groups + 1] for i in range(per)]
    value_grads = [part[i] for part in result[groups + 1 :] for i in range(per)]
    return result[0], key_grads, value_grads


def q_back_kernel(me, normed, grads, w0, w1, w2, w3, g0, g1, g2, g3, back):
    mine = me[0]
    step = pl.program_id(0)
    block = grads[...]
    for i, (weight, target) in enumerate(((w0, g0), (w1, g1), (w2, g2), (w3, g3))):
        target[...] = dot(normed[mine ^ i], block, 0, 0).astype(bf16)
        part = dot(block, weight[...], 1, 1)

        @pl.when(step == 0)
        def _(i=i, part=part):
            back[mine ^ i] = part

        @pl.when(step > 0)
        def _(i=i, part=part):
            back[mine ^ i] += part


def q_back(me, normed, grads, weights):
    rows = grads.shape[0]

    column = pl.BlockSpec((D // 4, COLS), lambda j: (0, j))
    result = pl.pallas_call(
        q_back_kernel,
        grid=(D // COLS,),
        in_specs=[SMEM, fixed(4, rows, D // 4), pl.BlockSpec((rows, COLS), lambda j: (0, j))]
        + [column] * 4,
        out_specs=[column] * 4 + [fixed(4, rows, D // 4)],
        out_shape=[jax.ShapeDtypeStruct((D // 4, D), bf16)] * 4
        + [jax.ShapeDtypeStruct((4, rows, D // 4), f32)],
        compiler_params=params(32),
        cost_estimate=cost(4),
        name="q_back",
    )(me, normed, grads, *weights)
    return result[:4], result[4]


def middle_grads_kernel(me, normed, grad_gateup, attended, grad_branch, hidden, grad_out, gain, *refs):
    gateups, others = refs[:4], refs[4:8]
    normed_by, attended_by, hidden_by, gain_by = refs[8:]
    mine = me[0]
    quarter, part = D // 4, FF // 4
    ones = jnp.ones((normed.shape[0], LANES), bf16)
    coarse = gain[...].astype(bf16)
    fine = (gain[...] - coarse.astype(f32)).astype(bf16)
    for i in range(4):
        columns = slice(i * quarter, (i + 1) * quarter)
        normed_by[i] = normed[:, columns]
        attended_by[i] = attended[:, columns]
        hidden_by[i] = hidden[:, i * part : (i + 1) * part]
        gain_by[i] = dot(coarse[:, columns], ones, 0, 0) + dot(fine[:, columns], ones, 0, 0)
    for i in (3, 1, 2, 0):
        for first in range(0, 2 * FF, D):
            columns = slice(first, first + D)
            gateups[i][:, columns] = dot(normed_by[mine ^ i], grad_gateup[:, columns], 0, 0).astype(bf16)
        others[i][:, :D] = dot(attended_by[mine ^ i], grad_branch[...], 0, 0).astype(bf16)
        down = dot(hidden_by[mine ^ i], grad_out[...], 0, 0).astype(bf16)
        others[i][:, D : 2 * D] = down[:quarter]
        others[i][: quarter // 2, 2 * D : D + FF] = down[quarter:, : D // 2]
        others[i][quarter // 2 :, 2 * D : D + FF] = down[quarter:, D // 2 :]
        others[i][:, D + FF :] = gain_by[mine ^ i].astype(bf16)


def middle_grads(me, normed, grad_gateup, attended, grad_branch, hidden, grad_out, gain):
    rows = normed.shape[0]
    result = pl.pallas_call(
        middle_grads_kernel,
        in_specs=[SMEM] + [WHOLE] * 7,
        out_specs=[WHOLE] * 8,
        out_shape=[jax.ShapeDtypeStruct((D // 4, 2 * FF), bf16)] * 4
        + [jax.ShapeDtypeStruct((D // 4, D + FF + LANES), bf16)] * 4,
        scratch_shapes=[
            pltpu.VMEM((4, rows, D // 4), bf16),
            pltpu.VMEM((4, rows, D // 4), bf16),
            pltpu.VMEM((4, rows, FF // 4), bf16),
            pltpu.VMEM((4, D // 4, LANES), f32),
        ],
        compiler_params=params(32),
        cost_estimate=cost(4),
        name="middle_grads",
    )(me, normed, grad_gateup, attended, grad_branch, hidden, grad_out, gain)
    return result[:4], result[4:]


def v_back_kernel(me, normed, own, one, two, w0, w1, w2, w3, start, g0, g1, g2, g3, back):
    mine = me[0]

    @pl.when(pl.program_id(0) == 0)
    def _():
        back[...] = start[...]

    block = (own[...].astype(f32) + one[...].astype(f32) + two[...].astype(f32)).astype(bf16)
    for i, (weight, target) in enumerate(((w0, g0), (w1, g1), (w2, g2), (w3, g3))):
        target[...] = dot(normed[mine ^ i], block, 0, 0).astype(bf16)
        back[mine ^ i] += dot(block, weight[...], 1, 1)


def v_back(me, normed, sums, weights, start):
    rows = sums[0].shape[0]
    column = pl.BlockSpec((D // 4, COLS), lambda j: (0, j))
    result = pl.pallas_call(
        v_back_kernel,
        grid=(D // COLS,),
        in_specs=[SMEM, fixed(4, rows, D // 4)]
        + [pl.BlockSpec((rows, COLS), lambda j: (0, j))] * 3
        + [column] * 4
        + [fixed(4, rows, D // 4)],
        out_specs=[column] * 4 + [fixed(4, rows, D // 4)],
        out_shape=[jax.ShapeDtypeStruct((D // 4, D), bf16)] * 4
        + [jax.ShapeDtypeStruct((4, rows, D // 4), f32)],
        compiler_params=params(32),
        cost_estimate=cost(4),
        name="v_back",
    )(me, normed, *sums, *weights, start)
    return result[:4], result[4]


def k_back_kernel(
    me, normed, own, one, two, w0, w1, w2, w3, cosine, sine,
    start, tokens, gains, grad_middle, g0, g1, g2, g3, grad_tokens, back, block_of,
):
    mine = me[0]
    step = pl.program_id(0)
    last = pl.num_programs(0) - 1
    quarter = D // 4
    targets = (g0, g1, g2, g3)

    @pl.when(step == 0)
    def _():
        back[...] = start[...]

    @pl.when(step < last)
    def _():
        total = own[...].astype(f32) + one[...].astype(f32) + two[...].astype(f32)
        for i in range(COLS // LANES):
            columns = slice(i * LANES, (i + 1) * LANES)
            part = total[:, columns]
            turned = part * cosine[...] - swap_halves(part) * sine[...]
            block_of[:, columns] = turned.astype(bf16)
        for i, weight in enumerate((w0, w1, w2, w3)):
            targets[i][...] = dot(normed[mine ^ i], block_of[...], 0, 0).astype(bf16)
            back[mine ^ i] += dot(block_of[...], weight[:quarter, :], 1, 1)

    @pl.when(step == last)
    def _():
        unit, inverse = normalise(tokens[...].astype(f32))
        ones = jnp.ones((unit.shape[0], COLS), bf16)
        for i in range(4):
            part = back[i] * unit[:, i * quarter : (i + 1) * quarter]
            coarse = part.astype(bf16)
            fine = (part - coarse.astype(f32)).astype(bf16)
            total = (dot(coarse, ones, 0, 0) + dot(fine, ones, 0, 0)).astype(bf16)
            for k in range(4):

                @pl.when((mine ^ k) == i)
                def _(k=k, total=total):
                    targets[k][...] = total

        incoming = jnp.concatenate([back[i] for i in range(4)], axis=1)
        gain = jnp.concatenate([gains[i] for i in range(4)], axis=1)
        scaled = incoming * gain
        mean_one = jnp.mean(scaled, axis=-1, keepdims=True)
        mean_two = jnp.mean(scaled * unit, axis=-1, keepdims=True)
        grad_tokens[...] = grad_middle[...] + inverse * (scaled - mean_one - unit * mean_two)


def k_back(me, normed, sums, weights, cosine, sine, start, tokens, gains, grad_middle):
    rows = tokens.shape[0]
    half = D // COLS

    def early(height):
        return pl.BlockSpec((height, COLS), lambda j: (0, jnp.minimum(j, half - 1)))

    result = pl.pallas_call(
        k_back_kernel,
        grid=(half + 1,),
        in_specs=[SMEM, fixed(4, rows, D // 4)]
        + [early(rows)] * 3
        + [early(D // 4 + 16)] * 4
        + [fixed(rows, LANES)] * 2
        + [fixed(4, rows, D // 4), fixed(rows, D), fixed(4, 1, D // 4), fixed(rows, D)],
        out_specs=[pl.BlockSpec((D // 4, COLS), lambda j: (0, j))] * 4 + [fixed(rows, D)],
        out_shape=[jax.ShapeDtypeStruct((D // 4, D + COLS), bf16)] * 4
        + [jax.ShapeDtypeStruct((rows, D), f32)],
        scratch_shapes=[
            pltpu.VMEM((4, rows, D // 4), f32),
            pltpu.VMEM((rows, COLS), bf16),
        ],
        compiler_params=params(56),
        cost_estimate=cost(6),
        name="k_back",
    )(me, normed, *sums, *weights, cosine, sine, start, tokens, gains, grad_middle)
    return result[:4], result[4]


def layer_norm(token_rows, gain_row):
    mean_value = jnp.mean(token_rows, axis=-1, keepdims=True)
    centered = token_rows - mean_value
    spread = jnp.mean(centered * centered, axis=-1, keepdims=True)
    return centered * lax.rsqrt(spread + norm_eps) * gain_row


def geglu(gate_part, up_part):
    return jax.nn.gelu(gate_part, approximate=False) * up_part


def rope_tables(positions):
    half = HEAD_DIM // 2
    frequency = theta_base ** (-2.0 * jnp.arange(half, dtype=f32) / HEAD_DIM)
    angles = positions.astype(f32)[:, None] * frequency[None, :]
    cosine, sine = jnp.cos(angles), jnp.sin(angles)
    return (
        jnp.concatenate([cosine] * 4, axis=1),
        jnp.concatenate([-sine, sine, -sine, sine], axis=1),
    )


def on_device(
    tokens,
    pair_order,
    norm_one,
    qkv_weight,
    out_weight,
    norm_two,
    gateup_weight,
    down_weight,
    cotangent,
):
    count = lax.axis_size("ctx")
    me = lax.axis_index("fsdp")
    me_row = jnp.reshape(me, (1,)).astype(jnp.int32)
    gain_row = jnp.concatenate(
        [jnp.pad(norm_one, (0, COLS - D // 4)), jnp.pad(norm_two, (0, D - COLS - D // 4))]
    )
    gain_rows = jnp.broadcast_to(gain_row[None, :], (16, D))
    k_weights = gather_pieces(jnp.concatenate([qkv_weight[:, D : 2 * D], gain_rows], axis=0))
    v_piece = after(qkv_weight[:, 2 * D :], k_weights[2])
    v_far = swap(v_piece, 2)
    q_weights = gather_pieces(after(qkv_weight[:, :D], v_far))
    out_pieces = gather_pieces(after(out_weight, q_weights[2]))
    gateup_pieces = gather_pieces(after(gateup_weight, out_pieces[2]))
    down_pieces = gather_pieces(after(down_weight, gateup_pieces[2]))
    pair_order = after(pair_order, k_weights[1])
    place = ring_place(lax.axis_index("ctx"), count)
    width = tokens.shape[1] // 2
    offsets = jnp.asarray(ring_offsets(count), jnp.int32)
    chunk_devices = ring_device((place + offsets) % count, count)
    blocks = jnp.sum(
        jnp.where(
            chunk_devices[:, None] == jnp.arange(count, dtype=jnp.int32)[None, :],
            pair_order[None, :],
            0,
        ),
        axis=1,
    )
    low_block = blocks[0]
    high_block = 2 * count - 1 - low_block
    within = jnp.arange(width, dtype=jnp.int32)
    positions = jnp.concatenate([low_block * width + within, high_block * width + within])
    cosine, sine = rope_tables(positions)

    token_rows = tokens[0]
    keys, normed, gains = project_keys(me_row, token_rows, k_weights, cosine, sine)
    v_weights = [v_piece, swap(v_piece, 1), v_far, swap(after(v_far, keys), 1)]
    values = project(me_row, normed, v_weights)
    all_keys, all_values = ring_gather(keys, values, count)
    queries = project(me_row, normed, q_weights, (cosine, sine))
    split = count - 3 if count == 8 else count // 2
    so_far = attend(0, blocks, queries, all_keys[:split], all_values[:split])
    weight_out = in_order(out_pieces, me)
    weight_gateup = in_order(gateup_pieces, me)
    weight_down = in_order(down_pieces, me)
    attended, exact, log_total = attend(
        split, blocks, queries, all_keys[split:], all_values[split:], so_far
    )

    gain_two = in_order([part[D // 4, COLS : COLS + D // 4] for part in k_weights], me).astype(f32)
    middle = token_rows.astype(f32) + jnp.dot(attended, weight_out, preferred_element_type=f32)
    normed_two = layer_norm(middle, gain_two).astype(bf16)
    gateup = jnp.dot(normed_two, weight_gateup, preferred_element_type=f32)
    hidden_f, geglu_pull = jax.vjp(geglu, gateup[:, :FF], gateup[:, FF:])
    hidden = hidden_f.astype(bf16)
    result = middle + jnp.dot(hidden, weight_down, preferred_element_type=f32)
    grad_out = cotangent[0]
    grad_hidden = dot(grad_out, weight_down, 1, 1)
    grad_gate, grad_up = geglu_pull(grad_hidden)
    grad_gateup = jnp.concatenate([grad_gate, grad_up], axis=1).astype(bf16)
    grad_normed_two = dot(grad_gateup, weight_gateup, 1, 1)
    unit_two, inverse_two = normalise(middle)
    scaled = grad_normed_two * gain_two
    mean_one = jnp.mean(scaled, axis=-1, keepdims=True)
    mean_two = jnp.mean(scaled * unit_two, axis=-1, keepdims=True)
    gain_product = grad_normed_two * unit_two
    grad_middle = grad_out.astype(f32) + inverse_two * (scaled - mean_one - unit_two * mean_two)
    grad_branch = grad_middle.astype(bf16)
    grad_attended = dot(grad_branch, weight_out, 1, 1).astype(bf16)

    cuts = [0, 3, 5, 7, 8] if count == 8 else [i * count // 4 for i in range(5)]
    slots = {offset: slot for slot, offset in enumerate(ring_offsets(count))}
    key_parts, value_parts = [None] * count, [None] * count
    grad_queries = None

    def back_part(which, held, earlier):
        first, last = cuts[which], cuts[which + 1]
        query_rows, _ = lax.optimization_barrier((queries, earlier))
        held, key_parts[first:last], value_parts[first:last] = attend_back(
            first, blocks, query_rows, grad_attended, exact, log_total,
            all_keys[first:last], all_values[first:last], held, (cosine, sine),
        )
        return held

    def unfold(piece):
        top, rest = piece[:, :D], piece[:, D:]
        return jnp.concatenate(
            [top, jnp.concatenate([rest[: D // 8], rest[D // 8 :]], axis=1)], axis=0
        )

    def added(parts, which, down, up, distance):
        pair = [parts[slots[-distance]], parts[slots[distance]]]
        groups = [(one, sums[which]) for one, sums in zip(pair, (down, up)) if sums[which] is not None]
        sums = iter(add_all(groups)) if groups else None
        return [
            one if held[which] is None else next(sums) for one, held in zip(pair, (down, up))
        ]

    sent = []

    def hop(down, up, distance):
        arrived = ([], [])
        for which, parts in enumerate((key_parts, value_parts)):
            one, other = added(parts, which, down, up, distance)
            sent.extend([one, other])
            arrived[0].append(shift(one, -1, count))
            arrived[1].append(shift(other, 1, count))
        return arrived

    def mirror(pieces):
        return add_rounded(pieces[2], pieces[3])

    def over_cores(pieces):
        return [pieces[0], swap(pieces[1], 1), pieces[2], swap(pieces[3], 1)]

    def ended(*values):
        return lax.optimization_barrier(values)

    one, two, three = cuts[1:4]
    gateup_grads, middle_grads_all = middle_grads(
        me_row, normed_two, grad_gateup, attended, grad_branch, hidden, grad_out, gain_product
    )
    gateup_grads, middle_grads_all = over_cores(gateup_grads), over_cores(middle_grads_all)
    grad_queries = back_part(3, None, gateup_grads[0])
    gateup_grads, middle_grads_all, grad_queries, key_parts[three:], value_parts[three:] = ended(
        gateup_grads, middle_grads_all, grad_queries, key_parts[three:], value_parts[three:]
    )
    down = [shift(key_parts[-1], -1, count), None]
    up = [None, shift(value_parts[-1], 1, count)]
    gateup_far = mirror(gateup_grads)
    gateup_last = [swap(gateup_far[:, :FF], 2)]
    grad_queries = back_part(2, grad_queries, gateup_far)
    down[0], up[1], gateup_last[0], gateup_far, middle_grads_all, grad_queries = ended(
        down[0], up[1], gateup_last[0], gateup_far, middle_grads_all, grad_queries
    )
    key_parts[two:three], value_parts[two:three], _ = ended(
        key_parts[two:three], value_parts[two:three], down[0]
    )
    distances = list(range(count // 2 - 1, 0, -1))
    down, up = hop(down, up, distances[0])
    gateup_last.append(swap(gateup_far[:, FF:], 2))
    middle_far = mirror(middle_grads_all)
    grad_queries = back_part(1, grad_queries, middle_far)
    gateup_last, middle_far, grad_queries, key_parts[one:two], value_parts[one:two] = ended(
        gateup_last, middle_far, grad_queries, key_parts[one:two], value_parts[one:two]
    )
    gateup_last = jnp.concatenate(gateup_last, axis=1)
    middle_last = swap(middle_far, 2)
    for distance in distances[1:-1]:
        if key_parts[slots[-distance]] is None:
            grad_queries = back_part(0, grad_queries, sent[-4:])
        down, up = hop(down, up, distance)
    if key_parts[0] is None:
        grad_queries = back_part(0, grad_queries, sent[-4:])
    down[0], up[0], middle_last, grad_queries, key_parts[:one], value_parts[:one] = ended(
        down[0], up[0], middle_last, grad_queries, key_parts[:one], value_parts[:one]
    )
    down, up = hop(down, up, distances[-1])
    q_pieces, start = q_back(me_row, normed, after(grad_queries, sent[-4:]), q_weights)
    q_pieces = over_cores(q_pieces)
    q_last = swap(mirror(q_pieces), 2)
    gateup_sum, middle_sum = (
        add_all([(pieces[0], pieces[1], last)])[0]
        for pieces, last in ((gateup_grads, gateup_last), (middle_grads_all, middle_last))
    )
    middle_rows = jnp.concatenate([gateup_sum, middle_sum], axis=1)
    v_pieces, start = v_back(me_row, normed, (value_parts[0], down[1], up[1]), v_weights, start)
    v_pieces = over_cores(v_pieces)
    v_far = mirror(v_pieces)
    v_last = swap(v_far, 2)
    key_sums, middle_rows, start, v_far = ended(
        (key_parts[0], down[0], up[0]), middle_rows, start, v_far
    )
    middle_total = RingTotal(middle_rows, count)
    middle_total.hop()
    k_pieces, grad_tokens = k_back(
        me_row, normed, key_sums, k_weights, cosine, sine, start, token_rows, gains, grad_middle
    )
    k_pieces, q_last, v_last, middle_total.up, middle_total.down = ended(
        k_pieces, q_last, v_last, middle_total.up, middle_total.down
    )
    q_sum = add_all([(q_pieces[0], q_pieces[1], q_last)])[0]
    v_sum = add_all([(v_pieces[0], v_pieces[1], v_last)])[0]
    k_pieces = over_cores(k_pieces)
    k_last = swap(mirror(k_pieces), 2)
    middle_total.hop()
    middle_total.hop()
    k_last, middle_total.up, middle_total.down = ended(
        k_last, middle_total.up, middle_total.down
    )
    k_sum = add_all([(k_pieces[0], k_pieces[1], k_last)])[0]
    kv_total = RingTotal(jnp.concatenate([q_sum, k_sum, v_sum], axis=1), count)
    while kv_total.done < kv_total.hops - 1:
        kv_total.hop()
        middle_total.hop()
        kv_total.up, kv_total.down, middle_total.up, middle_total.down = ended(
            kv_total.up, kv_total.down, middle_total.up, middle_total.down
        )
    ends = (0, 3 * D, 4 * D, 4 * D + FF, 4 * D + FF + LANES)
    grad_gateup_weight, grad_out_weight, grad_down, grad_gain = (
        middle_total.columns(slice(ends[i], ends[i + 1])) for i in range(4)
    )
    gain_two_own = grad_gain[:, 0]
    grad_down_weight = unfold(grad_down)
    kv_total.hop((grad_gateup_weight, grad_out_weight, grad_down_weight, gain_two_own))
    return (
        result.astype(bf16)[None],
        grad_tokens[None],
        kv_total.columns(slice(2 * D, 2 * D + LANES))[:, 0],
        jnp.concatenate(
            [kv_total.columns(slice(0, 2 * D)), kv_total.columns(slice(2 * D + COLS, 3 * D + COLS))], axis=1
        ),
        grad_out_weight,
        gain_two_own,
        grad_gateup_weight,
        grad_down_weight,
    )


def solution(mesh):
    return jax.shard_map(
        on_device,
        mesh=mesh,
        in_specs=(
            P("fsdp", "ctx", None),
            P(),
            P("fsdp"),
            P("fsdp", None),
            P("fsdp", None),
            P("fsdp"),
            P("fsdp", None),
            P("fsdp", None),
            P("fsdp", "ctx", None),
        ),
        out_specs=(
            P("fsdp", "ctx", None),
            P("fsdp", "ctx", None),
            P("fsdp"),
            P("fsdp", None),
            P("fsdp", None),
            P("fsdp"),
            P("fsdp", None),
            P("fsdp", None),
        ),
        check_vma=False,
    )
```

```python
from functools import partial

import jax
import jax.numpy as jnp
from jax import lax
from jax.experimental import pallas as pl
from jax.experimental.pallas import tpu as pltpu
from jax.sharding import PartitionSpec as P

D = 768
HEAD_DIM = 64
FF = 1152
LANES = 128
PAIRS = D // LANES
COLS = 256
SCALE = HEAD_DIM**-0.5

theta_base = 160000.0
norm_eps = 1e-05
neg_large = -1e30
f32 = jnp.float32
bf16 = jnp.bfloat16

SMEM = pl.BlockSpec(memory_space=pltpu.SMEM)
WHOLE = pl.BlockSpec(memory_space=pltpu.VMEM)


def params(megabytes):
    return pltpu.CompilerParams(vmem_limit_bytes=megabytes * 2**20)


def cost(microseconds):
    return pl.CostEstimate(flops=int(microseconds * 1.15e9), bytes_accessed=1000, transcendentals=0)


def dot(left, right, left_dim, right_dim):
    return lax.dot_general(
        left, right, (((left_dim,), (right_dim,)), ((), ())), preferred_element_type=f32
    )


def ring_device(place, count):
    return jnp.where(place < count // 2, 2 * place, 2 * (count - 1 - place) + 1)


def ring_place(device, count):
    return jnp.where(device % 2 == 0, device // 2, count - 1 - device // 2)


def shift(array, step, count):
    half = count // 2
    order = [2 * i if i < half else 2 * (count - 1 - i) + 1 for i in range(count)]
    pairs = [(order[i], order[(i + step) % count]) for i in range(count)]
    return lax.ppermute(array, "ctx", pairs)


def ring_offsets(count):
    half = count // 2
    offsets = [0]
    for distance in range(1, half):
        offsets += [-distance, distance]
    return offsets + [half]


def ring_gather(first, second, count):
    half = count // 2
    firsts, seconds = [first], [second]
    up, down = (first, second), (first, second)
    for _ in range(1, half):
        up = tuple(shift(part, 1, count) for part in up)
        down = tuple(shift(part, -1, count) for part in down)
        firsts += [up[0], down[0]]
        seconds += [up[1], down[1]]
    firsts.append(shift(up[0], 1, count))
    seconds.append(shift(down[1], -1, count))
    return firsts, seconds


def add_rounded(left, right):
    return (left.astype(f32) + right.astype(f32)).astype(bf16)


class RingTotal:
    def __init__(self, rows, count):
        self.rows, self.count = rows, count
        self.half = count // 2
        self.place = ring_place(lax.axis_index("ctx"), count)
        self.part = rows.shape[0] // count
        self.fits = rows.shape[0] % (8 * count) == 0
        self.hops = 2 * self.half if self.fits else 0
        self.done = 0
        self.up = self.down = None
        self.parts = [None] * count
        if not self.fits:
            self.total = lax.psum(rows, "ctx")

    def piece(self, offset):
        start = ((self.place + offset) % self.count) * self.part
        return lax.dynamic_slice_in_dim(self.rows, start, self.part, 0)

    def state(self):
        return [array for array in (self.up, self.down) if array is not None]

    def hop(self, earlier=()):
        if self.done >= self.hops:
            return
        self.done += 1
        if self.done <= self.half:
            distance = self.half + 1 - self.done
            down = self.piece(-distance)
            down = down if self.down is None else add_rounded(down, self.down)
            up = None
            if distance < self.half:
                up = self.piece(distance)
                up = up if self.up is None else add_rounded(up, self.up)
        else:
            if self.done == self.half + 1:
                own = self.piece(0).astype(f32) + self.down.astype(f32) + self.up.astype(f32)
                self.up = self.down = self.parts[0] = own.astype(bf16)
            distance = self.done - self.half
            up, down = self.up, (self.down if distance < self.half else None)
            if distance == self.half:
                self.down = None
        if earlier:
            up, down, _ = lax.optimization_barrier((up, down, earlier))
        if self.done <= self.half:
            self.down = shift(down, -1, self.count)
            if up is not None:
                self.up = shift(up, 1, self.count)
        else:
            self.up = self.parts[self.count - distance] = shift(up, 1, self.count)
            if down is not None:
                self.down = self.parts[distance] = shift(down, -1, self.count)

    def columns(self, columns):
        if not self.fits:
            return self.total[:, columns].astype(f32)
        line = [one[:, columns] for one in self.parts]
        twice = jnp.concatenate(line + line, axis=0)
        start = ((self.count - self.place) % self.count) * self.part
        return lax.dynamic_slice_in_dim(twice, start, self.rows.shape[0], 0).astype(f32)


def swap(array, mask):
    return lax.ppermute(array, "fsdp", [(i, i ^ mask) for i in range(4)])


def gather_pieces(piece):
    far = swap(piece, 2)
    return [piece, swap(piece, 1), far, swap(far, 1)]


def core_sums(pieces):
    near, far = swap(pieces[1], 1), swap(pieces[3], 1)
    return (pieces[0], near), add_all([(pieces[2], far)])[0]


def add_all(groups):
    return [sum(part.astype(f32) for part in group).astype(bf16) for group in groups]


def after(array, earlier):
    return lax.optimization_barrier((array, earlier))[0]


def in_order(pieces, me):
    odd = (me % 2) == 1
    high = (me // 2) == 1
    low_pair = [jnp.where(odd, pieces[1], pieces[0]), jnp.where(odd, pieces[0], pieces[1])]
    high_pair = [jnp.where(odd, pieces[3], pieces[2]), jnp.where(odd, pieces[2], pieces[3])]
    first = [jnp.where(high, b, a) for a, b in zip(low_pair, high_pair)]
    last = [jnp.where(high, a, b) for a, b in zip(low_pair, high_pair)]
    return jnp.concatenate(first + last, axis=0)


def out_of_order(whole, me):
    rows = whole.shape[0] // 4
    return [lax.dynamic_slice_in_dim(whole, (me ^ i) * rows, rows, 0) for i in range(4)]


def swap_halves(block):
    lane = lax.broadcasted_iota(jnp.int32, block.shape, 1)
    ahead = pltpu.roll(block, block.shape[1] - HEAD_DIM // 2, 1)
    behind = pltpu.roll(block, HEAD_DIM // 2, 1)
    return jnp.where(lane % HEAD_DIM < HEAD_DIM // 2, ahead, behind)


def normalise(rows):
    mean_value = jnp.mean(rows, axis=-1, keepdims=True)
    centered = rows - mean_value
    spread = jnp.mean(centered * centered, axis=-1, keepdims=True)
    inverse = lax.rsqrt(spread + norm_eps)
    return centered * inverse, inverse


def normed_times(normed, weights, mine):
    total = None
    for i, weight in enumerate(weights):
        part = dot(normed[mine ^ i], weight[: D // 4, :], 1, 0)
        total = part if total is None else total + part
    return total


def rotated(total, cosine, sine, target):
    for i in range(COLS // LANES):
        columns = slice(i * LANES, (i + 1) * LANES)
        block = total[:, columns]
        target[:, columns] = (block * cosine[...] + swap_halves(block) * sine[...]).astype(bf16)


def key_kernel(me, tokens, w0, w1, w2, w3, cosine, sine, keys, normed, gains):
    quarter = D // 4
    mine = me[0]
    weights = (w0, w1, w2, w3)

    @pl.when(pl.program_id(0) == 0)
    def _():
        unit, _ = normalise(tokens[...].astype(f32))
        for i, weight in enumerate(weights):
            gains[mine ^ i] = weight[quarter : quarter + 16, :quarter].astype(f32)[0:1, :]
        for i in range(4):
            normed[i] = (unit[:, i * quarter : (i + 1) * quarter] * gains[i]).astype(bf16)

    rotated(normed_times(normed, weights, mine), cosine, sine, keys)


def fixed(*shape):
    return pl.BlockSpec(shape, lambda j: (0,) * len(shape))


def project_keys(me, tokens, weights, cosine, sine):
    rows = tokens.shape[0]
    return pl.pallas_call(
        key_kernel,
        grid=(D // COLS,),
        in_specs=[SMEM, fixed(rows, D)]
        + [pl.BlockSpec((D // 4 + 16, COLS), lambda j: (0, j))] * 4
        + [fixed(rows, LANES)] * 2,
        out_specs=[
            pl.BlockSpec((rows, COLS), lambda j: (0, j)),
            fixed(4, rows, D // 4),
            fixed(4, 1, D // 4),
        ],
        out_shape=[
            jax.ShapeDtypeStruct((rows, D), bf16),
            jax.ShapeDtypeStruct((4, rows, D // 4), bf16),
            jax.ShapeDtypeStruct((4, 1, D // 4), f32),
        ],
        compiler_params=params(32),
        cost_estimate=cost(2),
        name="project_keys",
    )(me, tokens, *weights, cosine, sine)


def query_kernel(me, normed, w0, w1, w2, w3, cosine, sine, queries):
    rotated(normed_times(normed, (w0, w1, w2, w3), me[0]), cosine, sine, queries)


def value_kernel(me, normed, w0, w1, w2, w3, values):
    values[...] = normed_times(normed, (w0, w1, w2, w3), me[0]).astype(bf16)


def project(me, normed, weights, tables=()):
    rows = normed.shape[1]
    return pl.pallas_call(
        query_kernel if tables else value_kernel,
        grid=(D // COLS,),
        in_specs=[SMEM, fixed(4, rows, D // 4)]
        + [pl.BlockSpec((D // 4, COLS), lambda j: (0, j))] * 4
        + [fixed(rows, LANES)] * len(tables),
        out_specs=pl.BlockSpec((rows, COLS), lambda j: (0, j)),
        out_shape=jax.ShapeDtypeStruct((rows, D), bf16),
        compiler_params=params(32),
        cost_estimate=cost(2),
        name="project_queries" if tables else "project_values",
    )(me, normed, *weights, *tables)


def stacked(block, factor=None):
    if factor is not None:
        block = block * jnp.asarray(factor, block.dtype)
    lane = lax.broadcasted_iota(jnp.int32, block.shape, 1)
    zero = jnp.zeros_like(block)
    return jnp.concatenate(
        [jnp.where(lane < HEAD_DIM, block, zero), jnp.where(lane < HEAD_DIM, zero, block)], axis=0
    )


def unstacked(block):
    rows = block.shape[0] // 2
    lane = lax.broadcasted_iota(jnp.int32, (rows, block.shape[1]), 1)
    return jnp.where(lane < HEAD_DIM, block[:rows], block[rows:])


def causal(scores):
    rows, columns = scores.shape
    row = lax.broadcasted_iota(jnp.int32, scores.shape, 0) % (rows // 2)
    column = lax.broadcasted_iota(jnp.int32, scores.shape, 1)
    return jnp.where(column <= row, scores, neg_large)


def over_chunks(groups, per, first, visit, carry):
    for group in range(groups):
        start = first if group == 0 else 0
        if per == 1:
            if start == 0:
                carry = visit(group, 0, group, carry)
        else:

            def turn(i, held, group=group):
                return visit(group, i, group * per + i, held)

            carry = lax.fori_loop(start, per, turn, carry)
    return carry


def by_head(stacked_column):
    return unstacked(jnp.broadcast_to(stacked_column, (stacked_column.shape[0], LANES)))


def of_heads(block):
    shape = block.shape
    return jnp.concatenate(
        [
            jnp.broadcast_to(block[:, :1], shape),
            jnp.broadcast_to(block[:, HEAD_DIM : HEAD_DIM + 1], shape),
        ],
        axis=0,
    )


def attend_kernel(groups, per, base, merge, blocks, queries, *refs):
    keys, values = refs[:groups], refs[groups : 2 * groups]
    rest = refs[2 * groups :]
    before, rest = (rest[:4], rest[4:]) if merge else ((), rest)
    results, (stack, scores) = rest[:-2], rest[-2:]
    width = queries.shape[0] // 2
    own = blocks[0]
    low, high = slice(0, width), slice(width, 2 * width)
    with_own = base == 0
    empty = jnp.full((2 * width, LANES), neg_large, f32)
    nothing = jnp.zeros((2 * width, LANES), f32)

    def picked(chunk):
        up = blocks[base + chunk] > own
        which = up.astype(jnp.int32)
        return up, which, pl.ds(pl.multiple_of(which * width, width), width)

    for i, rows in enumerate((low, high)):
        stack[i] = stacked(queries[rows, :], SCALE)

    tops = (empty, empty)
    if with_own:
        first = causal(dot(stack[0], keys[0][0, low, :], 1, 1))
        second = causal(dot(stack[1], keys[0][0, high, :], 1, 1))
        third = dot(stack[1], keys[0][0, low, :], 1, 1)
        scores[0], scores[1], scores[2] = first, second, third
        tops = (first, jnp.maximum(second, third))

    def score(group, i, chunk, held):
        up, which, rows = picked(chunk)
        full = dot(stack[1], keys[group][i, low, :], 1, 1)
        part = dot(stack[which], keys[group][i, rows, :], 1, 1)
        scores[2 * chunk + 1] = full
        scores[2 * chunk + 2] = part
        return (
            jnp.maximum(held[0], jnp.where(up, empty, part)),
            jnp.maximum(jnp.maximum(held[1], full), jnp.where(up, part, empty)),
        )

    tops = over_chunks(groups, per, int(with_own), score, tops)
    top_low, top_high = (jnp.max(top, axis=1, keepdims=True) for top in tops)

    def weigh(slot, top, value_rows):
        weight = jnp.exp(scores[slot] - top)
        coarse = weight.astype(bf16)
        fine = (weight - coarse.astype(f32)).astype(bf16)
        return (
            weight,
            unstacked(dot(coarse, value_rows, 1, 0)),
            unstacked(dot(fine, value_rows, 1, 0)),
        )

    def summed(*parts):
        return tuple(sum(terms[1:], terms[0]) for terms in zip(*parts))

    none = (nothing, nothing[low], nothing[low])
    sums = (none, none)
    if with_own:
        sums = (
            weigh(0, top_low, values[0][0, low, :]),
            summed(
                weigh(1, top_high, values[0][0, high, :]), weigh(2, top_high, values[0][0, low, :])
            ),
        )

    def collect(group, i, chunk, held):
        up, which, rows = picked(chunk)
        full = weigh(2 * chunk + 1, top_high, values[group][i, low, :])
        part = weigh(
            2 * chunk + 2, jnp.where(up, top_high, top_low), values[group][i, rows, :]
        )
        to_low = tuple(jnp.where(up, jnp.zeros_like(term), term) for term in part)
        to_high = tuple(jnp.where(up, term, jnp.zeros_like(term)) for term in part)
        return summed(held[0], to_low), summed(held[1], full, to_high)

    sums = over_chunks(groups, per, int(with_own), collect, sums)
    for rows, top, (weight, coarse, fine) in zip((low, high), (top_low, top_high), sums):
        top = by_head(top)
        total = by_head(jnp.sum(weight, axis=1, keepdims=True))
        exact = coarse + fine
        if merge:
            old_top, old_total, old_coarse, old_exact = (ref[rows, :] for ref in before)
            new_top = jnp.maximum(top, old_top)
            now, then = jnp.exp(top - new_top), jnp.exp(old_top - new_top)
            total = total * now + old_total * then
            inverse = 1.0 / total
            attended, exact_out, log_total = results
            attended[rows, :] = ((coarse * now + old_coarse * then) * inverse).astype(bf16)
            exact_out[rows, :] = (exact * now + old_exact * then) * inverse
            log_total[rows, :] = new_top + jnp.log(total)
        else:
            for ref, value in zip(results, (top, total, coarse, exact)):
                ref[rows, :] = value


def grouped(chunks):
    per = 1 if len(chunks) <= 8 else len(chunks) // 4
    if per == 1:
        return [chunk[None] for chunk in chunks]
    return [jnp.stack(chunks[i : i + per]) for i in range(0, len(chunks), per)]


def column_block(rows):
    return pl.BlockSpec((rows, LANES), lambda j: (0, j))


def attend(base, blocks, queries, key_chunks, value_chunks, before=()):
    rows = queries.shape[0]
    keys, values = grouped(key_chunks), grouped(value_chunks)
    groups, per, count = len(keys), keys[0].shape[0], len(key_chunks)
    column = column_block(rows)
    chunk = pl.BlockSpec((per, rows, LANES), lambda j: (0, 0, j))
    types = (bf16, f32, f32) if before else (f32,) * 4
    return pl.pallas_call(
        partial(attend_kernel, groups, per, base, bool(before)),
        grid=(PAIRS,),
        in_specs=[SMEM, column] + [chunk] * (2 * groups) + [column] * len(before),
        out_specs=[column] * len(types),
        out_shape=[jax.ShapeDtypeStruct((rows, D), kind) for kind in types],
        scratch_shapes=[
            pltpu.VMEM((2, rows, LANES), bf16),
            pltpu.VMEM((2 * count + 1, rows, LANES), f32),
        ],
        compiler_params=params(56),
        cost_estimate=cost(2 * count),
        name=f"attend_{base}",
    )(blocks, queries, *keys, *values, *before)


def attend_back_kernel(groups, per, base, carried, blocks, queries, grads, exact, log_total, *refs):
    keys, values = refs[:groups], refs[groups : 2 * groups]
    rest = refs[2 * groups :]
    before, rest = (rest[:1], rest[1:]) if carried else ((), rest)
    with_own = base == 0
    (cosine, sine), rest = (rest[:2], rest[2:]) if with_own else ((None, None), rest)
    grad_queries = rest[0]
    grad_keys = rest[1 : groups + 1]
    grad_values = rest[groups + 1 : 2 * groups + 1]
    stack, grad_stack, deltas, logs = rest[2 * groups + 1 :]
    width = queries.shape[0] // 2
    own = blocks[0]
    low, high = slice(0, width), slice(width, 2 * width)

    for i, rows in enumerate((low, high)):
        stack[i] = stacked(queries[rows, :], SCALE)
        grad_rows = stacked(grads[rows, :])
        grad_stack[i] = grad_rows
        twice = jnp.concatenate([exact[rows, :], exact[rows, :]], axis=0)
        delta = jnp.sum(grad_rows.astype(f32) * twice, axis=1, keepdims=True)
        deltas[i] = jnp.broadcast_to(delta, deltas.shape[1:])
        logs[i] = of_heads(log_total[rows, :])

    def block(which, key_rows, value_rows, diagonal=False):
        query_rows, grad_rows = stack[which], grad_stack[which]
        raw = dot(query_rows, key_rows, 1, 1)
        if diagonal:
            raw = causal(raw)
        probability = jnp.exp(raw - logs[which])
        grad_prob = dot(grad_rows, value_rows, 1, 1)
        grad_scores = (probability * (grad_prob - deltas[which])).astype(bf16)
        return (
            unstacked(dot(grad_scores, key_rows, 1, 0)),
            dot(grad_scores, query_rows, 0, 0),
            dot(probability.astype(bf16), grad_rows, 0, 0),
        )

    if carried:
        sums = (before[0][low, :], before[0][high, :])
    else:
        sums = (jnp.zeros((width, LANES), f32),) * 2
    if with_own:
        key_low, value_low = keys[0][0, low, :], values[0][0, low, :]
        query_one, key_one, value_one = block(0, key_low, value_low, True)
        query_two, key_two, value_two = block(1, keys[0][0, high, :], values[0][0, high, :], True)
        query_all, key_all, value_all = block(1, key_low, value_low)
        sums = (sums[0] + query_one, sums[1] + query_two + query_all)
        grad_keys[0][0, low, :] = (key_one + key_all).astype(bf16)
        grad_values[0][0, low, :] = (value_one + value_all).astype(bf16)
        grad_keys[0][0, high, :] = key_two.astype(bf16)
        grad_values[0][0, high, :] = value_two.astype(bf16)

    def visit(group, i, chunk, held):
        up = blocks[base + chunk] > own
        which = up.astype(jnp.int32)
        rows = pl.ds(pl.multiple_of(which * width, width), width)
        query_all, key_all, value_all = block(1, keys[group][i, low, :], values[group][i, low, :])
        query_one, key_one, value_one = block(
            which, keys[group][i, rows, :], values[group][i, rows, :]
        )
        for target, whole, part in (
            (grad_keys[group], key_all, key_one),
            (grad_values[group], value_all, value_one),
        ):
            zero = jnp.zeros_like(part)
            target[i, low, :] = (whole + jnp.where(up, zero, part)).astype(bf16)
            target[i, high, :] = jnp.where(up, part, zero).astype(bf16)
        zero = jnp.zeros_like(query_one)
        return (
            held[0] + jnp.where(up, zero, query_one),
            held[1] + query_all + jnp.where(up, query_one, zero),
        )

    sums = over_chunks(groups, per, int(with_own), visit, sums)
    for rows, grad in zip((low, high), sums):
        if with_own:
            grad = grad * SCALE
            turned = grad * cosine[rows, :] - swap_halves(grad) * sine[rows, :]
            grad_queries[rows, :] = turned.astype(bf16)
        else:
            grad_queries[rows, :] = grad


def attend_back(base, blocks, queries, grads, exact, log_total, key_chunks, value_chunks, before, tables):
    rows = queries.shape[0]
    keys, values = grouped(key_chunks), grouped(value_chunks)
    groups, per, count = len(keys), keys[0].shape[0], len(key_chunks)
    column = column_block(rows)
    chunk = pl.BlockSpec((per, rows, LANES), lambda j: (0, 0, j))
    stat = pltpu.VMEM((2, rows, LANES), f32)
    half = pltpu.VMEM((2, rows, LANES), bf16)
    extra = (() if before is None else (before,)) + (tuple(tables) if base == 0 else ())
    extra_specs = ([] if before is None else [column]) + ([fixed(rows, LANES)] * 2 if base == 0 else [])
    result = pl.pallas_call(
        partial(attend_back_kernel, groups, per, base, before is not None),
        grid=(PAIRS,),
        in_specs=[SMEM] + [column] * 4 + [chunk] * (2 * groups) + extra_specs,
        out_specs=[column] + [chunk] * (2 * groups),
        out_shape=[jax.ShapeDtypeStruct((rows, D), bf16 if base == 0 else f32)]
        + [jax.ShapeDtypeStruct((per, rows, D), bf16)] * (2 * groups),
        scratch_shapes=[half, half, stat, stat],
        compiler_params=params(56),
        cost_estimate=cost(4.5 * count),
        name=f"attend_back_{base}",
    )(blocks, queries, grads, exact, log_total, *keys, *values, *extra)
    key_grads = [part[i] for part in result[1 : groups + 1] for i in range(per)]
    value_grads = [part[i] for part in result[groups + 1 :] for i in range(per)]
    return result[0], key_grads, value_grads


def q_back_kernel(me, normed, grads, w0, w1, w2, w3, g0, g1, g2, g3, back):
    mine = me[0]
    step = pl.program_id(0)
    block = grads[...]
    for i, (weight, target) in enumerate(((w0, g0), (w1, g1), (w2, g2), (w3, g3))):
        target[...] = dot(normed[mine ^ i], block, 0, 0).astype(bf16)
        part = dot(block, weight[...], 1, 1)

        @pl.when(step == 0)
        def _(i=i, part=part):
            back[mine ^ i] = part

        @pl.when(step > 0)
        def _(i=i, part=part):
            back[mine ^ i] += part


def q_back(me, normed, grads, weights):
    rows = grads.shape[0]

    column = pl.BlockSpec((D // 4, COLS), lambda j: (0, j))
    result = pl.pallas_call(
        q_back_kernel,
        grid=(D // COLS,),
        in_specs=[SMEM, fixed(4, rows, D // 4), pl.BlockSpec((rows, COLS), lambda j: (0, j))]
        + [column] * 4,
        out_specs=[column] * 4 + [fixed(4, rows, D // 4)],
        out_shape=[jax.ShapeDtypeStruct((D // 4, D), bf16)] * 4
        + [jax.ShapeDtypeStruct((4, rows, D // 4), f32)],
        compiler_params=params(32),
        cost_estimate=cost(4),
        name="q_back",
    )(me, normed, grads, *weights)
    return result[:4], result[4]


def middle_grads_kernel(me, normed, grad_gateup, attended, grad_branch, hidden, grad_out, gain, *refs):
    gateups, others = refs[:4], refs[4:8]
    normed_by, attended_by, hidden_by, gain_by = refs[8:]
    mine = me[0]
    quarter, part = D // 4, FF // 4
    ones = jnp.ones((normed.shape[0], LANES), bf16)
    coarse = gain[...].astype(bf16)
    fine = (gain[...] - coarse.astype(f32)).astype(bf16)
    for i in range(4):
        columns = slice(i * quarter, (i + 1) * quarter)
        normed_by[i] = normed[:, columns]
        attended_by[i] = attended[:, columns]
        hidden_by[i] = hidden[:, i * part : (i + 1) * part]
        gain_by[i] = dot(coarse[:, columns], ones, 0, 0) + dot(fine[:, columns], ones, 0, 0)
    for i in (3, 1, 2, 0):
        for first in range(0, 2 * FF, D):
            columns = slice(first, first + D)
            gateups[i][:, columns] = dot(normed_by[mine ^ i], grad_gateup[:, columns], 0, 0).astype(bf16)
        others[i][:, :D] = dot(attended_by[mine ^ i], grad_branch[...], 0, 0).astype(bf16)
        down = dot(hidden_by[mine ^ i], grad_out[...], 0, 0).astype(bf16)
        others[i][:, D : 2 * D] = down[:quarter]
        others[i][: quarter // 2, 2 * D : D + FF] = down[quarter:, : D // 2]
        others[i][quarter // 2 :, 2 * D : D + FF] = down[quarter:, D // 2 :]
        others[i][:, D + FF :] = gain_by[mine ^ i].astype(bf16)


def middle_grads(me, normed, grad_gateup, attended, grad_branch, hidden, grad_out, gain):
    rows = normed.shape[0]
    result = pl.pallas_call(
        middle_grads_kernel,
        in_specs=[SMEM] + [WHOLE] * 7,
        out_specs=[WHOLE] * 8,
        out_shape=[jax.ShapeDtypeStruct((D // 4, 2 * FF), bf16)] * 4
        + [jax.ShapeDtypeStruct((D // 4, D + FF + LANES), bf16)] * 4,
        scratch_shapes=[
            pltpu.VMEM((4, rows, D // 4), bf16),
            pltpu.VMEM((4, rows, D // 4), bf16),
            pltpu.VMEM((4, rows, FF // 4), bf16),
            pltpu.VMEM((4, D // 4, LANES), f32),
        ],
        compiler_params=params(32),
        cost_estimate=cost(4),
        name="middle_grads",
    )(me, normed, grad_gateup, attended, grad_branch, hidden, grad_out, gain)
    return result[:4], result[4:]


def v_back_kernel(me, normed, own, one, two, w0, w1, w2, w3, start, g0, g1, g2, g3, back):
    mine = me[0]

    @pl.when(pl.program_id(0) == 0)
    def _():
        back[...] = start[...]

    block = (own[...].astype(f32) + one[...].astype(f32) + two[...].astype(f32)).astype(bf16)
    for i, (weight, target) in enumerate(((w0, g0), (w1, g1), (w2, g2), (w3, g3))):
        target[...] = dot(normed[mine ^ i], block, 0, 0).astype(bf16)
        back[mine ^ i] += dot(block, weight[...], 1, 1)


def v_back(me, normed, sums, weights, start):
    rows = sums[0].shape[0]
    column = pl.BlockSpec((D // 4, COLS), lambda j: (0, j))
    result = pl.pallas_call(
        v_back_kernel,
        grid=(D // COLS,),
        in_specs=[SMEM, fixed(4, rows, D // 4)]
        + [pl.BlockSpec((rows, COLS), lambda j: (0, j))] * 3
        + [column] * 4
        + [fixed(4, rows, D // 4)],
        out_specs=[column] * 4 + [fixed(4, rows, D // 4)],
        out_shape=[jax.ShapeDtypeStruct((D // 4, D), bf16)] * 4
        + [jax.ShapeDtypeStruct((4, rows, D // 4), f32)],
        compiler_params=params(32),
        cost_estimate=cost(4),
        name="v_back",
    )(me, normed, *sums, *weights, start)
    return result[:4], result[4]


def k_back_kernel(
    me, normed, own, one, two, w0, w1, w2, w3, cosine, sine,
    start, tokens, gains, grad_middle, g0, g1, g2, g3, grad_tokens, back, block_of,
):
    mine = me[0]
    step = pl.program_id(0)
    last = pl.num_programs(0) - 1
    quarter = D // 4
    targets = (g0, g1, g2, g3)

    @pl.when(step == 0)
    def _():
        back[...] = start[...]

    @pl.when(step < last)
    def _():
        total = own[...].astype(f32) + one[...].astype(f32) + two[...].astype(f32)
        for i in range(COLS // LANES):
            columns = slice(i * LANES, (i + 1) * LANES)
            part = total[:, columns]
            turned = part * cosine[...] - swap_halves(part) * sine[...]
            block_of[:, columns] = turned.astype(bf16)
        for i, weight in enumerate((w0, w1, w2, w3)):
            targets[i][...] = dot(normed[mine ^ i], block_of[...], 0, 0).astype(bf16)
            back[mine ^ i] += dot(block_of[...], weight[:quarter, :], 1, 1)

    @pl.when(step == last)
    def _():
        unit, inverse = normalise(tokens[...].astype(f32))
        ones = jnp.ones((unit.shape[0], COLS), bf16)
        for i in range(4):
            part = back[i] * unit[:, i * quarter : (i + 1) * quarter]
            coarse = part.astype(bf16)
            fine = (part - coarse.astype(f32)).astype(bf16)
            total = (dot(coarse, ones, 0, 0) + dot(fine, ones, 0, 0)).astype(bf16)
            for k in range(4):

                @pl.when((mine ^ k) == i)
                def _(k=k, total=total):
                    targets[k][...] = total

        incoming = jnp.concatenate([back[i] for i in range(4)], axis=1)
        gain = jnp.concatenate([gains[i] for i in range(4)], axis=1)
        scaled = incoming * gain
        mean_one = jnp.mean(scaled, axis=-1, keepdims=True)
        mean_two = jnp.mean(scaled * unit, axis=-1, keepdims=True)
        grad_tokens[...] = grad_middle[...] + inverse * (scaled - mean_one - unit * mean_two)


def k_back(me, normed, sums, weights, cosine, sine, start, tokens, gains, grad_middle):
    rows = tokens.shape[0]
    half = D // COLS

    def early(height):
        return pl.BlockSpec((height, COLS), lambda j: (0, jnp.minimum(j, half - 1)))

    result = pl.pallas_call(
        k_back_kernel,
        grid=(half + 1,),
        in_specs=[SMEM, fixed(4, rows, D // 4)]
        + [early(rows)] * 3
        + [early(D // 4 + 16)] * 4
        + [fixed(rows, LANES)] * 2
        + [fixed(4, rows, D // 4), fixed(rows, D), fixed(4, 1, D // 4), fixed(rows, D)],
        out_specs=[pl.BlockSpec((D // 4, COLS), lambda j: (0, j))] * 4 + [fixed(rows, D)],
        out_shape=[jax.ShapeDtypeStruct((D // 4, D + COLS), bf16)] * 4
        + [jax.ShapeDtypeStruct((rows, D), f32)],
        scratch_shapes=[
            pltpu.VMEM((4, rows, D // 4), f32),
            pltpu.VMEM((rows, COLS), bf16),
        ],
        compiler_params=params(56),
        cost_estimate=cost(6),
        name="k_back",
    )(me, normed, *sums, *weights, cosine, sine, start, tokens, gains, grad_middle)
    return result[:4], result[4]


def layer_norm(token_rows, gain_row):
    mean_value = jnp.mean(token_rows, axis=-1, keepdims=True)
    centered = token_rows - mean_value
    spread = jnp.mean(centered * centered, axis=-1, keepdims=True)
    return centered * lax.rsqrt(spread + norm_eps) * gain_row


def geglu(gate_part, up_part):
    return jax.nn.gelu(gate_part, approximate=False) * up_part


def rope_tables(positions):
    half = HEAD_DIM // 2
    frequency = theta_base ** (-2.0 * jnp.arange(half, dtype=f32) / HEAD_DIM)
    angles = positions.astype(f32)[:, None] * frequency[None, :]
    cosine, sine = jnp.cos(angles), jnp.sin(angles)
    return (
        jnp.concatenate([cosine] * 4, axis=1),
        jnp.concatenate([-sine, sine, -sine, sine], axis=1),
    )


def on_device(
    tokens,
    pair_order,
    norm_one,
    qkv_weight,
    out_weight,
    norm_two,
    gateup_weight,
    down_weight,
    cotangent,
):
    count = lax.axis_size("ctx")
    me = lax.axis_index("fsdp")
    me_row = jnp.reshape(me, (1,)).astype(jnp.int32)
    gain_row = jnp.concatenate(
        [jnp.pad(norm_one, (0, COLS - D // 4)), jnp.pad(norm_two, (0, D - COLS - D // 4))]
    )
    gain_rows = jnp.broadcast_to(gain_row[None, :], (16, D))
    k_weights = gather_pieces(jnp.concatenate([qkv_weight[:, D : 2 * D], gain_rows], axis=0))
    v_piece = after(qkv_weight[:, 2 * D :], k_weights[2])
    v_far = swap(v_piece, 2)
    q_weights = gather_pieces(after(qkv_weight[:, :D], v_far))
    out_pieces = gather_pieces(after(out_weight, q_weights[2]))
    gateup_pieces = gather_pieces(after(gateup_weight, out_pieces[2]))
    down_pieces = gather_pieces(after(down_weight, gateup_pieces[2]))
    pair_order = after(pair_order, k_weights[1])
    place = ring_place(lax.axis_index("ctx"), count)
    width = tokens.shape[1] // 2
    offsets = jnp.asarray(ring_offsets(count), jnp.int32)
    chunk_devices = ring_device((place + offsets) % count, count)
    blocks = jnp.sum(
        jnp.where(
            chunk_devices[:, None] == jnp.arange(count, dtype=jnp.int32)[None, :],
            pair_order[None, :],
            0,
        ),
        axis=1,
    )
    low_block = blocks[0]
    high_block = 2 * count - 1 - low_block
    within = jnp.arange(width, dtype=jnp.int32)
    positions = jnp.concatenate([low_block * width + within, high_block * width + within])
    cosine, sine = rope_tables(positions)

    token_rows = tokens[0]
    keys, normed, gains = project_keys(me_row, token_rows, k_weights, cosine, sine)
    v_weights = [v_piece, swap(v_piece, 1), v_far, swap(after(v_far, keys), 1)]
    values = project(me_row, normed, v_weights)
    all_keys, all_values = ring_gather(keys, values, count)
    queries = project(me_row, normed, q_weights, (cosine, sine))
    split = count - 3 if count == 8 else count // 2
    so_far = attend(0, blocks, queries, all_keys[:split], all_values[:split])
    weight_out = in_order(out_pieces, me)
    weight_gateup = in_order(gateup_pieces, me)
    weight_down = in_order(down_pieces, me)
    attended, exact, log_total = attend(
        split, blocks, queries, all_keys[split:], all_values[split:], so_far
    )

    gain_two = in_order([part[D // 4, COLS : COLS + D // 4] for part in k_weights], me).astype(f32)
    middle = token_rows.astype(f32) + jnp.dot(attended, weight_out, preferred_element_type=f32)
    normed_two = layer_norm(middle, gain_two).astype(bf16)
    gateup = jnp.dot(normed_two, weight_gateup, preferred_element_type=f32)
    hidden_f, geglu_pull = jax.vjp(geglu, gateup[:, :FF], gateup[:, FF:])
    hidden = hidden_f.astype(bf16)
    result = middle + jnp.dot(hidden, weight_down, preferred_element_type=f32)
    grad_out = cotangent[0]
    grad_hidden = dot(grad_out, weight_down, 1, 1)
    grad_gate, grad_up = geglu_pull(grad_hidden)
    grad_gateup = jnp.concatenate([grad_gate, grad_up], axis=1).astype(bf16)
    grad_normed_two = dot(grad_gateup, weight_gateup, 1, 1)
    unit_two, inverse_two = normalise(middle)
    scaled = grad_normed_two * gain_two
    mean_one = jnp.mean(scaled, axis=-1, keepdims=True)
    mean_two = jnp.mean(scaled * unit_two, axis=-1, keepdims=True)
    gain_product = grad_normed_two * unit_two
    grad_middle = grad_out.astype(f32) + inverse_two * (scaled - mean_one - unit_two * mean_two)
    grad_branch = grad_middle.astype(bf16)
    grad_attended = dot(grad_branch, weight_out, 1, 1).astype(bf16)

    cuts = [0, 3, 5, 7, 8] if count == 8 else [i * count // 4 for i in range(5)]
    slots = {offset: slot for slot, offset in enumerate(ring_offsets(count))}
    key_parts, value_parts = [None] * count, [None] * count
    grad_queries = None

    def back_part(which, held, earlier):
        first, last = cuts[which], cuts[which + 1]
        query_rows, _ = lax.optimization_barrier((queries, earlier))
        held, key_parts[first:last], value_parts[first:last] = attend_back(
            first, blocks, query_rows, grad_attended, exact, log_total,
            all_keys[first:last], all_values[first:last], held, (cosine, sine),
        )
        return held

    def unfold(piece):
        top, rest = piece[:, :D], piece[:, D:]
        return jnp.concatenate(
            [top, jnp.concatenate([rest[: D // 8], rest[D // 8 :]], axis=1)], axis=0
        )

    def added(parts, which, down, up, distance):
        pair = [parts[slots[-distance]], parts[slots[distance]]]
        groups = [(one, sums[which]) for one, sums in zip(pair, (down, up)) if sums[which] is not None]
        sums = iter(add_all(groups)) if groups else None
        return [
            one if held[which] is None else next(sums) for one, held in zip(pair, (down, up))
        ]

    sent = []

    def hop(down, up, distance):
        arrived = ([], [])
        for which, parts in enumerate((key_parts, value_parts)):
            one, other = added(parts, which, down, up, distance)
            sent.extend([one, other])
            arrived[0].append(shift(one, -1, count))
            arrived[1].append(shift(other, 1, count))
        return arrived

    def mirror(pieces):
        return add_rounded(pieces[2], pieces[3])

    def over_cores(pieces):
        return [pieces[0], swap(pieces[1], 1), pieces[2], swap(pieces[3], 1)]

    def ended(*values):
        return lax.optimization_barrier(values)

    one, two, three = cuts[1:4]
    gateup_grads, middle_grads_all = middle_grads(
        me_row, normed_two, grad_gateup, attended, grad_branch, hidden, grad_out, gain_product
    )
    gateup_grads, middle_grads_all = over_cores(gateup_grads), over_cores(middle_grads_all)
    grad_queries = back_part(3, None, gateup_grads[0])
    gateup_grads, middle_grads_all, grad_queries, key_parts[three:], value_parts[three:] = ended(
        gateup_grads, middle_grads_all, grad_queries, key_parts[three:], value_parts[three:]
    )
    down = [shift(key_parts[-1], -1, count), None]
    up = [None, shift(value_parts[-1], 1, count)]
    gateup_far = mirror(gateup_grads)
    gateup_last = [swap(gateup_far[:, :FF], 2)]
    grad_queries = back_part(2, grad_queries, gateup_far)
    down[0], up[1], gateup_last[0], gateup_far, middle_grads_all, grad_queries = ended(
        down[0], up[1], gateup_last[0], gateup_far, middle_grads_all, grad_queries
    )
    key_parts[two:three], value_parts[two:three], _ = ended(
        key_parts[two:three], value_parts[two:three], down[0]
    )
    distances = list(range(count // 2 - 1, 0, -1))
    down, up = hop(down, up, distances[0])
    gateup_last.append(swap(gateup_far[:, FF:], 2))
    middle_far = mirror(middle_grads_all)
    grad_queries = back_part(1, grad_queries, middle_far)
    gateup_last, middle_far, grad_queries, key_parts[one:two], value_parts[one:two] = ended(
        gateup_last, middle_far, grad_queries, key_parts[one:two], value_parts[one:two]
    )
    gateup_last = jnp.concatenate(gateup_last, axis=1)
    middle_last = swap(middle_far, 2)
    for distance in distances[1:-1]:
        if key_parts[slots[-distance]] is None:
            grad_queries = back_part(0, grad_queries, sent[-4:])
        down, up = hop(down, up, distance)
    if key_parts[0] is None:
        grad_queries = back_part(0, grad_queries, sent[-4:])
    down[0], up[0], middle_last, grad_queries, key_parts[:one], value_parts[:one] = ended(
        down[0], up[0], middle_last, grad_queries, key_parts[:one], value_parts[:one]
    )
    down, up = hop(down, up, distances[-1])
    q_pieces, start = q_back(me_row, normed, after(grad_queries, sent[-4:]), q_weights)
    q_pieces = over_cores(q_pieces)
    q_last = swap(mirror(q_pieces), 2)
    gateup_sum, middle_sum = (
        add_all([(pieces[0], pieces[1], last)])[0]
        for pieces, last in ((gateup_grads, gateup_last), (middle_grads_all, middle_last))
    )
    middle_rows = jnp.concatenate([gateup_sum, middle_sum], axis=1)
    v_pieces, start = v_back(me_row, normed, (value_parts[0], down[1], up[1]), v_weights, start)
    v_pieces = over_cores(v_pieces)
    v_far = mirror(v_pieces)
    v_last = swap(v_far, 2)
    key_sums, middle_rows, start, v_far = ended(
        (key_parts[0], down[0], up[0]), middle_rows, start, v_far
    )
    middle_total = RingTotal(middle_rows, count)
    middle_total.hop()
    k_pieces, grad_tokens = k_back(
        me_row, normed, key_sums, k_weights, cosine, sine, start, token_rows, gains, grad_middle
    )
    k_pieces, q_last, v_last, middle_total.up, middle_total.down = ended(
        k_pieces, q_last, v_last, middle_total.up, middle_total.down
    )
    q_sum = add_all([(q_pieces[0], q_pieces[1], q_last)])[0]
    v_sum = add_all([(v_pieces[0], v_pieces[1], v_last)])[0]
    k_pieces = over_cores(k_pieces)
    k_last = swap(mirror(k_pieces), 2)
    middle_total.hop()
    middle_total.hop()
    k_last, middle_total.up, middle_total.down = ended(
        k_last, middle_total.up, middle_total.down
    )
    k_sum = add_all([(k_pieces[0], k_pieces[1], k_last)])[0]
    kv_total = RingTotal(jnp.concatenate([q_sum, k_sum[:, : D + LANES], v_sum], axis=1), count)
    while kv_total.done < kv_total.hops - 1:
        kv_total.hop()
        middle_total.hop()
        kv_total.up, kv_total.down, middle_total.up, middle_total.down = ended(
            kv_total.up, kv_total.down, middle_total.up, middle_total.down
        )
    ends = (0, 3 * D, 4 * D, 4 * D + FF, 4 * D + FF + LANES)
    grad_gateup_weight, grad_out_weight, grad_down, grad_gain = (
        middle_total.columns(slice(ends[i], ends[i + 1])) for i in range(4)
    )
    gain_two_own = grad_gain[:, 0]
    grad_down_weight = unfold(grad_down)
    kv_total.hop((grad_gateup_weight, grad_out_weight, grad_down_weight, gain_two_own))
    return (
        result.astype(bf16)[None],
        grad_tokens[None],
        kv_total.columns(slice(2 * D, 2 * D + LANES))[:, 0],
        jnp.concatenate(
            [kv_total.columns(slice(0, 2 * D)), kv_total.columns(slice(2 * D + LANES, 3 * D + LANES))], axis=1
        ),
        grad_out_weight,
        gain_two_own,
        grad_gateup_weight,
        grad_down_weight,
    )


def solution(mesh):
    return jax.shard_map(
        on_device,
        mesh=mesh,
        in_specs=(
            P("fsdp", "ctx", None),
            P(),
            P("fsdp"),
            P("fsdp", None),
            P("fsdp", None),
            P("fsdp"),
            P("fsdp", None),
            P("fsdp", None),
            P("fsdp", "ctx", None),
        ),
        out_specs=(
            P("fsdp", "ctx", None),
            P("fsdp", "ctx", None),
            P("fsdp"),
            P("fsdp", None),
            P("fsdp", None),
            P("fsdp"),
            P("fsdp", None),
            P("fsdp", None),
        ),
        check_vma=False,
    )
```
